32 devices in a mesh: section: 2 (over core), batch: 16 (over z, y, x).
Axes of the slice: x: 2, y: 2, z: 4, core: 2. Of those that a mesh axis runs over, the one named last changes fastest.
Arguments:
- enc_input: bfloat16 [64, 228, 768], P('batch'), may hold values from -6 to 6
- dec_input: bfloat16 [64, 32, 768], P('batch'), may hold values from -6 to 6
- out_grad: bfloat16 [64, 32, 768], P('batch'), may hold values from -6 to 6
- attn_qkv: bfloat16 [2, 768, 2304], P('section'), may hold values from -0.21875 to 0.21875
- attn_out: bfloat16 [2, 768, 768], P('section'), may hold values from -0.875 to 0.875
- mlp_in: bfloat16 [2, 768, 3072], P('section'), may hold values from -0.21875 to 0.21875
- mlp_out: bfloat16 [2, 3072, 768], P('section'), may hold values from -0.109375 to 0.109375
- cross_proj: bfloat16 [2, 768, 1536], P('section'), may hold values from -0.3125 to 0.3125
- norm_gain: bfloat16 [2, 3, 768], P('section'), may hold values from 0.099609375 to 1.8984375
- norm_shift: bfloat16 [2, 3, 768], P('section'), may hold values from -2 to 2
- image_count: int32 [16], P('batch'), may hold values from 0 to 4
- prefix_len: int32 [64], P('batch'), may hold values from 1 to 32
- suffix_len: int32 [64], P('batch'), may hold values from 1 to 32
Outputs:
- decoded: bfloat16 [64, 32, 768], P('batch', None, 'section')
- enc_input_grad: bfloat16 [64, 228, 768], P('batch', None, 'section')
- dec_input_grad: bfloat16 [64, 32, 768], P('batch', None, 'section')
- grad_attn_qkv: float32 [2, 768, 2304], P('section')
- grad_attn_out: float32 [2, 768, 768], P('section')
- grad_mlp_in: float32 [2, 768, 3072], P('section')
- grad_mlp_out: float32 [2, 3072, 768], P('section')
- grad_cross_proj: float32 [2, 768, 1536], P('section')
- grad_norm_gain: float32 [2, 3, 768], P('section')
- grad_norm_shift: float32 [2, 3, 768], P('section')
The draws below stay inside these ranges and needn't reach their ends.
Inputs may be any that keep to these rules, and one draw needn't show every extreme that they name: `image_count`: the items of a batch shard whose local number is below this count carry image patches; the patch positions of the others are masked. `prefix_len`: prefix positions at or beyond this length are padding. `suffix_len`: suffix positions at or beyond this length are padding as keys.
All inputs are finite; a program needn't handle non-finite values.
Results may differ from the reference program's by a relative error of at most 0.019.
Values may be sent and summed in bfloat16 or wider, within the bound.
A program may use at most 512 MiB of HBM per device.

```python
import math
import jax
import jax.numpy as jnp
from jax import lax

D = 768
HEAD_DIM = 64
FF = 3072
PATCHES = 196
PREFIX = 32
SUFFIX = 32
SEQ_ENC = 228
ITEMS_DEV = 4
ITEMS = 64
N_BATCH = 16


def draw_out_grad(key, part):
    key = jax.random.fold_in(key, 7)
    random_key = jax.random.fold_in(key, 1)
    common_key = jax.random.fold_in(key, 2)
    random_part = jnp.clip(jax.random.normal(random_key, (ITEMS, SUFFIX, D), jnp.float32), -4.0, 4.0)
    common_part = jnp.clip(jax.random.normal(common_key, (1, 1, D), jnp.float32), -4.0, 4.0)
    mixing = 0.5
    return (random_part + mixing * common_part).astype(jnp.bfloat16)


def set_ends(values, rng, low, largest):
    place = [jax.random.randint(jax.random.fold_in(rng, axis), (), 0, length) for axis, length in enumerate(values.shape)]
    longest = values.shape.index(max(values.shape))
    beside = place[:longest] + [(place[longest] + 1) % values.shape[longest]] + place[longest + 1:]
    return values.at[tuple(place)].set(low).at[tuple(beside)].set(largest)


def shard_levels(stream_key, extent, pieces, least, largest):
    gain, own = 1.0, jax.random.fold_in(stream_key, 6)
    for dim, blocks in pieces:
        heights = jnp.exp(jax.random.uniform(jax.random.fold_in(own, dim), (blocks,), jnp.float32, least / len(pieces), largest / len(pieces)))
        gain = gain * jnp.repeat(heights, extent[dim] // blocks).reshape([-1 if axis == dim else 1 for axis in range(len(extent))])
    return gain


def bell_draw(rng, extent, scale, limit, pieces=(), held_as=jnp.bfloat16):
    values = jax.random.normal(rng, extent, jnp.float32) * scale
    if len(pieces) > 0:
        values = shard_levels(rng, extent, pieces, -0.22, 0.18) * values
    return jnp.clip(values, min=-limit, max=limit).astype(held_as)


def setup_inputs(seed: int = 0) -> dict:
    streams_of = jax.random.split(jax.random.key(seed), 14)
    return {
        "enc_input": bell_draw(streams_of[0], (ITEMS, SEQ_ENC, D), 1.0, 6.0, ((0, 16),)),
        "dec_input": bell_draw(streams_of[1], (ITEMS, SUFFIX, D), 1.0, 6.0, ((0, 16),)),
        "out_grad": draw_out_grad(jax.random.fold_in(streams_of[13], 71), 0),
        "attn_qkv": bell_draw(streams_of[3], (2, D, 3 * D), D ** -0.5, 0.21875, ((0, 2),)),
        "attn_out": bell_draw(streams_of[4], (2, D, D), (D // 16) ** -0.5, 0.875, ((0, 2),)),
        "mlp_in": bell_draw(streams_of[5], (2, D, FF), D ** -0.5, 0.21875, ((0, 2),)),
        "mlp_out": bell_draw(streams_of[6], (2, FF, D), FF ** -0.5, 0.109375, ((0, 2),)),
        "cross_proj": bell_draw(streams_of[7], (2, D, 2 * D), (D // 2) ** -0.5, 0.3125, ((0, 2),)),
        "norm_gain": jnp.clip(1.0 + 0.18 * jax.random.normal(streams_of[8], (2, 3, D), jnp.float32), 0.099609375, 1.8984375).astype(jnp.bfloat16),
        "norm_shift": bell_draw(streams_of[9], (2, 3, D), 0.3, 2.0, ((0, 2),)),
        "image_count": set_ends(jax.random.randint(streams_of[10], (N_BATCH,), 0, ITEMS_DEV + 1), jax.random.fold_in(streams_of[10], 1), 0, ITEMS_DEV).astype(jnp.int32),
        "prefix_len": set_ends(jax.random.randint(streams_of[11], (ITEMS,), 1, PREFIX + 1), jax.random.fold_in(streams_of[11], 1), 1, PREFIX).astype(jnp.int32),
        "suffix_len": set_ends(jax.random.randint(streams_of[12], (ITEMS,), 1, SUFFIX + 1), jax.random.fold_in(streams_of[12], 1), 1, SUFFIX).astype(jnp.int32),
    }


@jax.custom_vjp
def low(v):
    return lax.optimization_barrier(v.astype(jnp.bfloat16)).astype(jnp.float32)

@jax.custom_vjp
def low_back(v):
    return v

def low_keep(v):
    return (low(v), None)

def low_pass(kept, grad):
    return (grad,)

def back_keep(v):
    return (v, None)

def back_low(kept, grad):
    return (low(grad),)
low.defvjp(low_keep, low_pass)
low_back.defvjp(back_keep, back_low)
far_below = -1000000000.0
epsilon = 1e-06

def layer_norm(inputs, gain_row, shift_row):
    average = lax.optimization_barrier(jnp.mean(inputs, axis=-1, keepdims=True))
    centered = inputs - average
    variance = lax.optimization_barrier(jnp.mean(centered * centered, axis=-1, keepdims=True))
    return centered * lax.rsqrt(variance + epsilon) * gain_row + shift_row

def matmul(left_side, matrix):
    return jnp.einsum('...d,df->...f', left_side, matrix, precision=lax.Precision.HIGHEST)

def attention(queries, key_rows, value_rows, allowed):
    group_size, query_len, model_width = queries.shape
    key_len = key_rows.shape[1]
    query_heads = queries.reshape(group_size, query_len, -1, HEAD_DIM)
    key_heads = key_rows.reshape(group_size, key_len, -1, HEAD_DIM)
    value_heads = value_rows.reshape(group_size, key_len, -1, HEAD_DIM)
    raw_scores = jnp.einsum('bqhe,bkhe->bhqk', query_heads, key_heads, precision=lax.Precision.HIGHEST) * HEAD_DIM ** (-0.5)
    scores = low_back(jnp.where(allowed[:, None], raw_scores, far_below))
    row_top = lax.optimization_barrier(jnp.max(scores, axis=-1, keepdims=True))
    exponent = jnp.exp(scores - row_top)
    probability = exponent / lax.optimization_barrier(jnp.sum(exponent, axis=-1, keepdims=True))
    attended = jnp.einsum('bhqk,bkhe->bqhe', low(probability), value_heads, precision=lax.Precision.HIGHEST)
    return low_back(low(attended.reshape(group_size, query_len, model_width)))

def self_block(inputs, gain_row, shift_row, qkv_matrix, out_matrix, allowed):
    normed = low(layer_norm(inputs, gain_row, shift_row))
    qkv = low_back(low(matmul(normed, qkv_matrix)))
    queries, key_rows, value_rows = jnp.split(qkv, 3, axis=-1)
    attended = attention(queries, key_rows, value_rows, allowed)
    return low_back(matmul(attended, out_matrix))

def feed_forward(hidden, gain_row, shift_row, up_matrix, down_matrix):
    normed = low(layer_norm(hidden, gain_row, shift_row))
    upward = low_back(matmul(normed, up_matrix))
    active = low(jax.nn.gelu(upward))
    return low_back(matmul(active, down_matrix))

def forward(enc_rows, dec_rows, weights, key_allowed, self_allowed):
    qkv_matrix, out_matrix, up_matrix, down_matrix, cross_matrix, gains, shifts = weights
    model_width = enc_rows.shape[-1]
    hidden = enc_rows + self_block(enc_rows, gains[0, 0], shifts[0, 0], qkv_matrix[0], out_matrix[0], key_allowed)
    result = hidden + feed_forward(hidden, gains[0, 1], shifts[0, 1], up_matrix[0], down_matrix[0])
    memory = low(layer_norm(result, gains[0, 2], shifts[0, 2]))
    keys_values = low_back(low(matmul(memory, cross_matrix[0])))
    hidden = dec_rows + self_block(dec_rows, gains[1, 0], shifts[1, 0], qkv_matrix[1], out_matrix[1], self_allowed)
    cross_normed = low(layer_norm(hidden, gains[1, 1], shifts[1, 1]))
    cross_queries = low_back(low(matmul(cross_normed, cross_matrix[1][:, :model_width])))
    attended = attention(cross_queries, keys_values[..., :model_width], keys_values[..., model_width:], key_allowed)
    middle = hidden + low_back(matmul(attended, cross_matrix[1][:, model_width:]))
    return middle + feed_forward(middle, gains[1, 2], shifts[1, 2], up_matrix[1], down_matrix[1])

def reference(enc_input, dec_input, out_grad, attn_qkv, attn_out, mlp_in, mlp_out, cross_proj, norm_gain, norm_shift, image_count, prefix_len, suffix_len):
    item_total = enc_input.shape[0]
    group_size = math.gcd(item_total, 16)
    groups = item_total // group_size
    weights = tuple((matrix.astype(jnp.float32) for matrix in (attn_qkv, attn_out, mlp_in, mlp_out, cross_proj, norm_gain, norm_shift)))
    item_index = jnp.arange(item_total, dtype=jnp.int32)
    has_image = item_index % ITEMS_DEV < image_count[item_index // ITEMS_DEV]
    positions = jnp.arange(SEQ_ENC, dtype=jnp.int32)
    key_allowed = jnp.where(positions[None, :] < PATCHES, has_image[:, None], positions[None, :] - PATCHES < prefix_len[:, None])[:, None, :]
    places = jnp.arange(SUFFIX, dtype=jnp.int32)
    self_allowed = (places[None, None, :] <= places[None, :, None]) & (places[None, None, :] < suffix_len[:, None, None])

    def regroup(array):
        return array.reshape((groups, group_size) + array.shape[1:])

    def one_group(totals, group_data):
        enc_rows, dec_rows, cotangent, key_part, self_part = group_data

        def local_forward(enc_values, dec_values, weight_values):
            return forward(enc_values, dec_values, weight_values, key_part, self_part)
        decoded, pullback = jax.vjp(local_forward, enc_rows.astype(jnp.float32), dec_rows.astype(jnp.float32), weights)
        grad_enc, grad_dec, grad_weights = pullback(cotangent.astype(jnp.float32))
        totals = jax.tree.map(jnp.add, totals, grad_weights)
        return (totals, (decoded.astype(jnp.bfloat16), grad_enc.astype(jnp.bfloat16), grad_dec.astype(jnp.bfloat16)))
    start_totals = jax.tree.map(jnp.zeros_like, weights)
    totals, outputs = lax.scan(one_group, start_totals, (regroup(enc_input), regroup(dec_input), regroup(out_grad), regroup(key_allowed), regroup(self_allowed)))
    decoded = outputs[0].reshape((item_total,) + outputs[0].shape[2:])
    grad_enc = outputs[1].reshape((item_total,) + outputs[1].shape[2:])
    grad_dec = outputs[2].reshape((item_total,) + outputs[2].shape[2:])
    return (decoded, grad_enc, grad_dec, totals[0], totals[1], totals[2], totals[3], totals[4], totals[5], totals[6])
```

```python
import functools

import jax
import jax.numpy as jnp
from jax import lax
from jax.experimental import pallas as pl
from jax.experimental.pallas import tpu as pltpu
from jax.sharding import PartitionSpec as P

HEAD_DIM = 64
PATCHES = 196
far_below = -1000000000.0
epsilon = 1e-06

MESH = pl.DeviceIdType.MESH
NZ = 4

def place():
    b = lax.axis_index("batch"); c = lax.axis_index("section")
    return b % 2, (b // 2) % 2, b // 4, c

def bid(x, y, z):
    return z * 4 + y * 2 + x

def ar_kernel(pairs, rows, width, g, norms, out, norms_out, acc, res, rx, up, dn, ry, nbuf, lsem, asend, arecv, zsend, zrecv, nsem):
    x, y, z, c = place()
    half, block, share = rows // 2, rows // 8, rows // 16

    def dev(x, y, z):
        return (c, bid(x, y, z))

    across = (dev(1 - x, y, z), dev(x, 1 - y, z))
    above, below = dev(x, y, z + 1), dev(x, y, z - 1)
    bit = (x, y)

    barrier = pltpu.get_barrier_semaphore()
    faraway = dev(x, y, (z + 2) % NZ)
    for d in across + (faraway,):
        pl.semaphore_signal(barrier, inc=1, device_id=d, device_id_type=MESH)

    @pl.when(z < NZ - 1)
    def _():
        pl.semaphore_signal(barrier, inc=1, device_id=above, device_id_type=MESH)

    @pl.when(z > 0)
    def _():
        pl.semaphore_signal(barrier, inc=1, device_id=below, device_id_type=MESH)

    pl.semaphore_wait(barrier, 3 + (z + NZ - 1) // NZ + (2 * NZ - 2 - z) // NZ)

    def rdma(src, dst, send, recv, device):
        return pltpu.make_async_remote_copy(src_ref=src, dst_ref=dst, send_sem=send, recv_sem=recv, device_id=device, device_id_type=MESH)

    def parts(t, f):
        p = 2 * t + f
        a, b = bit[f], bit[1 - f]
        own = a * half
        other = (1 - a) * half
        return p, own, other, b

    def rows_at(start, n):
        return pl.ds(pl.multiple_of(start, 16), n)

    def own_load(t, f):
        p, own, other, b = parts(t, f)
        return pltpu.make_async_copy(g.at[p, rows_at(own, half)], acc.at[p], lsem.at[p, 0])

    def own_store(t, f, k):
        p, own, other, b = parts(t, f)
        start = own if k == 0 else other
        return pltpu.make_async_copy(res.at[p, rows_at(start, half)], out.at[p, rows_at(start, half)], lsem.at[p, k + 1])

    def rs_a(t, f):
        p, own, other, b = parts(t, f)
        return rdma(g.at[p, rows_at(other, half)], rx.at[p], asend.at[p, 0], arecv.at[p, 0], across[f])

    def rs_up(t, f, k):
        p, own, other, b = parts(t, f)
        return rdma(acc.at[p, pl.ds(k * block, block)], up.at[p, k], zsend.at[p, 0, k], zrecv.at[p, 0, k], above)

    def rs_dn(t, f, k):
        p, own, other, b = parts(t, f)
        return rdma(acc.at[p, pl.ds(k * block, block)], dn.at[p, k], zsend.at[p, 1, k], zrecv.at[p, 1, k], below)

    def rs_b(t, f):
        p, own, other, b = parts(t, f)
        return rdma(acc.at[p, rows_at(z * block + (1 - b) * share, share)], ry.at[p], asend.at[p, 1], arecv.at[p, 1], across[1 - f])

    def ag_b(t, f):
        p, own, other, b = parts(t, f)
        s = res.at[p, rows_at(own + z * block + b * share, share)]
        return rdma(s, s, asend.at[p, 2], arecv.at[p, 2], across[1 - f])

    def ag_up(t, f, k):
        p, own, other, b = parts(t, f)
        s = res.at[p, rows_at(own + k * block, block)]
        return rdma(s, s, zsend.at[p, 2, k], zrecv.at[p, 2, k], above)

    def ag_dn(t, f, k):
        p, own, other, b = parts(t, f)
        s = res.at[p, rows_at(own + k * block, block)]
        return rdma(s, s, zsend.at[p, 3, k], zrecv.at[p, 3, k], below)

    def ag_a(t, f):
        p, own, other, b = parts(t, f)
        s = res.at[p, rows_at(own, half)]
        return rdma(s, s, asend.at[p, 3], arecv.at[p, 3], across[f])

    def s0(t, f):
        rs_a(t, f).start()
        own_load(t, f).start()

    def s1(t, f):
        p, own, other, b = parts(t, f)
        own_load(t, f).wait()
        rs_a(t, f).wait()
        acc[p] = acc[p] + rx[p]

        @pl.when(z == 0)
        def _():
            for k in range(NZ - 1, 0, -1):
                rs_up(t, f, k).start()

        @pl.when(z == NZ - 1)
        def _():
            for k in range(NZ - 1):
                rs_dn(t, f, k).start()

    def chain(t, f, j):
        p, own, other, b = parts(t, f)

        @pl.when(z == j)
        def _():
            for k in range(NZ - 1, j - 1, -1):
                rs_up(t, f, k).wait_recv()
                r = pl.ds(k * block, block)
                acc[p, r] = acc[p, r] + up[p, k]
                if k > j:
                    rs_up(t, f, k).start()

        @pl.when(z == NZ - 1 - j)
        def _():
            for k in range(NZ - j):
                rs_dn(t, f, k).wait_recv()
                r = pl.ds(k * block, block)
                acc[p, r] = acc[p, r] + dn[p, k]
                if k < NZ - 1 - j:
                    rs_dn(t, f, k).start()

    def s4(t, f):
        chain(t, f, NZ - 1)
        rs_b(t, f).start()

    def s5(t, f):
        p, own, other, b = parts(t, f)
        rs_b(t, f).wait()
        mine = z * block + b * share
        res[p, rows_at(own + mine, share)] = acc[p, rows_at(mine, share)] + ry[p]
        ag_b(t, f).start()

    def s6(t, f):
        ag_b(t, f).wait()

        @pl.when(z < NZ - 1)
        def _():
            ag_up(t, f, z).start()

        @pl.when(z > 0)
        def _():
            ag_dn(t, f, z).start()

    def spread(t, f, j):
        @pl.when(z >= j)
        def _():
            ag_up(t, f, z - j).wait_recv()

            @pl.when(z < NZ - 1)
            def _():
                ag_up(t, f, z - j).start()

        @pl.when(z + j <= NZ - 1)
        def _():
            ag_dn(t, f, z + j).wait_recv()

            @pl.when(z > 0)
            def _():
                ag_dn(t, f, z + j).start()

    def s9(t, f):
        spread(t, f, NZ - 1)
        ag_a(t, f).start()
        own_store(t, f, 0).start()

    def s10(t, f):
        ag_a(t, f).wait()
        own_store(t, f, 1).start()
        for k in range(NZ):
            @pl.when((z < k))
            def _(k=k):
                rs_up(t, f, k).wait_send()

            @pl.when((z > k))
            def _(k=k):
                rs_dn(t, f, k).wait_send()

            @pl.when((k <= z) & (z < NZ - 1))
            def _(k=k):
                ag_up(t, f, k).wait_send()

            @pl.when((k >= z) & (z > 0))
            def _(k=k):
                ag_dn(t, f, k).wait_send()

    def s11(t, f):
        own_store(t, f, 0).wait()
        own_store(t, f, 1).wait()

    mates = across + (dev(x, y, z + 1 - 2 * (z % 2)), faraway)

    def norm_swap(j):
        return rdma(norms_out, nbuf.at[j], nsem.at[0, j], nsem.at[1, j], mates[j])

    norms_out[...] = norms[...]
    norm_swap(0).start()

    stages = [s0, s1] + [functools.partial(lambda j, t, f: chain(t, f, j), j) for j in range(1, NZ - 1)] + [s4, s5, s6] + [
        functools.partial(lambda j, t, f: spread(t, f, j), j) for j in range(1, NZ - 1)] + [s9, s10, s11]
    ahead = 2

    def tick(tau, carry):
        for j in range(4):

            @pl.when(tau == 3 * j + 3)
            def _(j=j):
                norm_swap(j).wait()
                norms_out[...] = norms_out[...] + nbuf[j]
                if j < 3:
                    norm_swap(j + 1).start()

        for i, stage in enumerate(stages):
            lag = 0 if i == 0 else i - 1 + ahead
            t = tau - lag

            @pl.when((t >= 0) & (t < pairs))
            def _(stage=stage, t=t):
                stage(t, 0)
                stage(t, 1)
        return carry
    lax.fori_loop(0, pairs + len(stages) - 2 + ahead, tick, 0)


def all_reduce(g, norms, collective_id):
    n, rows, width = g.shape
    half, block, share = rows // 2, rows // 8, rows // 16
    bf = jnp.bfloat16
    return pl.pallas_call(
        functools.partial(ar_kernel, n // 2, rows, width),
        out_shape=(jax.ShapeDtypeStruct((n, rows, width), bf), jax.ShapeDtypeStruct(norms.shape, norms.dtype)),
        in_specs=[pl.BlockSpec(memory_space=pl.ANY), pl.BlockSpec(memory_space=pltpu.VMEM)],
        out_specs=(pl.BlockSpec(memory_space=pl.ANY), pl.BlockSpec(memory_space=pltpu.VMEM)),
        scratch_shapes=[
            pltpu.VMEM((n, half, width), bf),
            pltpu.VMEM((n, rows, width), bf),
            pltpu.VMEM((n, half, width), bf),
            pltpu.VMEM((n, NZ, block, width), bf),
            pltpu.VMEM((n, NZ, block, width), bf),
            pltpu.VMEM((n, share, width), bf),
            pltpu.VMEM((4,) + norms.shape, norms.dtype),
            pltpu.SemaphoreType.DMA((n, 3)),
            pltpu.SemaphoreType.DMA((n, 4)),
            pltpu.SemaphoreType.DMA((n, 4)),
            pltpu.SemaphoreType.DMA((n, 4, NZ)),
            pltpu.SemaphoreType.DMA((n, 4, NZ)),
            pltpu.SemaphoreType.DMA((2, 4)),
        ],
        compiler_params=pltpu.CompilerParams(collective_id=collective_id, has_side_effects=True, vmem_limit_bytes=60 * 2**20),
    )(g, norms)


def layer_norm(inputs, gain_row, shift_row):
    average = jnp.mean(inputs, axis=-1, keepdims=True)
    centered = inputs - average
    variance = jnp.mean(centered * centered, axis=-1, keepdims=True)
    return centered * lax.rsqrt(variance + epsilon) * gain_row + shift_row


def norm_back(inputs, gain_row, shift_row, grad_normed):
    unused, pullback = jax.vjp(layer_norm, inputs, gain_row, shift_row)
    return pullback(grad_normed)


def gelu_back(upward, grad_active):
    unused, pullback = jax.vjp(jax.nn.gelu, upward)
    return pullback(grad_active)[0]


def forward_product(left_side, matrix):
    return jnp.einsum("bld,df->blf", left_side, matrix, preferred_element_type=jnp.float32)


def backward_product(grad_rows, matrix):
    return jnp.einsum("blf,df->bld", grad_rows, matrix, preferred_element_type=jnp.float32)


def weight_product(left_side, grad_rows):
    return jnp.einsum("bld,blf->df", left_side, grad_rows, preferred_element_type=jnp.float32)


def split_heads(rows):
    return rows.reshape(rows.shape[0], rows.shape[1], -1, HEAD_DIM)


def masked_scores(query_heads, key_heads, allowed):
    scores = jnp.einsum(
        "bqhe,bkhe->bhqk", query_heads, key_heads, preferred_element_type=jnp.float32
    ) * HEAD_DIM ** (-0.5)
    return jnp.where(allowed[:, None], scores, far_below)


def attend(queries, key_rows, value_rows, allowed):
    scores = masked_scores(split_heads(queries), split_heads(key_rows), allowed)
    row_top = jnp.max(scores, axis=-1, keepdims=True)
    log_total = row_top + jnp.log(jnp.sum(jnp.exp(scores - row_top), axis=-1, keepdims=True))
    probability = jnp.exp(scores - log_total).astype(jnp.bfloat16)
    attended = jnp.einsum(
        "bhqk,bkhe->bqhe", probability, split_heads(value_rows), preferred_element_type=jnp.float32
    )
    return (attended.reshape(queries.shape).astype(jnp.bfloat16), log_total)


def attend_back(queries, key_rows, value_rows, allowed, log_total, grad_attended):
    query_heads = split_heads(queries)
    key_heads = split_heads(key_rows)
    value_heads = split_heads(value_rows)
    probability = jnp.exp(masked_scores(query_heads, key_heads, allowed) - log_total)
    grad_heads = split_heads(grad_attended)
    grad_probability = jnp.einsum(
        "bqhe,bkhe->bhqk", grad_heads, value_heads, preferred_element_type=jnp.float32
    )
    grad_values = jnp.einsum(
        "bhqk,bqhe->bkhe",
        probability.astype(jnp.bfloat16),
        grad_heads,
        preferred_element_type=jnp.float32,
    )
    inner = jnp.sum(probability * grad_probability, axis=-1, keepdims=True)
    grad_scores = (probability * (grad_probability - inner)).astype(jnp.bfloat16)
    grad_queries = jnp.einsum(
        "bhqk,bkhe->bqhe", grad_scores, key_heads, preferred_element_type=jnp.float32
    ) * HEAD_DIM ** (-0.5)
    grad_keys = jnp.einsum(
        "bhqk,bqhe->bkhe", grad_scores, query_heads, preferred_element_type=jnp.float32
    ) * HEAD_DIM ** (-0.5)
    return (
        grad_queries.reshape(queries.shape),
        grad_keys.reshape(key_rows.shape),
        grad_values.reshape(value_rows.shape),
    )


def self_attention(inputs, gain_row, shift_row, qkv_matrix, out_matrix, allowed):
    normed = layer_norm(inputs, gain_row, shift_row).astype(jnp.bfloat16)
    qkv = forward_product(normed, qkv_matrix).astype(jnp.bfloat16)
    queries, key_rows, value_rows = jnp.split(qkv, 3, axis=-1)
    attended, log_total = attend(queries, key_rows, value_rows, allowed)
    return ((normed, qkv, attended, log_total), forward_product(attended, out_matrix))


def self_attention_back(
    inputs, gain_row, shift_row, qkv_matrix, out_matrix, allowed, kept, grad_stream
):
    normed, qkv, attended, log_total = kept
    grad_low = grad_stream.astype(jnp.bfloat16)
    grad_out_matrix = weight_product(attended, grad_low)
    grad_attended = backward_product(grad_low, out_matrix).astype(jnp.bfloat16)
    queries, key_rows, value_rows = jnp.split(qkv, 3, axis=-1)
    grad_parts = attend_back(queries, key_rows, value_rows, allowed, log_total, grad_attended)
    grad_qkv = jnp.concatenate(grad_parts, axis=-1).astype(jnp.bfloat16)
    grad_qkv_matrix = weight_product(normed, grad_qkv)
    grad_inputs, grad_gain, grad_shift = norm_back(
        inputs, gain_row, shift_row, backward_product(grad_qkv, qkv_matrix)
    )
    return (grad_stream + grad_inputs, grad_qkv_matrix, grad_out_matrix, grad_gain, grad_shift)


def feed_forward(hidden, gain_row, shift_row, up_matrix, down_matrix):
    normed = layer_norm(hidden, gain_row, shift_row).astype(jnp.bfloat16)
    upward = forward_product(normed, up_matrix)
    active = jax.nn.gelu(upward).astype(jnp.bfloat16)
    return (normed, upward, active, forward_product(active, down_matrix))


def feed_forward_back(hidden, gain_row, shift_row, up_matrix, down_matrix, kept, grad_stream):
    normed, upward, active, unused = kept
    grad_low = grad_stream.astype(jnp.bfloat16)
    grad_down = weight_product(active, grad_low)
    grad_upward = gelu_back(upward, backward_product(grad_low, down_matrix)).astype(jnp.bfloat16)
    grad_up = weight_product(normed, grad_upward)
    grad_hidden, grad_gain, grad_shift = norm_back(
        hidden, gain_row, shift_row, backward_product(grad_upward, up_matrix)
    )
    return (grad_stream + grad_hidden, grad_up, grad_down, grad_gain, grad_shift)


def encoder_pass(enc_block, allowed, weights):
    qkv_matrix, out_matrix, up_matrix, down_matrix, cross_matrix, gains, shifts = weights
    inputs = enc_block.astype(jnp.float32)
    kept_attention, branch = self_attention(
        inputs, gains[0], shifts[0], qkv_matrix, out_matrix, allowed
    )
    hidden = inputs + branch
    kept_forward = feed_forward(hidden, gains[1], shifts[1], up_matrix, down_matrix)
    result = hidden + kept_forward[3]
    memory = layer_norm(result, gains[2], shifts[2]).astype(jnp.bfloat16)
    keys_values = forward_product(memory, cross_matrix).astype(jnp.bfloat16)
    return ((inputs, kept_attention, hidden, kept_forward, result, memory), keys_values)


def encoder_back(kept, allowed, weights, grad_keys_values):
    qkv_matrix, out_matrix, up_matrix, down_matrix, cross_matrix, gains, shifts = weights
    inputs, kept_attention, hidden, kept_forward, result, memory = kept
    grad_cross = weight_product(memory, grad_keys_values)
    grad_result, gain_two, shift_two = norm_back(
        result, gains[2], shifts[2], backward_product(grad_keys_values, cross_matrix)
    )
    grad_hidden, grad_up, grad_down, gain_one, shift_one = feed_forward_back(
        hidden, gains[1], shifts[1], up_matrix, down_matrix, kept_forward, grad_result
    )
    grad_inputs, grad_qkv, grad_attn_out, gain_zero, shift_zero = self_attention_back(
        inputs, gains[0], shifts[0], qkv_matrix, out_matrix, allowed, kept_attention, grad_hidden
    )
    grads = (
        grad_qkv,
        grad_attn_out,
        grad_up,
        grad_down,
        grad_cross,
        jnp.stack([gain_zero, gain_one, gain_two]),
        jnp.stack([shift_zero, shift_one, shift_two]),
    )
    return (grad_inputs.astype(jnp.bfloat16), grads)


def decoder_pass(dec_block, grad_block, keys_values, self_allowed, cross_allowed, weights):
    qkv_matrix, out_matrix, up_matrix, down_matrix, cross_matrix, gains, shifts = weights
    model_width = cross_matrix.shape[0]
    query_matrix = cross_matrix[:, :model_width]
    back_matrix = cross_matrix[:, model_width:]
    inputs = dec_block.astype(jnp.float32)
    kept_attention, branch = self_attention(
        inputs, gains[0], shifts[0], qkv_matrix, out_matrix, self_allowed
    )
    hidden = inputs + branch
    cross_normed = layer_norm(hidden, gains[1], shifts[1]).astype(jnp.bfloat16)
    cross_queries = forward_product(cross_normed, query_matrix).astype(jnp.bfloat16)
    key_rows, value_rows = jnp.split(keys_values, 2, axis=-1)
    cross_attended, cross_log = attend(cross_queries, key_rows, value_rows, cross_allowed)
    middle = hidden + forward_product(cross_attended, back_matrix)
    kept_forward = feed_forward(middle, gains[2], shifts[2], up_matrix, down_matrix)
    result = middle + kept_forward[3]
    grad_result = grad_block.astype(jnp.float32)
    grad_middle, grad_up, grad_down, gain_two, shift_two = feed_forward_back(
        middle, gains[2], shifts[2], up_matrix, down_matrix, kept_forward, grad_result
    )
    grad_low = grad_middle.astype(jnp.bfloat16)
    grad_back_matrix = weight_product(cross_attended, grad_low)
    grad_cross_attended = backward_product(grad_low, back_matrix).astype(jnp.bfloat16)
    grad_cross_queries, grad_key_rows, grad_value_rows = attend_back(
        cross_queries, key_rows, value_rows, cross_allowed, cross_log, grad_cross_attended
    )
    grad_keys_values = jnp.concatenate([grad_key_rows, grad_value_rows], axis=-1).astype(
        jnp.bfloat16
    )
    grad_queries_low = grad_cross_queries.astype(jnp.bfloat16)
    grad_query_matrix = weight_product(cross_normed, grad_queries_low)
    grad_norm_input, gain_one, shift_one = norm_back(
        hidden, gains[1], shifts[1], backward_product(grad_queries_low, query_matrix)
    )
    grad_hidden = grad_middle + grad_norm_input
    grad_inputs, grad_qkv, grad_attn_out, gain_zero, shift_zero = self_attention_back(
        inputs,
        gains[0],
        shifts[0],
        qkv_matrix,
        out_matrix,
        self_allowed,
        kept_attention,
        grad_hidden,
    )
    grads = (
        grad_qkv,
        grad_attn_out,
        grad_up,
        grad_down,
        jnp.concatenate([grad_query_matrix, grad_back_matrix], axis=1),
        jnp.stack([gain_zero, gain_one, gain_two]),
        jnp.stack([shift_zero, shift_one, shift_two]),
    )
    return (result.astype(jnp.bfloat16), grad_inputs.astype(jnp.bfloat16), grad_keys_values, grads)


def encoder_keys(has_image, prefix_rows, enc_len):
    positions = jnp.arange(enc_len, dtype=jnp.int32)
    patch_part = positions[None, :] < PATCHES
    return jnp.where(
        patch_part, has_image[:, None], positions[None, :] - PATCHES < prefix_rows[:, None]
    )[:, None, :]


def decoder_mask(suffix_rows, dec_len):
    positions = jnp.arange(dec_len, dtype=jnp.int32)
    return (positions[None, None, :] <= positions[None, :, None]) & (
        positions[None, None, :] < suffix_rows[:, None, None]
    )


WIDTH = 256


def to_panels(matrix):
    rows, columns = matrix.shape
    high = 768
    split = matrix.reshape(rows // high, high, columns // WIDTH, WIDTH)
    return split.transpose(0, 2, 1, 3).reshape(-1, high, WIDTH)


def from_panels(panels, shape):
    rows, columns = shape
    high = panels.shape[1]
    split = panels.reshape(rows // high, columns // WIDTH, high, WIDTH)
    return split.transpose(0, 2, 1, 3).reshape(shape).astype(jnp.float32)


def per_device(
    enc_input,
    dec_input,
    out_grad,
    attn_qkv,
    attn_out,
    mlp_in,
    mlp_out,
    cross_proj,
    norm_gain,
    norm_shift,
    image_count,
    prefix_len,
    suffix_len,
):
    section = lax.axis_index("section")
    items, enc_len, model_width = enc_input.shape
    dec_len = dec_input.shape[1]
    weights = (
        attn_qkv[0],
        attn_out[0],
        mlp_in[0],
        mlp_out[0],
        cross_proj[0],
        norm_gain[0].astype(jnp.float32),
        norm_shift[0].astype(jnp.float32),
    )
    has_image = jnp.arange(items, dtype=jnp.int32) < image_count[0]
    key_allowed = encoder_keys(has_image, prefix_len, enc_len)
    self_allowed = decoder_mask(suffix_len, dec_len)

    def blank(function, *args):
        return jax.tree.map(
            lambda a: jnp.zeros(a.shape, a.dtype), jax.eval_shape(function, *args)
        )

    def on_section(wanted, function, *args):
        return lax.cond(
            section == wanted, lambda: function(*args), lambda: blank(function, *args)
        )

    def packed(grads):
        panels = [to_panels(g.astype(jnp.bfloat16)) for g in grads[:5]]
        return jnp.concatenate(panels, axis=0), jnp.concatenate(
            [grads[5], grads[6], jnp.zeros((2, model_width), jnp.float32)], axis=0
        )

    kept, keys_values = on_section(
        0, lambda: encoder_pass(enc_input, key_allowed, weights)
    )
    arrived = lax.ppermute(keys_values, "section", [(0, 1)])

    def decode():
        out, grad, back, grads = decoder_pass(
            dec_input, out_grad, arrived, self_allowed, key_allowed, weights
        )
        return out, grad, back, packed(grads)

    dec_out, dec_grad, send_back, dec_packed = on_section(1, decode)
    returned = lax.ppermute(send_back, "section", [(1, 0)])

    def encode_back():
        grad, grads = encoder_back(kept, key_allowed, weights, returned)
        return grad, packed(grads)

    enc_grad, own_packed = lax.cond(
        section == 0, encode_back, lambda: (blank(encode_back)[0], dec_packed)
    )
    panels, norms = own_packed
    if lax.axis_size("batch") == 16:
        panels, norms = all_reduce(panels, norms, 0)
    else:
        panels = lax.psum(panels, "batch")
        norms = lax.psum(norms, "batch")
    grads = []
    first = 0
    for matrix in weights[:5]:
        count = matrix.size // (768 * WIDTH)
        grads.append(from_panels(panels[first : first + count], matrix.shape)[None])
        first += count
    half = model_width // 2

    def columns(array, start):
        return lax.dynamic_slice_in_dim(array, start, half, 2)

    on_first = section == 0
    swap = [(0, 1), (1, 0)]
    own_start, other_start = section * half, (1 - section) * half
    enc_theirs, out_theirs, dec_theirs = lax.ppermute(
        (columns(enc_grad, other_start), columns(dec_out, other_start), columns(dec_grad, other_start)),
        "section",
        swap,
    )
    return (
        jnp.where(on_first, out_theirs, columns(dec_out, own_start)),
        jnp.where(on_first, columns(enc_grad, own_start), enc_theirs),
        jnp.where(on_first, dec_theirs, columns(dec_grad, own_start)),
        *grads,
        norms[None, :3],
        norms[None, 3:6],
    )


def solution(mesh):
    items = P("batch", None, None)
    matrix = P("section", None, None)
    halves = P("batch", None, "section")
    return jax.shard_map(
        per_device,
        mesh=mesh,
        in_specs=(items,) * 3 + (matrix,) * 7 + (P("batch"),) * 3,
        out_specs=(halves,) * 3 + (matrix,) * 7,
        check_vma=False,
    )
```

```python
import functools

import jax
import jax.numpy as jnp
from jax import lax
from jax.experimental import pallas as pl
from jax.experimental.pallas import tpu as pltpu
from jax.sharding import PartitionSpec as P

PATCHES = 196
MESH = pl.DeviceIdType.MESH
bf16, f32 = jnp.bfloat16, jnp.float32
epsilon = 1e-06
far_below = -1000000000.0
HEAD = 64
SLAB = 128
TILE = 256
GELU_A = 0.7978845608028654
GELU_B = 0.044715


def nn(a, b):
    return jnp.dot(a, b, preferred_element_type=f32)


def nt(a, b):
    return lax.dot_general(a, b, (((1,), (1,)), ((), ())), preferred_element_type=f32)


def tn(a, b):
    return lax.dot_general(a, b, (((0,), (0,)), ((), ())), preferred_element_type=f32)


def normal(v):
    centered = v - jnp.mean(v, axis=-1, keepdims=True)
    spread = lax.rsqrt(jnp.mean(centered * centered, axis=-1, keepdims=True) + epsilon)
    return centered * spread, spread


def gelu_both(u):
    square = u * u
    bent = jnp.tanh(GELU_A * u * (1.0 + GELU_B * square))
    half = 0.5 * (1.0 + bent)
    slope = half + 0.5 * u * (1.0 - bent * bent) * (GELU_A * (1.0 + 3.0 * GELU_B * square))
    return u * half, slope


def at(start, size, unit):
    return pl.ds(pl.multiple_of(start, unit), size)


def fused_kernel(items, span, dec_len,
                 x_in, y_in, dz_in, wq_in, wo_in, wi_in, wd_in, wc_in, gain, shift, key_open, self_open,
                 panels, norms, dx_out, dec_out, dy_out,
                 w_qkv, w_out, w_up, w_down, w_cross,
                 qkv, prob, heads, low, rows_a, turned, hidden, result, active, slope, crossing, stage,
                 wsem, xsem, psem, send_sem, recv_sem):
    width = w_out.shape[0]
    hidden_units = w_up.shape[1]
    pairs = width // SLAB
    full = items * span
    blocks_up = hidden_units // width
    at_qkv, at_out, at_cross, at_up, at_down = 0, 3, 4, 6, 6 + blocks_up
    section = lax.axis_index("section")
    chip = lax.axis_index("batch")
    other = (1 - section, chip)

    barrier = pltpu.get_barrier_semaphore()
    pl.semaphore_signal(barrier, inc=1, device_id=other, device_id_type=MESH)

    weights = ((wq_in, w_qkv), (wo_in, w_out), (wi_in, w_up), (wd_in, w_down), (wc_in, w_cross))
    loads = [pltpu.make_async_copy(src, dst, wsem.at[n]) for n, (src, dst) in enumerate(weights)]

    lane = lax.broadcasted_iota(jnp.int32, (1, SLAB), 1)
    is_first = lane < HEAD
    mask_a = jnp.where(is_first, 1.0, 0.0).astype(bf16)
    mask_b = jnp.where(is_first, 0.0, 1.0).astype(bf16)
    scale = HEAD ** (-0.5)

    def stacked(slab, factor=1.0):
        return jnp.concatenate([slab * (mask_a * factor).astype(bf16), slab * (mask_b * factor).astype(bf16)], axis=0)

    def joined(both, rows):
        return jnp.where(is_first, both[:rows], both[rows:])

    def soft(scores, is_open):
        scores = jnp.where(is_open, scores, far_below)
        grown = jnp.exp(scores - jnp.max(scores, axis=-1, keepdims=True))
        return (grown * (1.0 / jnp.sum(grown, axis=-1, keepdims=True))).astype(bf16)

    def soft_back(p_low, dp):
        p = p_low.astype(f32)
        t = p * dp
        return (t - p * jnp.sum(t, axis=-1, keepdims=True)).astype(bf16)

    def wide(n):
        return at(n * width, width, width)

    def slab_of(n, h):
        return at(n * width + h * SLAB, SLAB, SLAB)

    def chunk(i):
        return pl.ds(i * span, span)

    def block_store(n, index):
        return pltpu.make_async_copy(stage.at[n % 2], panels.at[index], psem.at[n % 2])

    def emit(n, index, value):
        @pl.when(n >= 2)
        def _():
            block_store(n, index).wait()
        stage[n % 2] = value.astype(bf16)
        block_store(n, index).start()

    def norm_forward(value, index):
        unit, _ = normal(value)
        return (unit * gain[index : index + 1] + shift[index : index + 1]).astype(bf16)

    def norm_back(value, grad, index):
        unit, spread = normal(value)
        norms[index : index + 1] += jnp.sum(grad * unit, axis=0, keepdims=True)
        norms[3 + index : 4 + index] += jnp.sum(grad, axis=0, keepdims=True)
        scaled = grad * gain[index : index + 1]
        return spread * (
            scaled
            - jnp.mean(scaled, axis=-1, keepdims=True)
            - unit * jnp.mean(scaled * unit, axis=-1, keepdims=True)
        )

    def crossing_copy(source, n, tile):
        return pltpu.make_async_remote_copy(
            src_ref=source,
            dst_ref=crossing.at[:, at(tile * TILE, TILE, TILE)],
            send_sem=send_sem.at[n],
            recv_sem=recv_sem.at[tile],
            device_id=other,
            device_id_type=MESH,
        )

    tiles = width // TILE
    norms[...] = jnp.zeros_like(norms)

    @pl.when(section == 0)
    def _():
        x_load = pltpu.make_async_copy(x_in, low, xsem.at[0])
        x_load.start()
        for load in loads:
            load.start()
        x_load.wait()
        for i in range(items):
            rows_a[chunk(i)] = norm_forward(low[chunk(i)].astype(f32), 0)
        loads[0].wait()

        @pl.loop(0, 3)
        def _(j):
            for i in range(items):
                qkv[chunk(i), wide(j)] = nn(rows_a[chunk(i)], w_qkv[:, wide(j)]).astype(bf16)

        @pl.loop(0, items * pairs // 2)
        def _(it):
            i, h = it // (pairs // 2), 2 * (it % (pairs // 2))
            r = at(i * span, span, 16)
            for u in range(2):
                q, k, v = (qkv[r, slab_of(n, h + u)] for n in range(3))
                p = soft(nt(stacked(q, scale), k), key_open[i] > 0.0)
                prob[2 * it + u] = p
                heads[r, slab_of(0, h + u)] = joined(nn(p, v), span).astype(bf16)

        loads[1].wait()
        for i in range(items):
            r = chunk(i)
            value = low[r].astype(f32) + nn(heads[r], w_out[...])
            hidden[r] = value
            rows_a[r] = norm_forward(value, 1)
        loads[2].wait()

        @pl.loop(0, blocks_up)
        def _(j):
            for i in range(items):
                e, s = gelu_both(nn(rows_a[chunk(i)], w_up[:, wide(j)]))
                active[chunk(i), wide(j)] = e.astype(bf16)
                slope[chunk(i), wide(j)] = s.astype(bf16)

        loads[3].wait()
        for i in range(items):
            r = chunk(i)
            value = hidden[r] + nn(active[r], w_down[...])
            result[r] = value
            rows_a[r] = norm_forward(value, 2)
        loads[4].wait()
        pl.semaphore_wait(barrier, 1)

        def kv_send(n):
            return crossing_copy(turned.at[pl.ds(0, full), at((n % 3) * TILE, TILE, TILE)], n, n // 2 + tiles * (n % 2))

        for n in range(2 * tiles):
            tile = n // 2 + tiles * (n % 2)
            if n >= 3:
                kv_send(n - 3).wait_send()
            for i in range(items):
                turned[chunk(i), pl.ds((n % 3) * TILE, TILE)] = nn(rows_a[chunk(i)], w_cross[:, pl.ds(tile * TILE, TILE)]).astype(bf16)
            kv_send(n).start()
        for n in range(2 * tiles - 3, 2 * tiles):
            kv_send(n).wait_send()

        for n in range(2 * tiles):
            tile = n // 2 + tiles * (n % 2)
            crossing_copy(crossing.at[:, pl.ds(tile * TILE, TILE)], tile, tile).wait_recv()

        for i in range(items):
            r = chunk(i)
            value = norm_back(result[r], nt(crossing[r], w_cross[...]), 2)
            result[r] = value
            low[r] = value.astype(bf16)

        @pl.loop(0, 2)
        def _(j):
            emit(j, at_cross + j, tn(rows_a[...], crossing[:, wide(j)]))
        done = 2

        @pl.loop(0, blocks_up)
        def _(j):
            for i in range(items):
                r = chunk(i)
                slope[r, wide(j)] = (nt(low[r], w_down[wide(j)]) * slope[r, wide(j)].astype(f32)).astype(bf16)

        @pl.loop(0, blocks_up)
        def _(j):
            emit(done + j, at_down + j, tn(active[:, wide(j)], low[...]))
        done += blocks_up
        for i in range(items):
            rows_a[chunk(i)] = norm_forward(hidden[chunk(i)], 1)

        @pl.loop(0, blocks_up)
        def _(j):
            emit(done + j, at_up + j, tn(rows_a[...], slope[:, wide(j)]))
        done += blocks_up
        for i in range(items):
            r = chunk(i)
            value = result[r] + norm_back(hidden[r], nt(slope[r], w_up[...]), 1)
            result[r] = value
            low[r] = value.astype(bf16)
            rows_a[r] = nt(low[r], w_out[...]).astype(bf16)
        emit(done, at_out, tn(heads[...], low[...]))
        done += 1
        x_again = pltpu.make_async_copy(x_in, low, xsem.at[0])
        x_again.start()

        @pl.loop(0, items * pairs // 2)
        def _(it):
            i, h = it // (pairs // 2), 2 * (it % (pairs // 2))
            r = at(i * span, span, 16)
            for u in range(2):
                cq, ck, cv = (slab_of(n, h + u) for n in range(3))
                q, k, v = qkv[r, cq], qkv[r, ck], qkv[r, cv]
                both = stacked(rows_a[r, cq])
                p = prob[2 * it + u]
                ds = soft_back(p, nt(both, v))
                active[r, cq] = (joined(nn(ds, k), span) * scale).astype(bf16)
                active[r, ck] = tn(ds, stacked(q, scale)).astype(bf16)
                active[r, cv] = tn(p, both).astype(bf16)

        x_again.wait()
        for i in range(items):
            rows_a[chunk(i)] = norm_forward(low[chunk(i)].astype(f32), 0)

        @pl.loop(0, 3)
        def _(j):
            emit(done + j, at_qkv + j, tn(rows_a[...], active[:, wide(j)]))
        done += 3
        for i in range(items):
            r = chunk(i)
            grad = nt(active[r, pl.ds(0, 3 * width)], w_qkv[...])
            heads[r] = (result[r] + norm_back(low[r].astype(f32), grad, 0)).astype(bf16)
        dx_store = pltpu.make_async_copy(heads, dx_out, xsem.at[0])
        dx_store.start()
        block_store(0, 0).wait()
        block_store(1, 0).wait()
        dx_store.wait()

    @pl.when(section == 1)
    def _():
        dec = items * dec_len
        ra, rb, rc, rd = (pl.ds(n * dec, dec) for n in range(4))
        for n in (0, 1, 4, 2, 3):
            loads[n].start()
        rows_a[ra] = norm_forward(y_in[...].astype(f32), 0)
        loads[0].wait()

        @pl.loop(0, 3)
        def _(j):
            qkv[ra, wide(j)] = nn(rows_a[ra], w_qkv[:, wide(j)]).astype(bf16)

        own = self_open[...] > 0.0
        own = jnp.concatenate([own, own], axis=0)

        @pl.loop(0, pairs)
        def _(h):
            cq, ck, cv = (slab_of(n, h) for n in range(3))
            p = soft(nt(stacked(qkv[ra, cq], scale), qkv[ra, ck]), own)
            prob[h, pl.ds(0, 2 * dec), pl.ds(0, dec)] = p
            heads[ra, cq] = joined(nn(p, qkv[ra, cv]), dec).astype(bf16)

        loads[1].wait()
        value = y_in[...].astype(f32) + nn(heads[ra], w_out[...])
        hidden[ra] = value
        rows_a[rb] = norm_forward(value, 1)
        loads[4].wait()
        low[rb] = nn(rows_a[rb], w_cross[:, pl.ds(0, width)]).astype(bf16)
        loads[2].wait()
        loads[3].wait()

        part = 2 * dec_len
        spots = [(u, i) for u in range(TILE // SLAB) for i in range(items)]
        key_rows = jnp.concatenate([jnp.broadcast_to(key_open[i], (part, span)) for u, i in spots], axis=0)

        @pl.loop(0, tiles)
        def _(t):
            for tile in (t, tiles + t):
                crossing_copy(crossing.at[:, at(tile * TILE, TILE, TILE)], tile, tile).wait_recv()

            def slab(n, u):
                return at(n * width + t * TILE + u * SLAB, SLAB, SLAB)
            scores = [
                nt(stacked(low[pl.ds(dec + i * dec_len, dec_len), slab(0, u)], scale), crossing[chunk(i), slab(0, u)])
                for u, i in spots
            ]
            p = soft(jnp.concatenate(scores, axis=0), key_rows > 0.0)
            for u in range(TILE // SLAB):
                prob[pairs + t * (TILE // SLAB) + u, pl.ds(0, items * part)] = p[u * items * part : (u + 1) * items * part]
            for n, (u, i) in enumerate(spots):
                both = nn(p[n * part : (n + 1) * part], crossing[chunk(i), slab(1, u)])
                heads[pl.ds(dec + i * dec_len, dec_len), slab(0, u)] = joined(both, dec_len).astype(bf16)

        value = hidden[ra] + nn(heads[rb], w_cross[:, pl.ds(width, width)])
        hidden[rb] = value
        rows_a[rc] = norm_forward(value, 2)

        @pl.loop(0, blocks_up)
        def _(j):
            e, s = gelu_both(nn(rows_a[rc], w_up[:, wide(j)]))
            active[ra, wide(j)] = e.astype(bf16)
            active[rb, wide(j)] = (nt(dz_in[...], w_down[wide(j)]) * s).astype(bf16)

        value = dz_in[...].astype(f32) + norm_back(hidden[rb], nt(active[rb], w_up[...]), 2)
        result[ra] = value
        low[ra] = value.astype(bf16)
        rows_a[rd] = nt(low[ra], w_cross[:, pl.ds(width, width)]).astype(bf16)
        pl.semaphore_wait(barrier, 1)

        def kv_back(tile):
            return crossing_copy(slope.at[:, at(tile * TILE, TILE, TILE)], tile, tile)

        @pl.loop(0, tiles)
        def _(t):
            def slab(n, u):
                return at(n * width + t * TILE + u * SLAB, SLAB, SLAB)
            both = [stacked(rows_a[pl.ds(3 * dec + i * dec_len, dec_len), slab(0, u)]) for u, i in spots]
            dp = jnp.concatenate([nt(both[n], crossing[chunk(i), slab(1, u)]) for n, (u, i) in enumerate(spots)], axis=0)
            p = jnp.concatenate(
                [prob[pairs + t * (TILE // SLAB) + u, pl.ds(0, items * part)] for u in range(TILE // SLAB)], axis=0
            )
            ds = soft_back(p, dp)
            for n, (u, i) in enumerate(spots):
                lines = slice(n * part, (n + 1) * part)
                q = stacked(low[pl.ds(dec + i * dec_len, dec_len), slab(0, u)], scale)
                slope[chunk(i), slab(0, u)] = tn(ds[lines], q).astype(bf16)
                slope[chunk(i), slab(1, u)] = tn(p[lines], both[n]).astype(bf16)
            kv_back(t).start()
            kv_back(tiles + t).start()
            for n, (u, i) in enumerate(spots):
                lines = slice(n * part, (n + 1) * part)
                back = joined(nn(ds[lines], crossing[chunk(i), slab(0, u)]), dec_len) * scale
                low[pl.ds(3 * dec + i * dec_len, dec_len), slab(0, u)] = back.astype(bf16)

        @pl.loop(0, blocks_up)
        def _(j):
            emit(j, at_down + j, tn(active[ra, wide(j)], dz_in[...]))
        done = blocks_up

        @pl.loop(0, blocks_up)
        def _(j):
            emit(done + j, at_up + j, tn(rows_a[rc], active[rb, wide(j)]))
        done += blocks_up
        emit(done, at_cross + 1, tn(heads[rb], low[ra]))
        emit(done + 1, at_cross, tn(rows_a[rb], low[rd]))
        done += 2
        value = result[ra] + norm_back(hidden[ra], nt(low[rd], w_cross[:, pl.ds(0, width)]), 1)
        result[ra] = value
        low[ra] = value.astype(bf16)
        emit(done, at_out, tn(heads[ra], low[ra]))
        done += 1
        rows_a[rd] = nt(low[ra], w_out[...]).astype(bf16)

        @pl.loop(0, pairs)
        def _(h):
            cq, ck, cv = (slab_of(n, h) for n in range(3))
            q, k, v = qkv[ra, cq], qkv[ra, ck], qkv[ra, cv]
            both = stacked(rows_a[rd, cq])
            p = prob[h, pl.ds(0, 2 * dec), pl.ds(0, dec)]
            ds = soft_back(p, nt(both, v))
            qkv[rb, cq] = (joined(nn(ds, k), dec) * scale).astype(bf16)
            qkv[rb, ck] = tn(ds, stacked(q, scale)).astype(bf16)
            qkv[rb, cv] = tn(p, both).astype(bf16)

        @pl.loop(0, 3)
        def _(j):
            emit(done + j, at_qkv + j, tn(rows_a[ra], qkv[rb, wide(j)]))
        done += 3
        grad = nt(qkv[rb], w_qkv[...])
        dy_out[...] = (result[ra] + norm_back(y_in[...].astype(f32), grad, 0)).astype(bf16)
        dec_out[...] = (hidden[rb] + nn(active[ra], w_down[...])).astype(bf16)
        block_store(0, 0).wait()
        block_store(1, 0).wait()
        for tile in range(2 * tiles):
            kv_back(tile).wait_send()


def fused(x, y, dz, weights, gain, shift, key_open, self_open, items, span, dec_len, collective_id):
    wq, wo, wi, wd, wc = weights
    width, hidden_units = wi.shape
    full = items * span
    dec = items * dec_len
    count = sum(w.size for w in weights) // (width * width)
    here = pl.BlockSpec(memory_space=pltpu.VMEM)
    there = pl.BlockSpec(memory_space=pl.ANY)
    pairs = width // SLAB
    return pl.pallas_call(
        functools.partial(fused_kernel, items, span, dec_len),
        out_shape=(
            jax.ShapeDtypeStruct((count, width, width), bf16),
            jax.ShapeDtypeStruct((8, width), f32),
            jax.ShapeDtypeStruct((full, width), bf16),
            jax.ShapeDtypeStruct((dec, width), bf16),
            jax.ShapeDtypeStruct((dec, width), bf16),
        ),
        in_specs=[there, here, here] + [there] * 5 + [here] * 4,
        out_specs=(there, here, there, here, here),
        scratch_shapes=[
            pltpu.VMEM(wq.shape, bf16),
            pltpu.VMEM(wo.shape, bf16),
            pltpu.VMEM(wi.shape, bf16),
            pltpu.VMEM(wd.shape, bf16),
            pltpu.VMEM(wc.shape, bf16),
            pltpu.VMEM((full, 3 * width), bf16),
            pltpu.VMEM((items * pairs, 2 * span, span), bf16),
            pltpu.VMEM((full, width), bf16),
            pltpu.VMEM((full, width), bf16),
            pltpu.VMEM((full, width), bf16),
            pltpu.VMEM((full, width), bf16),
            pltpu.VMEM((full, width), f32),
            pltpu.VMEM((full, width), f32),
            pltpu.VMEM((full, hidden_units), bf16),
            pltpu.VMEM((full, hidden_units), bf16),
            pltpu.VMEM((full, 2 * width), bf16),
            pltpu.VMEM((2, width, width), bf16),
            pltpu.SemaphoreType.DMA((5,)),
            pltpu.SemaphoreType.DMA((1,)),
            pltpu.SemaphoreType.DMA((2,)),
            pltpu.SemaphoreType.DMA((2 * width // TILE,)),
            pltpu.SemaphoreType.DMA((2 * width // TILE,)),
        ],
        compiler_params=pltpu.CompilerParams(
            collective_id=collective_id, has_side_effects=True, vmem_limit_bytes=63 * 2**20
        ),
    )(x, y, dz, wq, wo, wi, wd, wc, gain, shift, key_open, self_open)


NZ = 4

def place():
    b = lax.axis_index("batch"); c = lax.axis_index("section")
    return b % 2, (b // 2) % 2, b // 4, c

def bid(x, y, z):
    return z * 4 + y * 2 + x

def ar_kernel(pairs, rows, width, across_block, g, norms, out, norms_out, acc, res, rx, up, dn, ry, nbuf, lsem, asend, arecv, zsend, zrecv, nsem):
    x, y, z, c = place()
    half, block, share = rows // 2, rows // 8, rows // 16

    def dev(x, y, z):
        return (c, bid(x, y, z))

    across = (dev(1 - x, y, z), dev(x, 1 - y, z))
    above, below = dev(x, y, z + 1), dev(x, y, z - 1)
    bit = (x, y)

    barrier = pltpu.get_barrier_semaphore()
    faraway = dev(x, y, (z + 2) % NZ)
    for d in across + (faraway,):
        pl.semaphore_signal(barrier, inc=1, device_id=d, device_id_type=MESH)

    @pl.when(z < NZ - 1)
    def _():
        pl.semaphore_signal(barrier, inc=1, device_id=above, device_id_type=MESH)

    @pl.when(z > 0)
    def _():
        pl.semaphore_signal(barrier, inc=1, device_id=below, device_id_type=MESH)

    pl.semaphore_wait(barrier, 3 + (z + NZ - 1) // NZ + (2 * NZ - 2 - z) // NZ)

    def rdma(src, dst, send, recv, device):
        return pltpu.make_async_remote_copy(src_ref=src, dst_ref=dst, send_sem=send, recv_sem=recv, device_id=device, device_id_type=MESH)

    def parts(t, f):
        p = 2 * t + f
        a, b = bit[f], bit[1 - f]
        own = a * half
        other = (1 - a) * half
        return p, own, other, b

    def rows_at(start, n):
        return pl.ds(pl.multiple_of(start, 16), n)

    def panel_of(array, p, start, n):
        columns = pl.ds(pl.multiple_of(p % across_block * width, 128), width)
        return array.at[p // across_block, rows_at(start, n), columns]

    def own_load(t, f):
        p, own, other, b = parts(t, f)
        return pltpu.make_async_copy(panel_of(g, p, own, half), acc.at[p], lsem.at[p, 0])

    def own_store(t, f, k):
        p, own, other, b = parts(t, f)
        start = own if k == 0 else other
        return pltpu.make_async_copy(res.at[p, rows_at(start, half)], panel_of(out, p, start, half), lsem.at[p, k + 1])

    def rs_a(t, f):
        p, own, other, b = parts(t, f)
        return rdma(panel_of(g, p, other, half), rx.at[p], asend.at[p, 0], arecv.at[p, 0], across[f])

    def rs_up(t, f, k):
        p, own, other, b = parts(t, f)
        return rdma(acc.at[p, pl.ds(k * block, block)], up.at[p, k], zsend.at[p, 0, k], zrecv.at[p, 0, k], above)

    def rs_dn(t, f, k):
        p, own, other, b = parts(t, f)
        return rdma(acc.at[p, pl.ds(k * block, block)], dn.at[p, k], zsend.at[p, 1, k], zrecv.at[p, 1, k], below)

    def rs_b(t, f):
        p, own, other, b = parts(t, f)
        return rdma(acc.at[p, rows_at(z * block + (1 - b) * share, share)], ry.at[p], asend.at[p, 1], arecv.at[p, 1], across[1 - f])

    def ag_b(t, f):
        p, own, other, b = parts(t, f)
        s = res.at[p, rows_at(own + z * block + b * share, share)]
        return rdma(s, s, asend.at[p, 2], arecv.at[p, 2], across[1 - f])

    def ag_up(t, f, k):
        p, own, other, b = parts(t, f)
        s = res.at[p, rows_at(own + k * block, block)]
        return rdma(s, s, zsend.at[p, 2, k], zrecv.at[p, 2, k], above)

    def ag_dn(t, f, k):
        p, own, other, b = parts(t, f)
        s = res.at[p, rows_at(own + k * block, block)]
        return rdma(s, s, zsend.at[p, 3, k], zrecv.at[p, 3, k], below)

    def ag_a(t, f):
        p, own, other, b = parts(t, f)
        s = res.at[p, rows_at(own, half)]
        return rdma(s, s, asend.at[p, 3], arecv.at[p, 3], across[f])

    def s0(t, f):
        rs_a(t, f).start()
        own_load(t, f).start()

    def s1(t, f):
        p, own, other, b = parts(t, f)
        own_load(t, f).wait()
        rs_a(t, f).wait()
        acc[p] = acc[p] + rx[p]

        @pl.when(z == 0)
        def _():
            for k in range(NZ - 1, 0, -1):
                rs_up(t, f, k).start()

        @pl.when(z == NZ - 1)
        def _():
            for k in range(NZ - 1):
                rs_dn(t, f, k).start()

    def chain(t, f, j):
        p, own, other, b = parts(t, f)

        @pl.when(z == j)
        def _():
            for k in range(NZ - 1, j - 1, -1):
                rs_up(t, f, k).wait_recv()
                r = pl.ds(k * block, block)
                acc[p, r] = acc[p, r] + up[p, k]
                if k > j:
                    rs_up(t, f, k).start()

        @pl.when(z == NZ - 1 - j)
        def _():
            for k in range(NZ - j):
                rs_dn(t, f, k).wait_recv()
                r = pl.ds(k * block, block)
                acc[p, r] = acc[p, r] + dn[p, k]
                if k < NZ - 1 - j:
                    rs_dn(t, f, k).start()

    def s4(t, f):
        chain(t, f, NZ - 1)
        rs_b(t, f).start()

    def s5(t, f):
        p, own, other, b = parts(t, f)
        rs_b(t, f).wait()
        mine = z * block + b * share
        res[p, rows_at(own + mine, share)] = acc[p, rows_at(mine, share)] + ry[p]
        ag_b(t, f).start()

    def s6(t, f):
        ag_b(t, f).wait()

        @pl.when(z < NZ - 1)
        def _():
            ag_up(t, f, z).start()

        @pl.when(z > 0)
        def _():
            ag_dn(t, f, z).start()

    def spread(t, f, j):
        @pl.when(z >= j)
        def _():
            ag_up(t, f, z - j).wait_recv()

            @pl.when(z < NZ - 1)
            def _():
                ag_up(t, f, z - j).start()

        @pl.when(z + j <= NZ - 1)
        def _():
            ag_dn(t, f, z + j).wait_recv()

            @pl.when(z > 0)
            def _():
                ag_dn(t, f, z + j).start()

    def s9(t, f):
        spread(t, f, NZ - 1)
        ag_a(t, f).start()
        own_store(t, f, 0).start()

    def s10(t, f):
        ag_a(t, f).wait()
        own_store(t, f, 1).start()
        for k in range(NZ):
            @pl.when((z < k))
            def _(k=k):
                rs_up(t, f, k).wait_send()

            @pl.when((z > k))
            def _(k=k):
                rs_dn(t, f, k).wait_send()

            @pl.when((k <= z) & (z < NZ - 1))
            def _(k=k):
                ag_up(t, f, k).wait_send()

            @pl.when((k >= z) & (z > 0))
            def _(k=k):
                ag_dn(t, f, k).wait_send()

    def s11(t, f):
        own_store(t, f, 0).wait()
        own_store(t, f, 1).wait()

    mates = across + (dev(x, y, z + 1 - 2 * (z % 2)), faraway)

    def norm_swap(j):
        return rdma(norms_out, nbuf.at[j], nsem.at[0, j], nsem.at[1, j], mates[j])

    norms_out[...] = norms[...]
    norm_swap(0).start()

    stages = [s0, s1] + [functools.partial(lambda j, t, f: chain(t, f, j), j) for j in range(1, NZ - 1)] + [s4, s5, s6] + [
        functools.partial(lambda j, t, f: spread(t, f, j), j) for j in range(1, NZ - 1)] + [s9, s10, s11]
    ahead = 2

    def tick(tau, carry):
        for j in range(4):

            @pl.when(tau == 3 * j + 3)
            def _(j=j):
                norm_swap(j).wait()
                norms_out[...] = norms_out[...] + nbuf[j]
                if j < 3:
                    norm_swap(j + 1).start()

        for i, stage in enumerate(stages):
            lag = 0 if i == 0 else i - 1 + ahead
            t = tau - lag

            @pl.when((t >= 0) & (t < pairs))
            def _(stage=stage, t=t):
                stage(t, 0)
                stage(t, 1)
        return carry
    lax.fori_loop(0, pairs + len(stages) - 2 + ahead, tick, 0)


def all_reduce(g, norms, collective_id):
    blocks, rows, block_width = g.shape
    width = 256
    across_block = block_width // width
    n = blocks * across_block
    half, block, share = rows // 2, rows // 8, rows // 16
    bf = jnp.bfloat16
    return pl.pallas_call(
        functools.partial(ar_kernel, n // 2, rows, width, across_block),
        out_shape=(jax.ShapeDtypeStruct(g.shape, bf), jax.ShapeDtypeStruct(norms.shape, norms.dtype)),
        in_specs=[pl.BlockSpec(memory_space=pl.ANY), pl.BlockSpec(memory_space=pltpu.VMEM)],
        out_specs=(pl.BlockSpec(memory_space=pl.ANY), pl.BlockSpec(memory_space=pltpu.VMEM)),
        scratch_shapes=[
            pltpu.VMEM((n, half, width), bf),
            pltpu.VMEM((n, rows, width), bf),
            pltpu.VMEM((n, half, width), bf),
            pltpu.VMEM((n, NZ, block, width), bf),
            pltpu.VMEM((n, NZ, block, width), bf),
            pltpu.VMEM((n, share, width), bf),
            pltpu.VMEM((4,) + norms.shape, norms.dtype),
            pltpu.SemaphoreType.DMA((n, 3)),
            pltpu.SemaphoreType.DMA((n, 4)),
            pltpu.SemaphoreType.DMA((n, 4)),
            pltpu.SemaphoreType.DMA((n, 4, NZ)),
            pltpu.SemaphoreType.DMA((n, 4, NZ)),
            pltpu.SemaphoreType.DMA((2, 4)),
        ],
        compiler_params=pltpu.CompilerParams(collective_id=collective_id, has_side_effects=True, vmem_limit_bytes=60 * 2**20),
    )(g, norms)


def unpack_kernel(counts, panels, *outs):
    step = pl.program_id(0)
    first = 0
    for count, out in zip(counts, outs):

        @pl.when((step >= first) & (step < first + count))
        def _(out=out):
            out[0] = panels[0].astype(f32)

        first += count


def unpack(panels, shapes):
    total, high, wide = panels.shape
    counts = [rows * columns // (high * wide) for rows, columns in shapes]
    out_specs = []
    first = 0
    for (rows, columns), count in zip(shapes, counts):
        across = columns // wide

        def place_of(step, first=first, count=count, across=across):
            own = jnp.clip(step - first, 0, count - 1)
            return 0, own // across, own % across

        out_specs.append(pl.BlockSpec((1, high, wide), place_of))
        first += count
    return pl.pallas_call(
        functools.partial(unpack_kernel, counts),
        grid=(total,),
        out_shape=[jax.ShapeDtypeStruct((1,) + shape, f32) for shape in shapes],
        in_specs=[pl.BlockSpec((1, high, wide), lambda step: (step, 0, 0))],
        out_specs=out_specs,
        compiler_params=pltpu.CompilerParams(vmem_limit_bytes=48 * 2**20),
    )(panels)


def per_device(
    enc_input,
    dec_input,
    out_grad,
    attn_qkv,
    attn_out,
    mlp_in,
    mlp_out,
    cross_proj,
    norm_gain,
    norm_shift,
    image_count,
    prefix_len,
    suffix_len,
):
    section = lax.axis_index("section")
    items, enc_len, width = enc_input.shape
    dec_len = dec_input.shape[1]
    span = -(-enc_len // 16) * 16
    weights = (attn_qkv[0], attn_out[0], mlp_in[0], mlp_out[0], cross_proj[0])
    positions = jnp.arange(span, dtype=jnp.int32)[None, :]
    has_image = (jnp.arange(items, dtype=jnp.int32) < image_count[0])[:, None]
    key_open = jnp.where(positions < PATCHES, has_image, positions - PATCHES < prefix_len[:, None])
    key_open = (key_open & (positions < enc_len)).astype(f32)[:, None, :]
    places = jnp.arange(items * dec_len, dtype=jnp.int32)
    item, spot = places // dec_len, places % dec_len
    self_open = (
        (item[:, None] == item[None, :])
        & (spot[None, :] <= spot[:, None])
        & (spot[None, :] < jnp.repeat(suffix_len, dec_len)[None, :])
    ).astype(f32)
    x = jnp.pad(enc_input, ((0, 0), (0, span - enc_len), (0, 0))).reshape(items * span, width)
    panels, norms, dx, dec_out, dy = fused(
        x,
        dec_input.reshape(-1, width),
        out_grad.reshape(-1, width),
        weights,
        norm_gain[0].astype(f32),
        norm_shift[0].astype(f32),
        key_open,
        self_open,
        items,
        span,
        dec_len,
        1,
    )
    if lax.axis_size("batch") == 16:
        panels, norms = all_reduce(panels, norms, 0)
    else:
        panels, norms = lax.psum(panels, "batch"), lax.psum(norms, "batch")
    dx, dec_out, dy, panels = lax.optimization_barrier((dx, dec_out, dy, panels))
    order = (0, 1, 4, 2, 3)
    blocks = unpack(panels, [weights[n].shape for n in order])
    grads = [blocks[order.index(n)] for n in range(len(order))]
    half = width // 2
    on_first = section == 0
    own_start, other_start = section * half, (1 - section) * half

    def columns(array, start):
        return lax.dynamic_slice_in_dim(array, start, half, 2)

    def swapped(array):
        return lax.ppermute(columns(array, other_start), "section", [(0, 1), (1, 0)])

    dx = dx.reshape(items, span, width)[:, :enc_len]
    dec_out = dec_out.reshape(dec_input.shape)
    dy = dy.reshape(dec_input.shape)
    return (
        jnp.where(on_first, swapped(dec_out), columns(dec_out, own_start)),
        jnp.where(on_first, columns(dx, own_start), swapped(dx)),
        jnp.where(on_first, swapped(dy), columns(dy, own_start)),
        *grads,
        norms[None, :3],
        norms[None, 3:6],
    )


def solution(mesh):
    items = P("batch", None, None)
    matrix = P("section", None, None)
    halves = P("batch", None, "section")
    return jax.shard_map(
        per_device,
        mesh=mesh,
        in_specs=(items,) * 3 + (matrix,) * 7 + (P("batch"),) * 3,
        out_specs=(halves,) * 3 + (matrix,) * 7,
        check_vma=False,
    )
```

```python
import functools

import jax
import jax.numpy as jnp
from jax import lax
from jax.experimental import pallas as pl
from jax.experimental.pallas import tpu as pltpu
from jax.sharding import PartitionSpec as P

PATCHES = 196
MESH = pl.DeviceIdType.MESH
bf16, f32 = jnp.bfloat16, jnp.float32
epsilon = 1e-06
far_below = -1000000000.0
HEAD = 64
SLAB = 128
TILE = 256
GELU_A = 0.7978845608028654
GELU_B = 0.044715


NZ = 4


def place():
    b = lax.axis_index("batch")
    return b % 2, (b // 2) % 2, b // 4, lax.axis_index("section")


def bid(x, y, z):
    return z * 4 + y * 2 + x


def nn(a, b):
    return jnp.dot(a, b, preferred_element_type=f32)


def nt(a, b):
    return lax.dot_general(a, b, (((1,), (1,)), ((), ())), preferred_element_type=f32)


def tn(a, b):
    return lax.dot_general(a, b, (((0,), (0,)), ((), ())), preferred_element_type=f32)


def normal(v):
    centered = v - jnp.mean(v, axis=-1, keepdims=True)
    spread = lax.rsqrt(jnp.mean(centered * centered, axis=-1, keepdims=True) + epsilon)
    return centered * spread, spread


def gelu_both(u):
    square = u * u
    bent = jnp.tanh(GELU_A * u * (1.0 + GELU_B * square))
    half = 0.5 * (1.0 + bent)
    slope = half + 0.5 * u * (1.0 - bent * bent) * (GELU_A * (1.0 + 3.0 * GELU_B * square))
    return u * half, slope


def at(start, size, unit):
    return pl.ds(pl.multiple_of(start, unit), size)


def fused_kernel(items, span, dec_len, gathers,
                 x_in, y_in, dz_in, wq_in, wo_in, wi_in, wd_in, wc_in, gain, shift, key_open, self_open,
                 panels, norms, dx_out, dec_out, dy_out, pool,
                 w_qkv, w_out, w_up, w_down, w_cross,
                 qkv, prob, heads, low, rows_a, turned, hidden, result, active, slope, crossing, stage,
                 wsem, xsem, psem, send_sem, recv_sem, zsend, zrecv, asend, arecv, lsem, hsend, hrecv):
    width = w_out.shape[0]
    hidden_units = w_up.shape[1]
    pairs = width // SLAB
    full = items * span
    blocks_up = hidden_units // width
    at_qkv, at_out, at_cross, at_up, at_down = 0, 3, 4, 6, 7
    section = lax.axis_index("section")
    chip = lax.axis_index("batch")
    other = (1 - section, chip)

    barrier = pltpu.get_barrier_semaphore()
    pl.semaphore_signal(barrier, inc=1, device_id=other, device_id_type=MESH)
    x, y, z, _ = place()
    beside = ((section, bid(1 - x, y, z)), (section, bid(x, 1 - y, z)))
    above, below = (section, bid(x, y, z + 1)), (section, bid(x, y, z - 1))
    if gathers:

        @pl.when(section == 1)
        def _():
            for device in beside:
                pl.semaphore_signal(barrier, inc=1, device_id=device, device_id_type=MESH)

            @pl.when(z < NZ - 1)
            def _():
                pl.semaphore_signal(barrier, inc=1, device_id=above, device_id_type=MESH)

            @pl.when(z > 0)
            def _():
                pl.semaphore_signal(barrier, inc=1, device_id=below, device_id_type=MESH)

    def pool_copy(kind, half, src, dst, send, recv, device):
        return pltpu.make_async_remote_copy(
            src_ref=src, dst_ref=dst, send_sem=send, recv_sem=recv, device_id=device, device_id_type=MESH
        )

    def half_rows(half):
        size = items * dec_len // 2
        return pl.ds(half * size, size)

    def along_z(kind, half, way, k, source=None):
        spot = pool.at[kind, k, y, x, half_rows(half)]
        return pool_copy(
            kind, half, spot if source is None else source, spot,
            zsend.at[kind, half, way, k], zrecv.at[kind, half, way, k], (above, below)[way],
        )

    def along_a(kind, half):
        spot = pool.at[kind, :, y, x, half_rows(half)]
        return pool_copy(kind, half, spot, spot, asend.at[kind, half, 0], arecv.at[kind, half, 0], beside[half])

    def along_b(kind, half):
        spot = pool.at[kind, :, y, :, half_rows(half)] if half == 0 else pool.at[kind, :, :, x, half_rows(half)]
        return pool_copy(kind, half, spot, spot, asend.at[kind, half, 1], arecv.at[kind, half, 1], beside[1 - half])

    def own_copy(kind, source):
        return pltpu.make_async_copy(source, pool.at[kind, z, y, x], lsem.at[kind])

    def gather_step(kind, step, source):
        if not gathers:
            return
        if step == 0:
            own_copy(kind, source).start()
        for half in range(2):
            if step == 0:
                mine = source.at[half_rows(half)]

                @pl.when(z < NZ - 1)
                def _():
                    along_z(kind, half, 0, z, mine).start()

                @pl.when(z > 0)
                def _():
                    along_z(kind, half, 1, z, mine).start()
            elif step < NZ:

                @pl.when(z >= step)
                def _():
                    along_z(kind, half, 0, z - step).wait_recv()

                    @pl.when(z < NZ - 1)
                    def _():
                        along_z(kind, half, 0, z - step).start()

                @pl.when(z + step <= NZ - 1)
                def _():
                    along_z(kind, half, 1, z + step).wait_recv()

                    @pl.when(z > 0)
                    def _():
                        along_z(kind, half, 1, z + step).start()
            elif step == NZ:
                if half == 0:
                    own_copy(kind, source).wait()
                along_a(kind, half).start()
            elif step == NZ + 1:
                along_a(kind, half).wait_recv()
                along_b(kind, half).start()
            else:
                along_b(kind, half).wait()
                along_a(kind, half).wait_send()
                for k in range(NZ):

                    @pl.when((k <= z) & (z < NZ - 1))
                    def _(k=k):
                        along_z(kind, half, 0, k).wait_send()

                    @pl.when((k >= z) & (z > 0))
                    def _(k=k):
                        along_z(kind, half, 1, k).wait_send()

    weights = ((wq_in, w_qkv), (wo_in, w_out), (wi_in, w_up), (wd_in, w_down), (wc_in, w_cross))
    loads = [pltpu.make_async_copy(src, dst, wsem.at[n]) for n, (src, dst) in enumerate(weights)]

    lane = lax.broadcasted_iota(jnp.int32, (1, SLAB), 1)
    is_first = lane < HEAD
    mask_a = jnp.where(is_first, 1.0, 0.0).astype(bf16)
    mask_b = jnp.where(is_first, 0.0, 1.0).astype(bf16)
    scale = HEAD ** (-0.5)

    def stacked(slab, factor=1.0):
        return jnp.concatenate([slab * (mask_a * factor).astype(bf16), slab * (mask_b * factor).astype(bf16)], axis=0)

    def joined(both, rows):
        return jnp.where(is_first, both[:rows], both[rows:])

    def soft(scores, is_open):
        scores = jnp.where(is_open, scores, far_below)
        grown = jnp.exp(scores - jnp.max(scores, axis=-1, keepdims=True))
        return (grown * (1.0 / jnp.sum(grown, axis=-1, keepdims=True))).astype(bf16)

    def soft_back(p_low, dp):
        p = p_low.astype(f32)
        t = p * dp
        return (t - p * jnp.sum(t, axis=-1, keepdims=True)).astype(bf16)

    def wide(n):
        return at(n * width, width, width)

    def slab_of(n, h):
        return at(n * width + h * SLAB, SLAB, SLAB)

    def chunk(i):
        return pl.ds(i * span, span)

    def block_store(n, index):
        return pltpu.make_async_copy(stage.at[n % 2], panels.at[index], psem.at[n % 2])

    def emit(n, index, value):
        @pl.when(n >= 2)
        def _():
            block_store(n, index).wait()
        stage[n % 2] = value.astype(bf16)
        block_store(n, index).start()

    def norm_forward(value, index):
        unit, _ = normal(value)
        return (unit * gain[index : index + 1] + shift[index : index + 1]).astype(bf16)

    def norm_back(value, grad, index):
        unit, spread = normal(value)
        norms[index : index + 1] += jnp.sum(grad * unit, axis=0, keepdims=True)
        norms[3 + index : 4 + index] += jnp.sum(grad, axis=0, keepdims=True)
        scaled = grad * gain[index : index + 1]
        return spread * (
            scaled
            - jnp.mean(scaled, axis=-1, keepdims=True)
            - unit * jnp.mean(scaled * unit, axis=-1, keepdims=True)
        )

    def crossing_copy(source, n, tile):
        return pltpu.make_async_remote_copy(
            src_ref=source,
            dst_ref=crossing.at[:, at(tile * TILE, TILE, TILE)],
            send_sem=send_sem.at[n],
            recv_sem=recv_sem.at[tile],
            device_id=other,
            device_id_type=MESH,
        )

    def end_copy(n):
        dec = items * dec_len
        return pltpu.make_async_remote_copy(
            src_ref=heads.at[pl.ds((2 + n) * dec, dec), pl.ds(0, width // 2)],
            dst_ref=(dy_out, dec_out)[n],
            send_sem=hsend.at[n],
            recv_sem=hrecv.at[n],
            device_id=other,
            device_id_type=MESH,
        )

    tiles = width // TILE
    norms[...] = jnp.zeros_like(norms)

    @pl.when(section == 0)
    def _():
        x_load = pltpu.make_async_copy(x_in, low, xsem.at[0])
        x_load.start()
        for load in loads:
            load.start()
        x_load.wait()
        for i in range(items):
            rows_a[chunk(i)] = norm_forward(low[chunk(i)].astype(f32), 0)
        loads[0].wait()

        @pl.loop(0, 3)
        def _(j):
            for i in range(items):
                qkv[chunk(i), wide(j)] = nn(rows_a[chunk(i)], w_qkv[:, wide(j)]).astype(bf16)

        @pl.loop(0, items * pairs // 2)
        def _(it):
            i, h = it // (pairs // 2), 2 * (it % (pairs // 2))
            r = at(i * span, span, 16)
            for u in range(2):
                q, k, v = (qkv[r, slab_of(n, h + u)] for n in range(3))
                p = soft(nt(stacked(q, scale), k), key_open[i] > 0.0)
                prob[2 * it + u] = p
                heads[r, slab_of(0, h + u)] = joined(nn(p, v), span).astype(bf16)

        loads[1].wait()
        for i in range(items):
            r = chunk(i)
            value = low[r].astype(f32) + nn(heads[r], w_out[...])
            hidden[r] = value
            rows_a[r] = norm_forward(value, 1)
        loads[2].wait()

        @pl.loop(0, blocks_up)
        def _(j):
            for i in range(items):
                e, s = gelu_both(nn(rows_a[chunk(i)], w_up[:, wide(j)]))
                active[chunk(i), wide(j)] = e.astype(bf16)
                slope[chunk(i), wide(j)] = s.astype(bf16)

        loads[3].wait()
        for i in range(items):
            r = chunk(i)
            value = hidden[r] + nn(active[r], w_down[...])
            result[r] = value
            rows_a[r] = norm_forward(value, 2)
        loads[4].wait()
        pl.semaphore_wait(barrier, 1)

        def kv_send(n):
            return crossing_copy(turned.at[pl.ds(0, full), at((n % 3) * TILE, TILE, TILE)], n, n // 2 + tiles * (n % 2))

        for n in range(2 * tiles):
            tile = n // 2 + tiles * (n % 2)
            if n >= 3:
                kv_send(n - 3).wait_send()
            for i in range(items):
                turned[chunk(i), pl.ds((n % 3) * TILE, TILE)] = nn(rows_a[chunk(i)], w_cross[:, pl.ds(tile * TILE, TILE)]).astype(bf16)
            kv_send(n).start()
        for n in range(2 * tiles - 3, 2 * tiles):
            kv_send(n).wait_send()

        for n in range(2 * tiles):
            tile = n // 2 + tiles * (n % 2)
            crossing_copy(crossing.at[:, pl.ds(tile * TILE, TILE)], tile, tile).wait_recv()

        for i in range(items):
            r = chunk(i)
            value = norm_back(result[r], nt(crossing[r], w_cross[...]), 2)
            result[r] = value
            low[r] = value.astype(bf16)

        @pl.loop(0, 2)
        def _(j):
            emit(j, at_cross + j, tn(rows_a[...], crossing[:, wide(j)]))
        done = 2

        @pl.loop(0, blocks_up)
        def _(j):
            for i in range(items):
                r = chunk(i)
                slope[r, wide(j)] = (nt(low[r], w_down[wide(j)]) * slope[r, wide(j)].astype(f32)).astype(bf16)

        @pl.loop(0, blocks_up)
        def _(j):
            emit(done + j, at_down + 2 * j, tn(active[:, wide(j)], low[...]))
        done += blocks_up
        for i in range(items):
            rows_a[chunk(i)] = norm_forward(hidden[chunk(i)], 1)

        @pl.loop(0, blocks_up)
        def _(j):
            emit(done + j, at_up + 2 * j, tn(rows_a[...], slope[:, wide(j)]))
        done += blocks_up
        for i in range(items):
            r = chunk(i)
            value = result[r] + norm_back(hidden[r], nt(slope[r], w_up[...]), 1)
            result[r] = value
            low[r] = value.astype(bf16)
            rows_a[r] = nt(low[r], w_out[...]).astype(bf16)
        emit(done, at_out, tn(heads[...], low[...]))
        done += 1
        x_again = pltpu.make_async_copy(x_in, low, xsem.at[0])
        x_again.start()

        @pl.loop(0, items * pairs // 2)
        def _(it):
            i, h = it // (pairs // 2), 2 * (it % (pairs // 2))
            r = at(i * span, span, 16)
            for u in range(2):
                cq, ck, cv = (slab_of(n, h + u) for n in range(3))
                q, k, v = qkv[r, cq], qkv[r, ck], qkv[r, cv]
                both = stacked(rows_a[r, cq])
                p = prob[2 * it + u]
                ds = soft_back(p, nt(both, v))
                active[r, cq] = (joined(nn(ds, k), span) * scale).astype(bf16)
                active[r, ck] = tn(ds, stacked(q, scale)).astype(bf16)
                active[r, cv] = tn(p, both).astype(bf16)

        x_again.wait()
        for i in range(items):
            rows_a[chunk(i)] = norm_forward(low[chunk(i)].astype(f32), 0)

        @pl.loop(0, 3)
        def _(j):
            emit(done + j, at_qkv + j, tn(rows_a[...], active[:, wide(j)]))
        done += 3
        for i in range(items):
            r = chunk(i)
            grad = nt(active[r, pl.ds(0, 3 * width)], w_qkv[...])
            heads[r] = (result[r] + norm_back(low[r].astype(f32), grad, 0)).astype(bf16)
        dx_store = pltpu.make_async_copy(heads, dx_out, xsem.at[0])
        dx_store.start()
        block_store(0, 0).wait()
        block_store(1, 0).wait()
        dx_store.wait()
        for n in range(2):
            end_copy(n).wait_recv()

    @pl.when(section == 1)
    def _():
        dec = items * dec_len
        ra, rb, rc, rd = (pl.ds(n * dec, dec) for n in range(4))
        for n in (0, 1, 4, 2, 3):
            loads[n].start()
        rows_a[ra] = norm_forward(y_in[...].astype(f32), 0)
        if gathers:
            pl.semaphore_wait(barrier, 3 + (z + NZ - 1) // NZ + (2 * NZ - 2 - z) // NZ)
        gather_step(0, 0, dz_in)
        loads[0].wait()

        @pl.loop(0, 3)
        def _(j):
            qkv[ra, wide(j)] = nn(rows_a[ra], w_qkv[:, wide(j)]).astype(bf16)

        own = self_open[...] > 0.0
        own = jnp.concatenate([own, own], axis=0)

        @pl.loop(0, pairs)
        def _(h):
            cq, ck, cv = (slab_of(n, h) for n in range(3))
            p = soft(nt(stacked(qkv[ra, cq], scale), qkv[ra, ck]), own)
            prob[h, pl.ds(0, 2 * dec), pl.ds(0, dec)] = p
            heads[ra, cq] = joined(nn(p, qkv[ra, cv]), dec).astype(bf16)

        gather_step(0, 1, dz_in)
        loads[1].wait()
        value = y_in[...].astype(f32) + nn(heads[ra], w_out[...])
        hidden[ra] = value
        rows_a[rb] = norm_forward(value, 1)
        loads[4].wait()
        low[rb] = nn(rows_a[rb], w_cross[:, pl.ds(0, width)]).astype(bf16)
        loads[2].wait()
        loads[3].wait()
        for step in range(2, NZ + 3):
            gather_step(0, step, dz_in)

        part = 2 * dec_len
        spots = [(u, i) for u in range(TILE // SLAB) for i in range(items)]
        key_rows = jnp.concatenate([jnp.broadcast_to(key_open[i], (part, span)) for u, i in spots], axis=0)

        @pl.loop(0, tiles)
        def _(t):
            for tile in (t, tiles + t):
                crossing_copy(crossing.at[:, at(tile * TILE, TILE, TILE)], tile, tile).wait_recv()

            def slab(n, u):
                return at(n * width + t * TILE + u * SLAB, SLAB, SLAB)
            scores = [
                nt(stacked(low[pl.ds(dec + i * dec_len, dec_len), slab(0, u)], scale), crossing[chunk(i), slab(0, u)])
                for u, i in spots
            ]
            p = soft(jnp.concatenate(scores, axis=0), key_rows > 0.0)
            for u in range(TILE // SLAB):
                prob[pairs + t * (TILE // SLAB) + u, pl.ds(0, items * part)] = p[u * items * part : (u + 1) * items * part]
            for n, (u, i) in enumerate(spots):
                both = nn(p[n * part : (n + 1) * part], crossing[chunk(i), slab(1, u)])
                heads[pl.ds(dec + i * dec_len, dec_len), slab(0, u)] = joined(both, dec_len).astype(bf16)

        value = hidden[ra] + nn(heads[rb], w_cross[:, pl.ds(width, width)])
        hidden[rb] = value
        rows_a[rc] = norm_forward(value, 2)
        mid = rows_a.at[rc]
        gather_step(1, 0, mid)

        @pl.loop(0, blocks_up)
        def _(j):
            e, s = gelu_both(nn(rows_a[rc], w_up[:, wide(j)]))
            active[ra, wide(j)] = e.astype(bf16)
            active[rb, wide(j)] = (nt(dz_in[...], w_down[wide(j)]) * s).astype(bf16)

        gather_step(1, 1, mid)

        value = dz_in[...].astype(f32) + norm_back(hidden[rb], nt(active[rb], w_up[...]), 2)
        result[ra] = value
        low[ra] = value.astype(bf16)
        rows_a[rd] = nt(low[ra], w_cross[:, pl.ds(width, width)]).astype(bf16)
        if not gathers:
            pl.semaphore_wait(barrier, 1)

        def kv_back(tile):
            return crossing_copy(slope.at[:, at(tile * TILE, TILE, TILE)], tile, tile)

        @pl.loop(0, tiles)
        def _(t):
            def slab(n, u):
                return at(n * width + t * TILE + u * SLAB, SLAB, SLAB)
            both = [stacked(rows_a[pl.ds(3 * dec + i * dec_len, dec_len), slab(0, u)]) for u, i in spots]
            dp = jnp.concatenate([nt(both[n], crossing[chunk(i), slab(1, u)]) for n, (u, i) in enumerate(spots)], axis=0)
            p = jnp.concatenate(
                [prob[pairs + t * (TILE // SLAB) + u, pl.ds(0, items * part)] for u in range(TILE // SLAB)], axis=0
            )
            ds = soft_back(p, dp)
            for n, (u, i) in enumerate(spots):
                lines = slice(n * part, (n + 1) * part)
                q = stacked(low[pl.ds(dec + i * dec_len, dec_len), slab(0, u)], scale)
                slope[chunk(i), slab(0, u)] = tn(ds[lines], q).astype(bf16)
                slope[chunk(i), slab(1, u)] = tn(p[lines], both[n]).astype(bf16)
            kv_back(t).start()
            kv_back(tiles + t).start()
            for n, (u, i) in enumerate(spots):
                lines = slice(n * part, (n + 1) * part)
                back = joined(nn(ds[lines], crossing[chunk(i), slab(0, u)]), dec_len) * scale
                low[pl.ds(3 * dec + i * dec_len, dec_len), slab(0, u)] = back.astype(bf16)

        gather_step(1, 2, mid)

        done = 0
        if not gathers:

            @pl.loop(0, blocks_up)
            def _(j):
                emit(j, at_down + 2 * j, tn(active[ra, wide(j)], dz_in[...]))

            @pl.loop(0, blocks_up)
            def _(j):
                emit(blocks_up + j, at_up + 2 * j, tn(rows_a[rc], active[rb, wide(j)]))
            done = 2 * blocks_up
        emit(done, at_cross + 1, tn(heads[rb], low[ra]))
        emit(done + 1, at_cross, tn(rows_a[rb], low[rd]))
        done += 2
        gather_step(1, 3, mid)
        value = result[ra] + norm_back(hidden[ra], nt(low[rd], w_cross[:, pl.ds(0, width)]), 1)
        result[ra] = value
        low[ra] = value.astype(bf16)
        emit(done, at_out, tn(heads[ra], low[ra]))
        done += 1
        rows_a[rd] = nt(low[ra], w_out[...]).astype(bf16)
        gather_step(1, 4, mid)

        @pl.loop(0, pairs)
        def _(h):
            cq, ck, cv = (slab_of(n, h) for n in range(3))
            q, k, v = qkv[ra, cq], qkv[ra, ck], qkv[ra, cv]
            both = stacked(rows_a[rd, cq])
            p = prob[h, pl.ds(0, 2 * dec), pl.ds(0, dec)]
            ds = soft_back(p, nt(both, v))
            qkv[rb, cq] = (joined(nn(ds, k), dec) * scale).astype(bf16)
            qkv[rb, ck] = tn(ds, stacked(q, scale)).astype(bf16)
            qkv[rb, cv] = tn(p, both).astype(bf16)

        gather_step(1, 5, mid)

        @pl.loop(0, 3)
        def _(j):
            emit(done + j, at_qkv + j, tn(rows_a[ra], qkv[rb, wide(j)]))
        done += 3
        grad = nt(qkv[rb], w_qkv[...])
        half_width = width // 2
        ends = (
            (result[ra] + norm_back(y_in[...].astype(f32), grad, 0)).astype(bf16),
            (hidden[rb] + nn(active[ra], w_down[...])).astype(bf16),
        )
        for n, (value, out) in enumerate(zip(ends, (dy_out, dec_out))):
            out[...] = value[:, half_width:]
            heads[pl.ds((2 + n) * dec, dec), pl.ds(0, half_width)] = value[:, :half_width]
            end_copy(n).start()
        block_store(0, 0).wait()
        block_store(1, 0).wait()
        for n in range(2):
            end_copy(n).wait_send()
        for tile in range(2 * tiles):
            kv_back(tile).wait_send()
        gather_step(1, 6, mid)


def fused(x, y, dz, weights, gain, shift, key_open, self_open, items, span, dec_len, gathers, collective_id):
    wq, wo, wi, wd, wc = weights
    width, hidden_units = wi.shape
    full = items * span
    dec = items * dec_len
    count = sum(w.size for w in weights) // (width * width)
    here = pl.BlockSpec(memory_space=pltpu.VMEM)
    there = pl.BlockSpec(memory_space=pl.ANY)
    pairs = width // SLAB
    return pl.pallas_call(
        functools.partial(fused_kernel, items, span, dec_len, gathers),
        out_shape=(
            jax.ShapeDtypeStruct((count, width, width), bf16),
            jax.ShapeDtypeStruct((8, width), f32),
            jax.ShapeDtypeStruct((full, width), bf16),
            jax.ShapeDtypeStruct((dec, width // 2), bf16),
            jax.ShapeDtypeStruct((dec, width // 2), bf16),
            jax.ShapeDtypeStruct((2, NZ, 2, 2, dec, width), bf16),
        ),
        in_specs=[there, here, here] + [there] * 5 + [here] * 4,
        out_specs=(there, here, there, here, here, there),
        scratch_shapes=[
            pltpu.VMEM(wq.shape, bf16),
            pltpu.VMEM(wo.shape, bf16),
            pltpu.VMEM(wi.shape, bf16),
            pltpu.VMEM(wd.shape, bf16),
            pltpu.VMEM(wc.shape, bf16),
            pltpu.VMEM((full, 3 * width), bf16),
            pltpu.VMEM((items * pairs, 2 * span, span), bf16),
            pltpu.VMEM((full, width), bf16),
            pltpu.VMEM((full, width), bf16),
            pltpu.VMEM((full, width), bf16),
            pltpu.VMEM((full, width), bf16),
            pltpu.VMEM((full, width), f32),
            pltpu.VMEM((full, width), f32),
            pltpu.VMEM((full, hidden_units), bf16),
            pltpu.VMEM((full, hidden_units), bf16),
            pltpu.VMEM((full, 2 * width), bf16),
            pltpu.VMEM((2, width, width), bf16),
            pltpu.SemaphoreType.DMA((5,)),
            pltpu.SemaphoreType.DMA((1,)),
            pltpu.SemaphoreType.DMA((2,)),
            pltpu.SemaphoreType.DMA((2 * width // TILE,)),
            pltpu.SemaphoreType.DMA((2 * width // TILE,)),
            pltpu.SemaphoreType.DMA((2, 2, 2, NZ)),
            pltpu.SemaphoreType.DMA((2, 2, 2, NZ)),
            pltpu.SemaphoreType.DMA((2, 2, 2)),
            pltpu.SemaphoreType.DMA((2, 2, 2)),
            pltpu.SemaphoreType.DMA((2,)),
            pltpu.SemaphoreType.DMA((2,)),
            pltpu.SemaphoreType.DMA((2,)),
        ],
        compiler_params=pltpu.CompilerParams(
            collective_id=collective_id, has_side_effects=True, vmem_limit_bytes=63 * 2**20
        ),
    )(x, y, dz, wq, wo, wi, wd, wc, gain, shift, key_open, self_open)


def ar_kernel(pairs, rows, width, across_block, g, norms, dx, out, norms_out, dx_half, acc, res, rx, up, dn, ry, nbuf, lsem, asend, arecv, zsend, zrecv, nsem, dsem):
    x, y, z, c = place()
    pairs = pairs[0] + (pairs[1] - pairs[0]) * c
    half, block, share = rows // 2, rows // 8, rows // 16

    def dev(x, y, z):
        return (c, bid(x, y, z))

    across = (dev(1 - x, y, z), dev(x, 1 - y, z))
    above, below = dev(x, y, z + 1), dev(x, y, z - 1)
    bit = (x, y)

    barrier = pltpu.get_barrier_semaphore()
    faraway = dev(x, y, (z + 2) % NZ)
    for d in across + (faraway,):
        pl.semaphore_signal(barrier, inc=1, device_id=d, device_id_type=MESH)

    @pl.when(z < NZ - 1)
    def _():
        pl.semaphore_signal(barrier, inc=1, device_id=above, device_id_type=MESH)

    @pl.when(z > 0)
    def _():
        pl.semaphore_signal(barrier, inc=1, device_id=below, device_id_type=MESH)

    mate = (1 - c, bid(x, y, z))

    @pl.when(c == 1)
    def _():
        pl.semaphore_signal(barrier, inc=1, device_id=mate, device_id_type=MESH)

    pl.semaphore_wait(barrier, 4 - c + (z + NZ - 1) // NZ + (2 * NZ - 2 - z) // NZ)

    def rdma(src, dst, send, recv, device):
        return pltpu.make_async_remote_copy(src_ref=src, dst_ref=dst, send_sem=send, recv_sem=recv, device_id=device, device_id_type=MESH)

    half_width = dx.shape[1] // 2
    dx_own = pltpu.make_async_copy(dx.at[:, pl.ds(0, half_width)], dx_half, dsem.at[0])
    dx_other = rdma(dx.at[:, pl.ds(half_width, half_width)], dx_half, dsem.at[1], dsem.at[2], mate)

    @pl.when(c == 0)
    def _():
        dx_own.start()
        dx_other.start()

    def parts(t, f):
        p = 2 * t + f
        a, b = bit[f], bit[1 - f]
        own = a * half
        other = (1 - a) * half
        return p, own, other, b

    def rows_at(start, n):
        return pl.ds(pl.multiple_of(start, 16), n)

    def panel_of(array, p, start, n):
        columns = pl.ds(pl.multiple_of(p % across_block * width, 128), width)
        return array.at[p // across_block, rows_at(start, n), columns]

    def own_load(t, f):
        p, own, other, b = parts(t, f)
        return pltpu.make_async_copy(panel_of(g, p, own, half), acc.at[p], lsem.at[p, 0])

    def own_store(t, f, k):
        p, own, other, b = parts(t, f)
        start = own if k == 0 else other
        return pltpu.make_async_copy(res.at[p, rows_at(start, half)], panel_of(out, p, start, half), lsem.at[p, k + 1])

    def rs_a(t, f):
        p, own, other, b = parts(t, f)
        return rdma(panel_of(g, p, other, half), rx.at[p], asend.at[p, 0], arecv.at[p, 0], across[f])

    def rs_up(t, f, k):
        p, own, other, b = parts(t, f)
        return rdma(acc.at[p, pl.ds(k * block, block)], up.at[p, k], zsend.at[p, 0, k], zrecv.at[p, 0, k], above)

    def rs_dn(t, f, k):
        p, own, other, b = parts(t, f)
        return rdma(acc.at[p, pl.ds(k * block, block)], dn.at[p, k], zsend.at[p, 1, k], zrecv.at[p, 1, k], below)

    def rs_b(t, f):
        p, own, other, b = parts(t, f)
        return rdma(acc.at[p, rows_at(z * block + (1 - b) * share, share)], ry.at[p], asend.at[p, 1], arecv.at[p, 1], across[1 - f])

    def ag_b(t, f):
        p, own, other, b = parts(t, f)
        s = res.at[p, rows_at(own + z * block + b * share, share)]
        return rdma(s, s, asend.at[p, 2], arecv.at[p, 2], across[1 - f])

    def ag_up(t, f, k):
        p, own, other, b = parts(t, f)
        s = res.at[p, rows_at(own + k * block, block)]
        return rdma(s, s, zsend.at[p, 2, k], zrecv.at[p, 2, k], above)

    def ag_dn(t, f, k):
        p, own, other, b = parts(t, f)
        s = res.at[p, rows_at(own + k * block, block)]
        return rdma(s, s, zsend.at[p, 3, k], zrecv.at[p, 3, k], below)

    def ag_a(t, f):
        p, own, other, b = parts(t, f)
        s = res.at[p, rows_at(own, half)]
        return rdma(s, s, asend.at[p, 3], arecv.at[p, 3], across[f])

    def s0(t, f):
        rs_a(t, f).start()
        own_load(t, f).start()

    def s1(t, f):
        p, own, other, b = parts(t, f)
        own_load(t, f).wait()
        rs_a(t, f).wait()
        acc[p] = acc[p] + rx[p]

        @pl.when(z == 0)
        def _():
            for k in range(NZ - 1, 0, -1):
                rs_up(t, f, k).start()

        @pl.when(z == NZ - 1)
        def _():
            for k in range(NZ - 1):
                rs_dn(t, f, k).start()

    def chain(t, f, j):
        p, own, other, b = parts(t, f)

        @pl.when(z == j)
        def _():
            for k in range(NZ - 1, j - 1, -1):
                rs_up(t, f, k).wait_recv()
                r = pl.ds(k * block, block)
                acc[p, r] = acc[p, r] + up[p, k]
                if k > j:
                    rs_up(t, f, k).start()

        @pl.when(z == NZ - 1 - j)
        def _():
            for k in range(NZ - j):
                rs_dn(t, f, k).wait_recv()
                r = pl.ds(k * block, block)
                acc[p, r] = acc[p, r] + dn[p, k]
                if k < NZ - 1 - j:
                    rs_dn(t, f, k).start()

    def s4(t, f):
        chain(t, f, NZ - 1)
        rs_b(t, f).start()

    def s5(t, f):
        p, own, other, b = parts(t, f)
        rs_b(t, f).wait()
        mine = z * block + b * share
        res[p, rows_at(own + mine, share)] = acc[p, rows_at(mine, share)] + ry[p]
        ag_b(t, f).start()

    def s6(t, f):
        ag_b(t, f).wait()

        @pl.when(z < NZ - 1)
        def _():
            ag_up(t, f, z).start()

        @pl.when(z > 0)
        def _():
            ag_dn(t, f, z).start()

    def spread(t, f, j):
        @pl.when(z >= j)
        def _():
            ag_up(t, f, z - j).wait_recv()

            @pl.when(z < NZ - 1)
            def _():
                ag_up(t, f, z - j).start()

        @pl.when(z + j <= NZ - 1)
        def _():
            ag_dn(t, f, z + j).wait_recv()

            @pl.when(z > 0)
            def _():
                ag_dn(t, f, z + j).start()

    def s9(t, f):
        spread(t, f, NZ - 1)
        ag_a(t, f).start()
        own_store(t, f, 0).start()

    def s10(t, f):
        ag_a(t, f).wait()
        own_store(t, f, 1).start()
        for k in range(NZ):
            @pl.when((z < k))
            def _(k=k):
                rs_up(t, f, k).wait_send()

            @pl.when((z > k))
            def _(k=k):
                rs_dn(t, f, k).wait_send()

            @pl.when((k <= z) & (z < NZ - 1))
            def _(k=k):
                ag_up(t, f, k).wait_send()

            @pl.when((k >= z) & (z > 0))
            def _(k=k):
                ag_dn(t, f, k).wait_send()

    def s11(t, f):
        own_store(t, f, 0).wait()
        own_store(t, f, 1).wait()

    mates = across + (dev(x, y, z + 1 - 2 * (z % 2)), faraway)

    def norm_swap(j):
        return rdma(norms_out, nbuf.at[j], nsem.at[0, j], nsem.at[1, j], mates[j])

    norms_out[...] = norms[...]
    norm_swap(0).start()

    stages = [s0, s1] + [functools.partial(lambda j, t, f: chain(t, f, j), j) for j in range(1, NZ - 1)] + [s4, s5, s6] + [
        functools.partial(lambda j, t, f: spread(t, f, j), j) for j in range(1, NZ - 1)] + [s9, s10, s11]
    ahead = 2

    def tick(tau, carry):
        for j in range(4):

            @pl.when(tau == 3 * j + 3)
            def _(j=j):
                norm_swap(j).wait()
                norms_out[...] = norms_out[...] + nbuf[j]
                if j < 3:
                    norm_swap(j + 1).start()

        for i, stage in enumerate(stages):
            lag = 0 if i == 0 else i - 1 + ahead
            t = tau - lag

            @pl.when((t >= 0) & (t < pairs))
            def _(stage=stage, t=t):
                stage(t, 0)
                stage(t, 1)
        return carry
    lax.fori_loop(0, pairs + len(stages) - 2 + ahead, tick, 0)

    @pl.when(c == 0)
    def _():
        dx_own.wait()
        dx_other.wait_send()

    @pl.when(c == 1)
    def _():
        dx_other.wait_recv()


def all_reduce(g, norms, dx, counts, collective_id):
    blocks, rows, block_width = g.shape
    width = 256
    across_block = block_width // width
    n = blocks * across_block
    half, block, share = rows // 2, rows // 8, rows // 16
    bf = jnp.bfloat16
    return pl.pallas_call(
        functools.partial(ar_kernel, [count * across_block // 2 for count in counts], rows, width, across_block),
        out_shape=(
            jax.ShapeDtypeStruct(g.shape, bf),
            jax.ShapeDtypeStruct(norms.shape, norms.dtype),
            jax.ShapeDtypeStruct((dx.shape[0], dx.shape[1] // 2), bf),
        ),
        in_specs=[pl.BlockSpec(memory_space=pl.ANY), pl.BlockSpec(memory_space=pltpu.VMEM), pl.BlockSpec(memory_space=pl.ANY)],
        out_specs=(pl.BlockSpec(memory_space=pl.ANY), pl.BlockSpec(memory_space=pltpu.VMEM), pl.BlockSpec(memory_space=pl.ANY)),
        scratch_shapes=[
            pltpu.VMEM((n, half, width), bf),
            pltpu.VMEM((n, rows, width), bf),
            pltpu.VMEM((n, half, width), bf),
            pltpu.VMEM((n, NZ, block, width), bf),
            pltpu.VMEM((n, NZ, block, width), bf),
            pltpu.VMEM((n, share, width), bf),
            pltpu.VMEM((4,) + norms.shape, norms.dtype),
            pltpu.SemaphoreType.DMA((n, 3)),
            pltpu.SemaphoreType.DMA((n, 4)),
            pltpu.SemaphoreType.DMA((n, 4)),
            pltpu.SemaphoreType.DMA((n, 4, NZ)),
            pltpu.SemaphoreType.DMA((n, 4, NZ)),
            pltpu.SemaphoreType.DMA((2, 4)),
            pltpu.SemaphoreType.DMA((3,)),
        ],
        compiler_params=pltpu.CompilerParams(collective_id=collective_id, has_side_effects=True, vmem_limit_bytes=60 * 2**20),
    )(g, norms, dx)


def finish_kernel(counts, gathers, panels, pool, up_in, down_in, *rest):
    outs, (rows, grads, w_up, w_down, active, bent, sems) = rest[:5], rest[5:]
    step = pl.program_id(0)
    section = lax.axis_index("section")
    plain = counts[0] + counts[1] + counts[2]
    first = 0
    for count, out in zip(counts[:3], outs):

        @pl.when((step >= first) & (step < first + count))
        def _(out=out):
            out[0] = panels[0].astype(f32)

        first += count
    up, down = outs[3:]
    turn = (step - plain) % 2
    if gathers:
        width = rows.shape[1]
        loads = [
            pltpu.make_async_copy(src, dst, sems.at[n])
            for n, (src, dst) in enumerate(
                ((pool.at[1], rows), (pool.at[0], grads), (up_in, w_up), (down_in, w_down))
            )
        ]

        @pl.when((step == 0) & (section == 1))
        def _():
            for load in loads:
                load.start()

        @pl.when((step == plain) & (section == 1))
        def _():
            for load in loads:
                load.wait()

        @pl.when((step >= plain) & (turn == 0) & (section == 1))
        def _():
            cols = at((step - plain) // 2 * width, width, width)
            size = 512

            @pl.loop(0, rows.shape[0] // size)
            def _(i):
                r = at(i * size, size, size)
                e, s = gelu_both(nn(rows[r], w_up[:, cols]))
                active[r] = e.astype(bf16)
                bent[r] = (nt(grads[r], w_down[cols]) * s).astype(bf16)
            up[0] = tn(rows[...], bent[...])

        @pl.when((step >= plain) & (turn == 1) & (section == 1))
        def _():
            down[0] = tn(active[...], grads[...])

    summed = (section == 0) if gathers else (section >= 0)

    @pl.when((step >= plain) & (turn == 0) & summed)
    def _():
        up[0] = panels[0].astype(f32)

    @pl.when((step >= plain) & (turn == 1) & summed)
    def _():
        down[0] = panels[0].astype(f32)


def finish(panels, pool, w_up, w_down, shapes, gathers):
    total, high, wide = panels.shape
    counts = [rows * columns // (high * wide) for rows, columns in shapes]
    plain = sum(counts[:3])
    out_specs = []
    first = 0
    for (rows, columns), count in zip(shapes[:3], counts):

        def place_of(step, first=first, count=count):
            return 0, 0, jnp.clip(step - first, 0, count - 1)

        out_specs.append(pl.BlockSpec((1, high, wide), place_of))
        first += count
    out_specs.append(pl.BlockSpec((1, high, wide), lambda step: (0, 0, jnp.clip((step - plain) // 2, 0, counts[3] - 1))))
    out_specs.append(pl.BlockSpec((1, high, wide), lambda step: (0, jnp.clip((step - plain - 1) // 2, 0, counts[4] - 1), 0)))
    there = pl.BlockSpec(memory_space=pl.ANY)
    gathered = pool.shape[1] if gathers else 16
    return pl.pallas_call(
        functools.partial(finish_kernel, counts, gathers),
        grid=(total,),
        out_shape=[jax.ShapeDtypeStruct((1,) + shape, f32) for shape in shapes],
        in_specs=[pl.BlockSpec((1, high, wide), lambda step: (step, 0, 0)), there, there, there],
        out_specs=out_specs,
        scratch_shapes=[
            pltpu.VMEM((gathered, wide), bf16),
            pltpu.VMEM((gathered, wide), bf16),
            pltpu.VMEM(w_up.shape, bf16),
            pltpu.VMEM(w_down.shape, bf16),
            pltpu.VMEM((gathered, wide), bf16),
            pltpu.VMEM((gathered, wide), bf16),
            pltpu.SemaphoreType.DMA((4,)),
        ],
        compiler_params=pltpu.CompilerParams(vmem_limit_bytes=63 * 2**20),
    )(panels, pool, w_up, w_down)


def per_device(
    enc_input,
    dec_input,
    out_grad,
    attn_qkv,
    attn_out,
    mlp_in,
    mlp_out,
    cross_proj,
    norm_gain,
    norm_shift,
    image_count,
    prefix_len,
    suffix_len,
):
    section = lax.axis_index("section")
    items, enc_len, width = enc_input.shape
    dec_len = dec_input.shape[1]
    span = -(-enc_len // 16) * 16
    weights = (attn_qkv[0], attn_out[0], mlp_in[0], mlp_out[0], cross_proj[0])
    positions = jnp.arange(span, dtype=jnp.int32)[None, :]
    has_image = (jnp.arange(items, dtype=jnp.int32) < image_count[0])[:, None]
    key_open = jnp.where(positions < PATCHES, has_image, positions - PATCHES < prefix_len[:, None])
    key_open = (key_open & (positions < enc_len)).astype(f32)[:, None, :]
    places = jnp.arange(items * dec_len, dtype=jnp.int32)
    item, spot = places // dec_len, places % dec_len
    self_open = (
        (item[:, None] == item[None, :])
        & (spot[None, :] <= spot[:, None])
        & (spot[None, :] < jnp.repeat(suffix_len, dec_len)[None, :])
    ).astype(f32)
    x = jnp.pad(enc_input, ((0, 0), (0, span - enc_len), (0, 0))).reshape(items * span, width)
    gathers = lax.axis_size("batch") == 16
    panels, norms, dx, dec_out, dy, pool = fused(
        x,
        dec_input.reshape(-1, width),
        out_grad.reshape(-1, width),
        weights,
        norm_gain[0].astype(f32),
        norm_shift[0].astype(f32),
        key_open,
        self_open,
        items,
        span,
        dec_len,
        gathers,
        1,
    )
    if gathers:
        blocks = panels.shape[0]
        panels, norms, dx_half = all_reduce(panels, norms, dx, (blocks, blocks - 2 * mlp_in.shape[2] // width), 0)
    else:
        panels, norms = lax.psum(panels, "batch"), lax.psum(norms, "batch")
        half = width // 2
        theirs = lax.dynamic_slice_in_dim(dx, (1 - section) * half, half, 1)
        theirs = lax.ppermute(theirs, "section", [(0, 1), (1, 0)])
        dx_half = jnp.where(section == 0, dx[:, :half], theirs)
    order = (0, 1, 4, 2, 3)
    pool = pool.reshape(2, -1, width) if gathers else pool[:, 0, 0, 0]
    blocks = finish(panels, pool, weights[2], weights[3], [weights[n].shape for n in order], gathers)
    grads = [blocks[order.index(n)] for n in range(len(order))]
    half = width // 2
    return (
        dec_out.reshape(items, dec_len, half),
        dx_half.reshape(items, span, half)[:, :enc_len],
        dy.reshape(items, dec_len, half),
        *grads,
        norms[None, :3],
        norms[None, 3:6],
    )


def solution(mesh):
    items = P("batch", None, None)
    matrix = P("section", None, None)
    halves = P("batch", None, "section")
    return jax.shard_map(
        per_device,
        mesh=mesh,
        in_specs=(items,) * 3 + (matrix,) * 7 + (P("batch"),) * 3,
        out_specs=(halves,) * 3 + (matrix,) * 7,
        check_vma=False,
    )
```

```python
import functools

import jax
import jax.numpy as jnp
from jax import lax
from jax.experimental import pallas as pl
from jax.experimental.pallas import tpu as pltpu
from jax.sharding import PartitionSpec as P

PATCHES = 196
MESH = pl.DeviceIdType.MESH
bf16, f32 = jnp.bfloat16, jnp.float32
epsilon = 1e-06
far_below = -1000000000.0
HEAD = 64
SLAB = 128
TILE = 256
GELU_A = 0.7978845608028654
GELU_B = 0.044715


NZ = 4


def place():
    b = lax.axis_index("batch")
    return b % 2, (b // 2) % 2, b // 4, lax.axis_index("section")


def bid(x, y, z):
    return z * 4 + y * 2 + x


def nn(a, b):
    return jnp.dot(a, b, preferred_element_type=f32)


def nt(a, b):
    return lax.dot_general(a, b, (((1,), (1,)), ((), ())), preferred_element_type=f32)


def tn(a, b):
    return lax.dot_general(a, b, (((0,), (0,)), ((), ())), preferred_element_type=f32)


def normal(v):
    centered = v - jnp.mean(v, axis=-1, keepdims=True)
    spread = lax.rsqrt(jnp.mean(centered * centered, axis=-1, keepdims=True) + epsilon)
    return centered * spread, spread


def gelu_both(u):
    square = u * u
    bent = jnp.tanh(GELU_A * u * (1.0 + GELU_B * square))
    half = 0.5 * (1.0 + bent)
    slope = half + 0.5 * u * (1.0 - bent * bent) * (GELU_A * (1.0 + 3.0 * GELU_B * square))
    return u * half, slope


def at(start, size, unit):
    return pl.ds(pl.multiple_of(start, unit), size)


def fused_kernel(items, span, dec_len, gathers,
                 x_in, y_in, dz_in, wq_in, wo_in, wi_in, wd_in, wc_in, gain, shift, key_open, self_open,
                 panels, norms, dx_out, dec_out, dy_out, pool,
                 w_qkv, w_out, w_up, w_down, w_cross,
                 qkv, prob, heads, low, rows_a, turned, hidden, result, active, slope, crossing, stage,
                 wsem, xsem, psem, send_sem, recv_sem, zsend, zrecv, asend, arecv, lsem, hsend, hrecv):
    width = w_out.shape[0]
    hidden_units = w_up.shape[1]
    pairs = width // SLAB
    full = items * span
    blocks_up = hidden_units // width
    at_qkv, at_out, at_cross, at_up, at_down = 0, 3, 4, 6, 7
    section = lax.axis_index("section")
    chip = lax.axis_index("batch")
    other = (1 - section, chip)

    barrier = pltpu.get_barrier_semaphore()
    pl.semaphore_signal(barrier, inc=1, device_id=other, device_id_type=MESH)
    x, y, z, _ = place()
    beside = ((section, bid(1 - x, y, z)), (section, bid(x, 1 - y, z)))
    above, below = (section, bid(x, y, z + 1)), (section, bid(x, y, z - 1))
    if gathers:

        @pl.when(section == 1)
        def _():
            for device in beside:
                pl.semaphore_signal(barrier, inc=1, device_id=device, device_id_type=MESH)

            @pl.when(z < NZ - 1)
            def _():
                pl.semaphore_signal(barrier, inc=1, device_id=above, device_id_type=MESH)

            @pl.when(z > 0)
            def _():
                pl.semaphore_signal(barrier, inc=1, device_id=below, device_id_type=MESH)

    def pool_copy(kind, half, src, dst, send, recv, device):
        return pltpu.make_async_remote_copy(
            src_ref=src, dst_ref=dst, send_sem=send, recv_sem=recv, device_id=device, device_id_type=MESH
        )

    def half_rows(half):
        size = items * dec_len // 2
        return pl.ds(half * size, size)

    def along_z(kind, half, way, k, source=None):
        spot = pool.at[kind, k, y, x, half_rows(half)]
        return pool_copy(
            kind, half, spot if source is None else source, spot,
            zsend.at[kind, half, way, k], zrecv.at[kind, half, way, k], (above, below)[way],
        )

    def along_a(kind, half):
        spot = pool.at[kind, :, y, x, half_rows(half)]
        return pool_copy(kind, half, spot, spot, asend.at[kind, half, 0], arecv.at[kind, half, 0], beside[half])

    def along_b(kind, half):
        spot = pool.at[kind, :, y, :, half_rows(half)] if half == 0 else pool.at[kind, :, :, x, half_rows(half)]
        return pool_copy(kind, half, spot, spot, asend.at[kind, half, 1], arecv.at[kind, half, 1], beside[1 - half])

    def own_copy(kind, source):
        return pltpu.make_async_copy(source, pool.at[kind, z, y, x], lsem.at[kind])

    def gather_step(kind, step, source):
        if not gathers:
            return
        if step == 0:
            own_copy(kind, source).start()
        for half in range(2):
            if step == 0:
                mine = source.at[half_rows(half)]

                @pl.when(z < NZ - 1)
                def _():
                    along_z(kind, half, 0, z, mine).start()

                @pl.when(z > 0)
                def _():
                    along_z(kind, half, 1, z, mine).start()
            elif step < NZ:

                @pl.when(z >= step)
                def _():
                    along_z(kind, half, 0, z - step).wait_recv()

                    @pl.when(z < NZ - 1)
                    def _():
                        along_z(kind, half, 0, z - step).start()

                @pl.when(z + step <= NZ - 1)
                def _():
                    along_z(kind, half, 1, z + step).wait_recv()

                    @pl.when(z > 0)
                    def _():
                        along_z(kind, half, 1, z + step).start()
            elif step == NZ:
                if half == 0:
                    own_copy(kind, source).wait()
                along_a(kind, half).start()
            elif step == NZ + 1:
                along_a(kind, half).wait_recv()
                along_b(kind, half).start()
            else:
                along_b(kind, half).wait()
                along_a(kind, half).wait_send()
                for k in range(NZ):

                    @pl.when((k <= z) & (z < NZ - 1))
                    def _(k=k):
                        along_z(kind, half, 0, k).wait_send()

                    @pl.when((k >= z) & (z > 0))
                    def _(k=k):
                        along_z(kind, half, 1, k).wait_send()

    weights = ((wq_in, w_qkv), (wo_in, w_out), (wi_in, w_up), (wd_in, w_down), (wc_in, w_cross))
    loads = [pltpu.make_async_copy(src, dst, wsem.at[n]) for n, (src, dst) in enumerate(weights)]

    lane = lax.broadcasted_iota(jnp.int32, (1, SLAB), 1)
    is_first = lane < HEAD
    mask_a = jnp.where(is_first, 1.0, 0.0).astype(bf16)
    mask_b = jnp.where(is_first, 0.0, 1.0).astype(bf16)
    scale = HEAD ** (-0.5)

    def stacked(slab, factor=1.0):
        return jnp.concatenate([slab * (mask_a * factor).astype(bf16), slab * (mask_b * factor).astype(bf16)], axis=0)

    def joined(both, rows):
        return jnp.where(is_first, both[:rows], both[rows:])

    def soft(scores, is_open):
        scores = jnp.where(is_open, scores, far_below)
        grown = jnp.exp(scores - jnp.max(scores, axis=-1, keepdims=True))
        return (grown * (1.0 / jnp.sum(grown, axis=-1, keepdims=True))).astype(bf16)

    def soft_back(p_low, dp):
        p = p_low.astype(f32)
        t = p * dp
        return (t - p * jnp.sum(t, axis=-1, keepdims=True)).astype(bf16)

    def wide(n):
        return at(n * width, width, width)

    def slab_of(n, h):
        return at(n * width + h * SLAB, SLAB, SLAB)

    def chunk(i):
        return pl.ds(i * span, span)

    def block_store(n, index):
        return pltpu.make_async_copy(stage.at[n % 2], panels.at[index], psem.at[n % 2])

    def emit(n, index, value):
        @pl.when(n >= 2)
        def _():
            block_store(n, index).wait()
        stage[n % 2] = value.astype(bf16)
        block_store(n, index).start()

    def norm_forward(value, index):
        unit, _ = normal(value)
        return (unit * gain[index : index + 1] + shift[index : index + 1]).astype(bf16)

    def norm_back(value, grad, index):
        unit, spread = normal(value)
        norms[index : index + 1] += jnp.sum(grad * unit, axis=0, keepdims=True)
        norms[3 + index : 4 + index] += jnp.sum(grad, axis=0, keepdims=True)
        scaled = grad * gain[index : index + 1]
        return spread * (
            scaled
            - jnp.mean(scaled, axis=-1, keepdims=True)
            - unit * jnp.mean(scaled * unit, axis=-1, keepdims=True)
        )

    def crossing_copy(source, n, tile):
        return pltpu.make_async_remote_copy(
            src_ref=source,
            dst_ref=crossing.at[:, at(tile * TILE, TILE, TILE)],
            send_sem=send_sem.at[n],
            recv_sem=recv_sem.at[tile],
            device_id=other,
            device_id_type=MESH,
        )

    def end_copy(n):
        dec = items * dec_len
        return pltpu.make_async_remote_copy(
            src_ref=heads.at[pl.ds((2 + n) * dec, dec), pl.ds(0, width // 2)],
            dst_ref=(dy_out, dec_out)[n],
            send_sem=hsend.at[n],
            recv_sem=hrecv.at[n],
            device_id=other,
            device_id_type=MESH,
        )

    tiles = width // TILE
    norms[...] = jnp.zeros_like(norms)

    @pl.when(section == 0)
    def _():
        x_load = pltpu.make_async_copy(x_in, low, xsem.at[0])
        x_load.start()
        for load in loads:
            load.start()
        x_load.wait()
        for i in range(items):
            rows_a[chunk(i)] = norm_forward(low[chunk(i)].astype(f32), 0)
        loads[0].wait()

        @pl.loop(0, 3)
        def _(j):
            for i in range(items):
                qkv[chunk(i), wide(j)] = nn(rows_a[chunk(i)], w_qkv[:, wide(j)]).astype(bf16)

        @pl.loop(0, items * pairs // 2)
        def _(it):
            i, h = it // (pairs // 2), 2 * (it % (pairs // 2))
            r = at(i * span, span, 16)
            for u in range(2):
                q, k, v = (qkv[r, slab_of(n, h + u)] for n in range(3))
                p = soft(nt(stacked(q, scale), k), key_open[i] > 0.0)
                prob[2 * it + u] = p
                heads[r, slab_of(0, h + u)] = joined(nn(p, v), span).astype(bf16)

        loads[1].wait()
        for i in range(items):
            r = chunk(i)
            value = low[r].astype(f32) + nn(heads[r], w_out[...])
            hidden[r] = value
            rows_a[r] = norm_forward(value, 1)
        loads[2].wait()

        @pl.loop(0, blocks_up)
        def _(j):
            for i in range(items):
                e, s = gelu_both(nn(rows_a[chunk(i)], w_up[:, wide(j)]))
                active[chunk(i), wide(j)] = e.astype(bf16)
                slope[chunk(i), wide(j)] = s.astype(bf16)

        loads[3].wait()
        for i in range(items):
            r = chunk(i)
            value = hidden[r] + nn(active[r], w_down[...])
            result[r] = value
            rows_a[r] = norm_forward(value, 2)
        loads[4].wait()
        pl.semaphore_wait(barrier, 1)

        def kv_send(n):
            return crossing_copy(turned.at[pl.ds(0, full), at((n % 3) * TILE, TILE, TILE)], n, n // 2 + tiles * (n % 2))

        for n in range(2 * tiles):
            tile = n // 2 + tiles * (n % 2)
            if n >= 3:
                kv_send(n - 3).wait_send()
            for i in range(items):
                turned[chunk(i), pl.ds((n % 3) * TILE, TILE)] = nn(rows_a[chunk(i)], w_cross[:, pl.ds(tile * TILE, TILE)]).astype(bf16)
            kv_send(n).start()
        for n in range(2 * tiles - 3, 2 * tiles):
            kv_send(n).wait_send()

        for n in range(2 * tiles):
            tile = n // 2 + tiles * (n % 2)
            crossing_copy(crossing.at[:, pl.ds(tile * TILE, TILE)], tile, tile).wait_recv()

        for i in range(items):
            r = chunk(i)
            value = norm_back(result[r], nt(crossing[r], w_cross[...]), 2)
            result[r] = value
            low[r] = value.astype(bf16)

        @pl.loop(0, 2)
        def _(j):
            emit(j, at_cross + j, tn(rows_a[...], crossing[:, wide(j)]))
        done = 2

        @pl.loop(0, blocks_up)
        def _(j):
            for i in range(items):
                r = chunk(i)
                slope[r, wide(j)] = (nt(low[r], w_down[wide(j)]) * slope[r, wide(j)].astype(f32)).astype(bf16)

        @pl.loop(0, blocks_up)
        def _(j):
            emit(done + j, at_down + 2 * j, tn(active[:, wide(j)], low[...]))
        done += blocks_up
        for i in range(items):
            rows_a[chunk(i)] = norm_forward(hidden[chunk(i)], 1)

        @pl.loop(0, blocks_up)
        def _(j):
            emit(done + j, at_up + 2 * j, tn(rows_a[...], slope[:, wide(j)]))
        done += blocks_up
        for i in range(items):
            r = chunk(i)
            value = result[r] + norm_back(hidden[r], nt(slope[r], w_up[...]), 1)
            result[r] = value
            low[r] = value.astype(bf16)
            rows_a[r] = nt(low[r], w_out[...]).astype(bf16)
        emit(done, at_out, tn(heads[...], low[...]))
        done += 1
        x_again = pltpu.make_async_copy(x_in, low, xsem.at[0])
        x_again.start()

        @pl.loop(0, items * pairs // 2)
        def _(it):
            i, h = it // (pairs // 2), 2 * (it % (pairs // 2))
            r = at(i * span, span, 16)
            for u in range(2):
                cq, ck, cv = (slab_of(n, h + u) for n in range(3))
                q, k, v = qkv[r, cq], qkv[r, ck], qkv[r, cv]
                both = stacked(rows_a[r, cq])
                p = prob[2 * it + u]
                ds = soft_back(p, nt(both, v))
                active[r, cq] = (joined(nn(ds, k), span) * scale).astype(bf16)
                active[r, ck] = tn(ds, stacked(q, scale)).astype(bf16)
                active[r, cv] = tn(p, both).astype(bf16)

        x_again.wait()
        for i in range(items):
            rows_a[chunk(i)] = norm_forward(low[chunk(i)].astype(f32), 0)

        @pl.loop(0, 3)
        def _(j):
            emit(done + j, at_qkv + j, tn(rows_a[...], active[:, wide(j)]))
        done += 3
        for i in range(items):
            r = chunk(i)
            grad = nt(active[r, pl.ds(0, 3 * width)], w_qkv[...])
            heads[r] = (result[r] + norm_back(low[r].astype(f32), grad, 0)).astype(bf16)
        dx_store = pltpu.make_async_copy(heads, dx_out, xsem.at[0])
        dx_store.start()
        block_store(0, 0).wait()
        block_store(1, 0).wait()
        dx_store.wait()
        for n in range(2):
            end_copy(n).wait_recv()

    @pl.when(section == 1)
    def _():
        dec = items * dec_len
        ra, rb, rc, rd = (pl.ds(n * dec, dec) for n in range(4))
        for n in (0, 1, 4, 2, 3):
            loads[n].start()
        rows_a[ra] = norm_forward(y_in[...].astype(f32), 0)
        if gathers:
            pl.semaphore_wait(barrier, 3 + (z + NZ - 1) // NZ + (2 * NZ - 2 - z) // NZ)
        gather_step(0, 0, dz_in)
        loads[0].wait()

        @pl.loop(0, 3)
        def _(j):
            qkv[ra, wide(j)] = nn(rows_a[ra], w_qkv[:, wide(j)]).astype(bf16)

        own = self_open[...] > 0.0
        own = jnp.concatenate([own, own], axis=0)

        @pl.loop(0, pairs)
        def _(h):
            cq, ck, cv = (slab_of(n, h) for n in range(3))
            p = soft(nt(stacked(qkv[ra, cq], scale), qkv[ra, ck]), own)
            prob[h, pl.ds(0, 2 * dec), pl.ds(0, dec)] = p
            heads[ra, cq] = joined(nn(p, qkv[ra, cv]), dec).astype(bf16)

        gather_step(0, 1, dz_in)
        loads[1].wait()
        value = y_in[...].astype(f32) + nn(heads[ra], w_out[...])
        hidden[ra] = value
        rows_a[rb] = norm_forward(value, 1)
        loads[4].wait()
        low[rb] = nn(rows_a[rb], w_cross[:, pl.ds(0, width)]).astype(bf16)
        loads[2].wait()
        loads[3].wait()
        for step in range(2, NZ + 3):
            gather_step(0, step, dz_in)

        part = 2 * dec_len
        spots = [(u, i) for u in range(TILE // SLAB) for i in range(items)]
        key_rows = jnp.concatenate([jnp.broadcast_to(key_open[i], (part, span)) for u, i in spots], axis=0)

        @pl.loop(0, tiles)
        def _(t):
            for tile in (t, tiles + t):
                crossing_copy(crossing.at[:, at(tile * TILE, TILE, TILE)], tile, tile).wait_recv()

            def slab(n, u):
                return at(n * width + t * TILE + u * SLAB, SLAB, SLAB)
            scores = [
                nt(stacked(low[pl.ds(dec + i * dec_len, dec_len), slab(0, u)], scale), crossing[chunk(i), slab(0, u)])
                for u, i in spots
            ]
            p = soft(jnp.concatenate(scores, axis=0), key_rows > 0.0)
            for u in range(TILE // SLAB):
                prob[pairs + t * (TILE // SLAB) + u, pl.ds(0, items * part)] = p[u * items * part : (u + 1) * items * part]
            for n, (u, i) in enumerate(spots):
                both = nn(p[n * part : (n + 1) * part], crossing[chunk(i), slab(1, u)])
                heads[pl.ds(dec + i * dec_len, dec_len), slab(0, u)] = joined(both, dec_len).astype(bf16)

        value = hidden[ra] + nn(heads[rb], w_cross[:, pl.ds(width, width)])
        hidden[rb] = value
        rows_a[rc] = norm_forward(value, 2)
        mid = rows_a.at[rc]
        gather_step(1, 0, mid)

        @pl.loop(0, blocks_up)
        def _(j):
            e, s = gelu_both(nn(rows_a[rc], w_up[:, wide(j)]))
            active[ra, wide(j)] = e.astype(bf16)
            active[rb, wide(j)] = (nt(dz_in[...], w_down[wide(j)]) * s).astype(bf16)

        gather_step(1, 1, mid)

        value = dz_in[...].astype(f32) + norm_back(hidden[rb], nt(active[rb], w_up[...]), 2)
        result[ra] = value
        low[ra] = value.astype(bf16)
        rows_a[rd] = nt(low[ra], w_cross[:, pl.ds(width, width)]).astype(bf16)
        if not gathers:
            pl.semaphore_wait(barrier, 1)

        def kv_back(tile):
            return crossing_copy(slope.at[:, at(tile * TILE, TILE, TILE)], tile, tile)

        @pl.loop(0, tiles)
        def _(t):
            def slab(n, u):
                return at(n * width + t * TILE + u * SLAB, SLAB, SLAB)
            both = [stacked(rows_a[pl.ds(3 * dec + i * dec_len, dec_len), slab(0, u)]) for u, i in spots]
            dp = jnp.concatenate([nt(both[n], crossing[chunk(i), slab(1, u)]) for n, (u, i) in enumerate(spots)], axis=0)
            p = jnp.concatenate(
                [prob[pairs + t * (TILE // SLAB) + u, pl.ds(0, items * part)] for u in range(TILE // SLAB)], axis=0
            )
            ds = soft_back(p, dp)
            for n, (u, i) in enumerate(spots):
                lines = slice(n * part, (n + 1) * part)
                q = stacked(low[pl.ds(dec + i * dec_len, dec_len), slab(0, u)], scale)
                slope[chunk(i), slab(0, u)] = tn(ds[lines], q).astype(bf16)
                slope[chunk(i), slab(1, u)] = tn(p[lines], both[n]).astype(bf16)
            kv_back(t).start()
            kv_back(tiles + t).start()
            for n, (u, i) in enumerate(spots):
                lines = slice(n * part, (n + 1) * part)
                back = joined(nn(ds[lines], crossing[chunk(i), slab(0, u)]), dec_len) * scale
                low[pl.ds(3 * dec + i * dec_len, dec_len), slab(0, u)] = back.astype(bf16)

        gather_step(1, 2, mid)

        done = 0
        if not gathers:

            @pl.loop(0, blocks_up)
            def _(j):
                emit(j, at_down + 2 * j, tn(active[ra, wide(j)], dz_in[...]))

            @pl.loop(0, blocks_up)
            def _(j):
                emit(blocks_up + j, at_up + 2 * j, tn(rows_a[rc], active[rb, wide(j)]))
            done = 2 * blocks_up
        emit(done, at_cross + 1, tn(heads[rb], low[ra]))
        emit(done + 1, at_cross, tn(rows_a[rb], low[rd]))
        done += 2
        gather_step(1, 3, mid)
        value = result[ra] + norm_back(hidden[ra], nt(low[rd], w_cross[:, pl.ds(0, width)]), 1)
        result[ra] = value
        low[ra] = value.astype(bf16)
        emit(done, at_out, tn(heads[ra], low[ra]))
        done += 1
        rows_a[rd] = nt(low[ra], w_out[...]).astype(bf16)
        gather_step(1, 4, mid)

        @pl.loop(0, pairs)
        def _(h):
            cq, ck, cv = (slab_of(n, h) for n in range(3))
            q, k, v = qkv[ra, cq], qkv[ra, ck], qkv[ra, cv]
            both = stacked(rows_a[rd, cq])
            p = prob[h, pl.ds(0, 2 * dec), pl.ds(0, dec)]
            ds = soft_back(p, nt(both, v))
            qkv[rb, cq] = (joined(nn(ds, k), dec) * scale).astype(bf16)
            qkv[rb, ck] = tn(ds, stacked(q, scale)).astype(bf16)
            qkv[rb, cv] = tn(p, both).astype(bf16)

        gather_step(1, 5, mid)

        @pl.loop(0, 3)
        def _(j):
            emit(done + j, at_qkv + j, tn(rows_a[ra], qkv[rb, wide(j)]))
        done += 3
        grad = nt(qkv[rb], w_qkv[...])
        half_width = width // 2
        ends = (
            (result[ra] + norm_back(y_in[...].astype(f32), grad, 0)).astype(bf16),
            (hidden[rb] + nn(active[ra], w_down[...])).astype(bf16),
        )
        for n, (value, out) in enumerate(zip(ends, (dy_out, dec_out))):
            out[...] = value[:, half_width:]
            heads[pl.ds((2 + n) * dec, dec), pl.ds(0, half_width)] = value[:, :half_width]
            end_copy(n).start()
        block_store(0, 0).wait()
        block_store(1, 0).wait()
        for n in range(2):
            end_copy(n).wait_send()
        for tile in range(2 * tiles):
            kv_back(tile).wait_send()
        gather_step(1, 6, mid)


def fused(x, y, dz, weights, gain, shift, key_open, self_open, items, span, dec_len, gathers, collective_id):
    wq, wo, wi, wd, wc = weights
    width, hidden_units = wi.shape
    full = items * span
    dec = items * dec_len
    count = sum(w.size for w in weights) // (width * width)
    here = pl.BlockSpec(memory_space=pltpu.VMEM)
    there = pl.BlockSpec(memory_space=pl.ANY)
    pairs = width // SLAB
    return pl.pallas_call(
        functools.partial(fused_kernel, items, span, dec_len, gathers),
        out_shape=(
            jax.ShapeDtypeStruct((count, width, width), bf16),
            jax.ShapeDtypeStruct((8, width), f32),
            jax.ShapeDtypeStruct((full, width), bf16),
            jax.ShapeDtypeStruct((dec, width // 2), bf16),
            jax.ShapeDtypeStruct((dec, width // 2), bf16),
            jax.ShapeDtypeStruct((2, NZ, 2, 2, dec, width), bf16),
        ),
        in_specs=[there, here, here] + [there] * 5 + [here] * 4,
        out_specs=(there, here, there, here, here, there),
        scratch_shapes=[
            pltpu.VMEM(wq.shape, bf16),
            pltpu.VMEM(wo.shape, bf16),
            pltpu.VMEM(wi.shape, bf16),
            pltpu.VMEM(wd.shape, bf16),
            pltpu.VMEM(wc.shape, bf16),
            pltpu.VMEM((full, 3 * width), bf16),
            pltpu.VMEM((items * pairs, 2 * span, span), bf16),
            pltpu.VMEM((full, width), bf16),
            pltpu.VMEM((full, width), bf16),
            pltpu.VMEM((full, width), bf16),
            pltpu.VMEM((full, width), bf16),
            pltpu.VMEM((full, width), f32),
            pltpu.VMEM((full, width), f32),
            pltpu.VMEM((full, hidden_units), bf16),
            pltpu.VMEM((full, hidden_units), bf16),
            pltpu.VMEM((full, 2 * width), bf16),
            pltpu.VMEM((2, width, width), bf16),
            pltpu.SemaphoreType.DMA((5,)),
            pltpu.SemaphoreType.DMA((1,)),
            pltpu.SemaphoreType.DMA((2,)),
            pltpu.SemaphoreType.DMA((2 * width // TILE,)),
            pltpu.SemaphoreType.DMA((2 * width // TILE,)),
            pltpu.SemaphoreType.DMA((2, 2, 2, NZ)),
            pltpu.SemaphoreType.DMA((2, 2, 2, NZ)),
            pltpu.SemaphoreType.DMA((2, 2, 2)),
            pltpu.SemaphoreType.DMA((2, 2, 2)),
            pltpu.SemaphoreType.DMA((2,)),
            pltpu.SemaphoreType.DMA((2,)),
            pltpu.SemaphoreType.DMA((2,)),
        ],
        compiler_params=pltpu.CompilerParams(
            collective_id=collective_id, has_side_effects=True, vmem_limit_bytes=63 * 2**20
        ),
    )(x, y, dz, wq, wo, wi, wd, wc, gain, shift, key_open, self_open)


AHEAD = 2
LATE = 2


def ar_kernel(pairs, rows, width, across_block, g, norms, dx, out, norms_out, dx_half, acc, res, rx, up, dn, ry, nbuf, lsem, asend, arecv, zsend, zrecv, nsem, dsem):
    x, y, z, c = place()
    pairs = pairs[0] + (pairs[1] - pairs[0]) * c
    half, block = rows // 2, rows // 8

    def dev(x, y, z):
        return (c, bid(x, y, z))

    across = (dev(1 - x, y, z), dev(x, 1 - y, z))
    above, below = dev(x, y, z + 1), dev(x, y, z - 1)
    bit = (x, y)

    barrier = pltpu.get_barrier_semaphore()
    faraway = dev(x, y, (z + 2) % NZ)
    for d in across + (faraway,):
        pl.semaphore_signal(barrier, inc=1, device_id=d, device_id_type=MESH)

    @pl.when(z < NZ - 1)
    def _():
        pl.semaphore_signal(barrier, inc=1, device_id=above, device_id_type=MESH)

    @pl.when(z > 0)
    def _():
        pl.semaphore_signal(barrier, inc=1, device_id=below, device_id_type=MESH)

    mate = (1 - c, bid(x, y, z))

    @pl.when(c == 1)
    def _():
        pl.semaphore_signal(barrier, inc=1, device_id=mate, device_id_type=MESH)

    pl.semaphore_wait(barrier, 4 - c + (z + NZ - 1) // NZ + (2 * NZ - 2 - z) // NZ)

    def rdma(src, dst, send, recv, device):
        return pltpu.make_async_remote_copy(src_ref=src, dst_ref=dst, send_sem=send, recv_sem=recv, device_id=device, device_id_type=MESH)

    half_width = dx.shape[1] // 2
    dx_own = pltpu.make_async_copy(dx.at[:, pl.ds(0, half_width)], dx_half, dsem.at[0])
    dx_other = rdma(dx.at[:, pl.ds(half_width, half_width)], dx_half, dsem.at[1], dsem.at[2], mate)

    @pl.when(c == 0)
    def _():
        dx_own.start()
        dx_other.start()

    def parts(t, f):
        p = 2 * t + f
        a, b = bit[f], bit[1 - f]
        own = a * half
        other = (1 - a) * half
        return p, own, other, b

    def rows_at(start, n):
        return pl.ds(pl.multiple_of(start, 16), n)

    def panel_of(array, p, start, n):
        columns = pl.ds(pl.multiple_of(p % across_block * width, 128), width)
        return array.at[p // across_block, rows_at(start, n), columns]

    def own_load(t, f):
        p, own, other, b = parts(t, f)
        return pltpu.make_async_copy(panel_of(g, p, own, half), acc.at[p], lsem.at[p, 0])

    def own_store(t, f, k):
        p, own, other, b = parts(t, f)
        start = own if k == 0 else other
        return pltpu.make_async_copy(res.at[p, rows_at(start, half)], panel_of(out, p, start, half), lsem.at[p, k])

    def rs_a(t, f):
        p, own, other, b = parts(t, f)
        return rdma(panel_of(g, p, other, half), rx.at[p], asend.at[p], arecv.at[p, 0], across[f])

    def rs_up(t, f, j):
        p = 2 * t + f
        r = pl.ds((j + 1) * block, (NZ - 1 - j) * block)
        return rdma(acc.at[p, r], up.at[p, r], zsend.at[p, 0], zrecv.at[p, 0, 0], above)

    def rs_dn(t, f, j):
        p = 2 * t + f
        r = pl.ds(0, j * block)
        return rdma(acc.at[p, r], dn.at[p, r], zsend.at[p, 1], zrecv.at[p, 1, 0], below)

    def both_b(t, f):
        p, own, other, b = parts(t, f)
        return rdma(acc.at[p, rows_at(z * block, block)], ry.at[p], asend.at[p], arecv.at[p, 1], across[1 - f])

    def ag_up(t, f, m):
        p, own, other, b = parts(t, f)
        s = res.at[p, rows_at(own + (z - m) * block, block)]
        return rdma(s, s, zsend.at[p, 0], zrecv.at[p, 0, 1 + m], above)

    def ag_dn(t, f, m):
        p, own, other, b = parts(t, f)
        s = res.at[p, rows_at(own + (z + m) * block, block)]
        return rdma(s, s, zsend.at[p, 1], zrecv.at[p, 1, 1 + m], below)

    def ag_a(t, f):
        p, own, other, b = parts(t, f)
        s = res.at[p, rows_at(own, half)]
        return rdma(s, s, asend.at[p], arecv.at[p, 2], across[f])

    def s0(t, f):
        rs_a(t, f).start()
        own_load(t, f).start()

    def s1(t, f):
        p, own, other, b = parts(t, f)
        own_load(t, f).wait()
        rs_a(t, f).wait()
        acc[p] = acc[p] + rx[p]

        @pl.when(z == 0)
        def _():
            rs_up(t, f, 0).start()

        @pl.when(z == NZ - 1)
        def _():
            rs_dn(t, f, NZ - 1).start()

    def chain(t, f, j):
        p = 2 * t + f

        @pl.when(z == j)
        def _():
            rs_up(t, f, j - 1).wait_recv()
            r = pl.ds(j * block, (NZ - j) * block)
            acc[p, r] = acc[p, r] + up[p, r]
            if j < NZ - 1:
                rs_up(t, f, j).start()

        @pl.when(z == NZ - 1 - j)
        def _():
            rs_dn(t, f, NZ - j).wait_recv()
            r = pl.ds(0, (NZ - j) * block)
            acc[p, r] = acc[p, r] + dn[p, r]
            if j < NZ - 1:
                rs_dn(t, f, NZ - 1 - j).start()

    def s4(t, f):
        chain(t, f, NZ - 1)
        both_b(t, f).start()

    def s5(t, f):
        p, own, other, b = parts(t, f)
        both_b(t, f).wait()
        res[p, rows_at(own + z * block, block)] = acc[p, rows_at(z * block, block)] + ry[p]

        for j in range(NZ):

            @pl.when(z == j)
            def _(j=j):
                if j < NZ - 1:
                    rs_up(t, f, j).wait_send()
                    ag_up(t, f, 0).start()
                if j > 0:
                    rs_dn(t, f, j).wait_send()
                    ag_dn(t, f, 0).start()

    def spread(t, f, j):
        @pl.when(z >= j)
        def _():
            ag_up(t, f, j - 1).wait_recv()

            @pl.when(z < NZ - 1)
            def _():
                ag_up(t, f, j - 1).wait_send()
                ag_up(t, f, j).start()

        @pl.when(z + j <= NZ - 1)
        def _():
            ag_dn(t, f, j - 1).wait_recv()

            @pl.when(z > 0)
            def _():
                ag_dn(t, f, j - 1).wait_send()
                ag_dn(t, f, j).start()

    def s9(t, f):
        spread(t, f, NZ - 1)
        ag_a(t, f).start()
        own_store(t, f, 0).start()

    def s10(t, f):
        ag_a(t, f).wait()
        own_store(t, f, 1).start()
        @pl.when(z < NZ - 1)
        def _():
            ag_up(t, f, 0).wait_send()

        @pl.when(z > 0)
        def _():
            ag_dn(t, f, 0).wait_send()

    def s11(t, f):
        own_store(t, f, 0).wait()
        own_store(t, f, 1).wait()

    mates = across + (dev(x, y, z + 1 - 2 * (z % 2)), faraway)

    def norm_swap(j):
        return rdma(norms_out, nbuf.at[j], nsem.at[0, j], nsem.at[1, j], mates[j])

    norms_out[...] = norms[...]
    norm_swap(0).start()

    stages = (
        [(0, s0), (AHEAD, s1)]
        + [(AHEAD + j, functools.partial(lambda j, t, f: chain(t, f, j), j)) for j in range(1, NZ - 1)]
        + [(AHEAD + NZ - 1, s4), (AHEAD + NZ, s5)]
        + [(AHEAD + NZ + j, functools.partial(lambda j, t, f: spread(t, f, j), j)) for j in range(1, NZ - 1)]
        + [(AHEAD + 2 * NZ - 1, s9), (AHEAD + 2 * NZ + LATE, s10), (AHEAD + 2 * NZ + 1 + LATE, s11)]
    )

    def tick(tau, carry):
        for j in range(4):

            @pl.when(tau == 3 * j + 3)
            def _(j=j):
                norm_swap(j).wait()
                norms_out[...] = norms_out[...] + nbuf[j]
                if j < 3:
                    norm_swap(j + 1).start()

        for lag, stage in stages:
            t = tau - lag

            @pl.when((t >= 0) & (t < pairs))
            def _(stage=stage, t=t):
                stage(t, 0)
                stage(t, 1)
        return carry
    lax.fori_loop(0, pairs + AHEAD + 2 * NZ + 2 + LATE, tick, 0)

    @pl.when(c == 0)
    def _():
        dx_own.wait()
        dx_other.wait_send()

    @pl.when(c == 1)
    def _():
        dx_other.wait_recv()


def all_reduce(g, norms, dx, counts, collective_id):
    blocks, rows, block_width = g.shape
    width = 256
    across_block = block_width // width
    n = blocks * across_block
    half, block = rows // 2, rows // 8
    bf = jnp.bfloat16
    return pl.pallas_call(
        functools.partial(ar_kernel, [count * across_block // 2 for count in counts], rows, width, across_block),
        out_shape=(
            jax.ShapeDtypeStruct(g.shape, bf),
            jax.ShapeDtypeStruct(norms.shape, norms.dtype),
            jax.ShapeDtypeStruct((dx.shape[0], dx.shape[1] // 2), bf),
        ),
        in_specs=[pl.BlockSpec(memory_space=pl.ANY), pl.BlockSpec(memory_space=pltpu.VMEM), pl.BlockSpec(memory_space=pl.ANY)],
        out_specs=(pl.BlockSpec(memory_space=pl.ANY), pl.BlockSpec(memory_space=pltpu.VMEM), pl.BlockSpec(memory_space=pl.ANY)),
        scratch_shapes=[
            pltpu.VMEM((n, half, width), bf),
            pltpu.VMEM((n, rows, width), bf),
            pltpu.VMEM((n, half, width), bf),
            pltpu.VMEM((n, half, width), bf),
            pltpu.VMEM((n, half, width), bf),
            pltpu.VMEM((n, block, width), bf),
            pltpu.VMEM((4,) + norms.shape, norms.dtype),
            pltpu.SemaphoreType.DMA((n, 2)),
            pltpu.SemaphoreType.DMA((n,)),
            pltpu.SemaphoreType.DMA((n, 3)),
            pltpu.SemaphoreType.DMA((n, 2)),
            pltpu.SemaphoreType.DMA((n, 2, NZ)),
            pltpu.SemaphoreType.DMA((2, 4)),
            pltpu.SemaphoreType.DMA((3,)),
        ],
        compiler_params=pltpu.CompilerParams(collective_id=collective_id, has_side_effects=True, vmem_limit_bytes=60 * 2**20),
    )(g, norms, dx)


SLOTS = 4


def finish_kernel(counts, gathers, panels, pool, up_in, down_in, *rest):
    outs = rest[:5]
    inbox, stage, rows, grads, w_up, w_down, active, bent, sems, in_sems, out_sems = rest[5:]
    width = panels.shape[1]
    plain = sum(counts[:3])
    total = sum(counts)
    section = lax.axis_index("section")
    targets = []
    for count, out in zip(counts[:3], outs):
        targets += [out.at[0, :, pl.ds(j * width, width)] for j in range(count)]
    for j in range(counts[3]):
        targets += [outs[3].at[0, :, pl.ds(j * width, width)], outs[4].at[0, pl.ds(j * width, width)]]

    def load(n):
        return pltpu.make_async_copy(panels.at[n], inbox.at[n], in_sems.at[n])

    def store(n):
        return pltpu.make_async_copy(stage.at[n % SLOTS], targets[n], out_sems.at[n % SLOTS])

    def put(n, value):
        if n >= SLOTS:
            store(n - SLOTS).wait()
        stage[n % SLOTS] = value
        store(n).start()

    def widen(n):
        load(n).wait()
        put(n, inbox[n].astype(f32))

    for n in range(plain):
        load(n).start()
    summed = (section == 0) if gathers else (section >= 0)
    whole = [
        pltpu.make_async_copy(src, dst, sems.at[n])
        for n, (src, dst) in enumerate(((pool.at[1], rows), (pool.at[0], grads), (up_in, w_up), (down_in, w_down)))
    ]

    @pl.when(summed)
    def _():
        for n in range(plain, total):
            load(n).start()

    if gathers:

        @pl.when(section == 1)
        def _():
            for copy in whole:
                copy.start()

    for n in range(plain):
        widen(n)

    @pl.when(summed)
    def _():
        for n in range(plain, total):
            widen(n)

    if gathers:

        @pl.when(section == 1)
        def _():
            for copy in whole:
                copy.wait()
            size = rows.shape[0] // 4
            for j in range(counts[3]):
                cols = pl.ds(j * width, width)

                @pl.loop(0, 4)
                def _(i):
                    r = at(i * size, size, size)
                    e, s = gelu_both(nn(rows[r], w_up[:, cols]))
                    active[r] = e.astype(bf16)
                    bent[r] = (nt(grads[r], w_down[cols]) * s).astype(bf16)
                put(plain + 2 * j, tn(rows[...], bent[...]))
                put(plain + 2 * j + 1, tn(active[...], grads[...]))

    for n in range(total - SLOTS, total):
        store(n).wait()


def finish(panels, pool, w_up, w_down, shapes, gathers):
    total, high, wide = panels.shape
    counts = [rows * columns // (high * wide) for rows, columns in shapes]
    there = pl.BlockSpec(memory_space=pl.ANY)
    gathered = pool.shape[1] if gathers else 16
    return pl.pallas_call(
        functools.partial(finish_kernel, counts, gathers),
        out_shape=[jax.ShapeDtypeStruct((1,) + shape, f32) for shape in shapes],
        in_specs=[there] * 4,
        out_specs=[there] * 5,
        scratch_shapes=[
            pltpu.VMEM(panels.shape, bf16),
            pltpu.VMEM((SLOTS, high, wide), f32),
            pltpu.VMEM((gathered, wide), bf16),
            pltpu.VMEM((gathered, wide), bf16),
            pltpu.VMEM(w_up.shape, bf16),
            pltpu.VMEM(w_down.shape, bf16),
            pltpu.VMEM((gathered, wide), bf16),
            pltpu.VMEM((gathered, wide), bf16),
            pltpu.SemaphoreType.DMA((4,)),
            pltpu.SemaphoreType.DMA((total,)),
            pltpu.SemaphoreType.DMA((SLOTS,)),
        ],
        compiler_params=pltpu.CompilerParams(vmem_limit_bytes=62 * 2**20),
    )(panels, pool, w_up, w_down)


def per_device(
    enc_input,
    dec_input,
    out_grad,
    attn_qkv,
    attn_out,
    mlp_in,
    mlp_out,
    cross_proj,
    norm_gain,
    norm_shift,
    image_count,
    prefix_len,
    suffix_len,
):
    section = lax.axis_index("section")
    items, enc_len, width = enc_input.shape
    dec_len = dec_input.shape[1]
    span = -(-enc_len // 16) * 16
    weights = (attn_qkv[0], attn_out[0], mlp_in[0], mlp_out[0], cross_proj[0])
    positions = jnp.arange(span, dtype=jnp.int32)[None, :]
    has_image = (jnp.arange(items, dtype=jnp.int32) < image_count[0])[:, None]
    key_open = jnp.where(positions < PATCHES, has_image, positions - PATCHES < prefix_len[:, None])
    key_open = (key_open & (positions < enc_len)).astype(f32)[:, None, :]
    places = jnp.arange(items * dec_len, dtype=jnp.int32)
    item, spot = places // dec_len, places % dec_len
    self_open = (
        (item[:, None] == item[None, :])
        & (spot[None, :] <= spot[:, None])
        & (spot[None, :] < jnp.repeat(suffix_len, dec_len)[None, :])
    ).astype(f32)
    x = jnp.pad(enc_input, ((0, 0), (0, span - enc_len), (0, 0))).reshape(items * span, width)
    gathers = lax.axis_size("batch") == 16
    panels, norms, dx, dec_out, dy, pool = fused(
        x,
        dec_input.reshape(-1, width),
        out_grad.reshape(-1, width),
        weights,
        norm_gain[0].astype(f32),
        norm_shift[0].astype(f32),
        key_open,
        self_open,
        items,
        span,
        dec_len,
        gathers,
        1,
    )
    if gathers:
        blocks = panels.shape[0]
        panels, norms, dx_half = all_reduce(panels, norms, dx, (blocks, blocks - 2 * mlp_in.shape[2] // width), 0)
    else:
        panels, norms = lax.psum(panels, "batch"), lax.psum(norms, "batch")
        half = width // 2
        theirs = lax.dynamic_slice_in_dim(dx, (1 - section) * half, half, 1)
        theirs = lax.ppermute(theirs, "section", [(0, 1), (1, 0)])
        dx_half = jnp.where(section == 0, dx[:, :half], theirs)
    order = (0, 1, 4, 2, 3)
    pool = pool.reshape(2, -1, width) if gathers else pool[:, 0, 0, 0]
    blocks = finish(panels, pool, weights[2], weights[3], [weights[n].shape for n in order], gathers)
    grads = [blocks[order.index(n)] for n in range(len(order))]
    half = width // 2
    return (
        dec_out.reshape(items, dec_len, half),
        dx_half.reshape(items, span, half)[:, :enc_len],
        dy.reshape(items, dec_len, half),
        *grads,
        norms[None, :3],
        norms[None, 3:6],
    )


def solution(mesh):
    items = P("batch", None, None)
    matrix = P("section", None, None)
    halves = P("batch", None, "section")
    return jax.shard_map(
        per_device,
        mesh=mesh,
        in_specs=(items,) * 3 + (matrix,) * 7 + (P("batch"),) * 3,
        out_specs=(halves,) * 3 + (matrix,) * 7,
        check_vma=False,
    )
```

```python
import functools

import jax
import jax.numpy as jnp
from jax import lax
from jax.experimental import pallas as pl
from jax.experimental.pallas import tpu as pltpu
from jax.sharding import PartitionSpec as P

PATCHES = 196
MESH = pl.DeviceIdType.MESH
bf16, f32 = jnp.bfloat16, jnp.float32
epsilon = 1e-06
far_below = -1000000000.0
HEAD = 64
SLAB = 128
TILE = 256
GELU_A = 0.7978845608028654
GELU_B = 0.044715


NZ = 4


def place():
    b = lax.axis_index("batch")
    return b % 2, (b // 2) % 2, b // 4, lax.axis_index("section")


def bid(x, y, z):
    return z * 4 + y * 2 + x


def nn(a, b):
    return jnp.dot(a, b, preferred_element_type=f32)


def nt(a, b):
    return lax.dot_general(a, b, (((1,), (1,)), ((), ())), preferred_element_type=f32)


def tn(a, b):
    return lax.dot_general(a, b, (((0,), (0,)), ((), ())), preferred_element_type=f32)


def normal(v):
    centered = v - jnp.mean(v, axis=-1, keepdims=True)
    spread = lax.rsqrt(jnp.mean(centered * centered, axis=-1, keepdims=True) + epsilon)
    return centered * spread, spread


def gelu_both(u):
    square = u * u
    part = 0.5 + 0.5 * jnp.tanh(u * (GELU_A + (GELU_A * GELU_B) * square))
    slope = part + (part - part * part) * (u * (2.0 * GELU_A + (6.0 * GELU_A * GELU_B) * square))
    return u * part, slope


def at(start, size, unit):
    return pl.ds(pl.multiple_of(start, unit), size)


def fused_kernel(items, span, dec_len, gathers,
                 x_in, y_in, dz_in, wq_in, wo_in, wi_in, wd_in, wc_in, gain, shift, key_open, self_open,
                 panels, norms, dx_out, dec_out, dy_out, pool,
                 w_qkv, w_out, w_up, w_down, w_cross,
                 qkv, prob, heads, low, rows_a, hidden, result, active, slope, crossing, stage,
                 wsem, xsem, psem, send_sem, recv_sem, zsend, zrecv, asend, arecv, lsem, hsend, hrecv):
    width = w_out.shape[0]
    hidden_units = w_up.shape[1]
    pairs = width // SLAB
    full = items * span
    blocks_up = hidden_units // width
    at_qkv, at_out, at_cross, at_up, at_down = 0, 3, 4, 6, 7
    section = lax.axis_index("section")
    chip = lax.axis_index("batch")
    other = (1 - section, chip)

    barrier = pltpu.get_barrier_semaphore()
    pl.semaphore_signal(barrier, inc=1, device_id=other, device_id_type=MESH)
    x, y, z, _ = place()
    beside = ((section, bid(1 - x, y, z)), (section, bid(x, 1 - y, z)))
    above, below = (section, bid(x, y, z + 1)), (section, bid(x, y, z - 1))
    if gathers:

        @pl.when(section == 1)
        def _():
            for device in beside:
                pl.semaphore_signal(barrier, inc=1, device_id=device, device_id_type=MESH)

            @pl.when(z < NZ - 1)
            def _():
                pl.semaphore_signal(barrier, inc=1, device_id=above, device_id_type=MESH)

            @pl.when(z > 0)
            def _():
                pl.semaphore_signal(barrier, inc=1, device_id=below, device_id_type=MESH)

    def pool_copy(kind, half, src, dst, send, recv, device):
        return pltpu.make_async_remote_copy(
            src_ref=src, dst_ref=dst, send_sem=send, recv_sem=recv, device_id=device, device_id_type=MESH
        )

    def half_rows(half):
        size = items * dec_len // 2
        return pl.ds(half * size, size)

    def along_z(kind, half, way, k, source=None):
        spot = pool.at[kind, k, y, x, half_rows(half)]
        return pool_copy(
            kind, half, spot if source is None else source, spot,
            zsend.at[kind, half, way, k], zrecv.at[kind, half, way, k], (above, below)[way],
        )

    def along_a(kind, half):
        spot = pool.at[kind, :, y, x, half_rows(half)]
        return pool_copy(kind, half, spot, spot, asend.at[kind, half, 0], arecv.at[kind, half, 0], beside[half])

    def along_b(kind, half):
        spot = pool.at[kind, :, y, :, half_rows(half)] if half == 0 else pool.at[kind, :, :, x, half_rows(half)]
        return pool_copy(kind, half, spot, spot, asend.at[kind, half, 1], arecv.at[kind, half, 1], beside[1 - half])

    def own_copy(kind, source):
        return pltpu.make_async_copy(source, pool.at[kind, z, y, x], lsem.at[kind])

    def gather_step(kind, step, source):
        if not gathers:
            return
        if step == 0:
            own_copy(kind, source).start()
        for half in range(2):
            if step == 0:
                mine = source.at[half_rows(half)]

                @pl.when(z < NZ - 1)
                def _():
                    along_z(kind, half, 0, z, mine).start()

                @pl.when(z > 0)
                def _():
                    along_z(kind, half, 1, z, mine).start()
            elif step < NZ:

                @pl.when(z >= step)
                def _():
                    along_z(kind, half, 0, z - step).wait_recv()

                    @pl.when(z < NZ - 1)
                    def _():
                        along_z(kind, half, 0, z - step).start()

                @pl.when(z + step <= NZ - 1)
                def _():
                    along_z(kind, half, 1, z + step).wait_recv()

                    @pl.when(z > 0)
                    def _():
                        along_z(kind, half, 1, z + step).start()
            elif step == NZ:
                if half == 0:
                    own_copy(kind, source).wait()
                along_a(kind, half).start()
            elif step == NZ + 1:
                along_a(kind, half).wait_recv()
                along_b(kind, half).start()
            else:
                along_b(kind, half).wait()
                along_a(kind, half).wait_send()
                for k in range(NZ):

                    @pl.when((k <= z) & (z < NZ - 1))
                    def _(k=k):
                        along_z(kind, half, 0, k).wait_send()

                    @pl.when((k >= z) & (z > 0))
                    def _(k=k):
                        along_z(kind, half, 1, k).wait_send()

    weights = ((wq_in, w_qkv), (wo_in, w_out), (wi_in, w_up), (wd_in, w_down), (wc_in, w_cross))
    loads = [pltpu.make_async_copy(src, dst, wsem.at[n]) for n, (src, dst) in enumerate(weights)]

    lane = lax.broadcasted_iota(jnp.int32, (1, SLAB), 1)
    is_first = lane < HEAD
    mask_a = jnp.where(is_first, 1.0, 0.0).astype(bf16)
    mask_b = jnp.where(is_first, 0.0, 1.0).astype(bf16)
    scale = HEAD ** (-0.5)

    def stacked(slab, factor=1.0):
        return jnp.concatenate([slab * (mask_a * factor).astype(bf16), slab * (mask_b * factor).astype(bf16)], axis=0)

    def joined(both, rows):
        return jnp.where(is_first, both[:rows], both[rows:])

    def soft(scores, is_open):
        scores = jnp.where(is_open, scores, far_below)
        grown = jnp.exp(scores - jnp.max(scores, axis=-1, keepdims=True))
        return (grown * (1.0 / jnp.sum(grown, axis=-1, keepdims=True))).astype(bf16)

    def soft_back(p_low, dp):
        p = p_low.astype(f32)
        t = p * dp
        return (t - p * jnp.sum(t, axis=-1, keepdims=True)).astype(bf16)

    def wide(n):
        return at(n * width, width, width)

    def slab_of(n, h):
        return at(n * width + h * SLAB, SLAB, SLAB)

    def chunk(i):
        return pl.ds(i * span, span)

    def block_store(n, index):
        return pltpu.make_async_copy(stage.at[n % 2], panels.at[index], psem.at[n % 2])

    def emit(n, index, value):
        @pl.when(n >= 2)
        def _():
            block_store(n, index).wait()
        stage[n % 2] = value.astype(bf16)
        block_store(n, index).start()

    def norm_forward(value, index):
        unit, _ = normal(value)
        return (unit * gain[index : index + 1] + shift[index : index + 1]).astype(bf16)

    def norm_back(value, grad, index):
        unit, spread = normal(value)
        norms[index : index + 1] += jnp.sum(grad * unit, axis=0, keepdims=True)
        norms[3 + index : 4 + index] += jnp.sum(grad, axis=0, keepdims=True)
        scaled = grad * gain[index : index + 1]
        return spread * (
            scaled
            - jnp.mean(scaled, axis=-1, keepdims=True)
            - unit * jnp.mean(scaled * unit, axis=-1, keepdims=True)
        )

    def crossing_copy(source, n, tile):
        return pltpu.make_async_remote_copy(
            src_ref=source,
            dst_ref=crossing.at[:, at(tile * TILE, TILE, TILE)],
            send_sem=send_sem.at[n],
            recv_sem=recv_sem.at[tile],
            device_id=other,
            device_id_type=MESH,
        )

    def end_copy(n):
        dec = items * dec_len
        return pltpu.make_async_remote_copy(
            src_ref=heads.at[pl.ds((2 + n) * dec, dec), pl.ds(0, width // 2)],
            dst_ref=(dy_out, dec_out)[n],
            send_sem=hsend.at[n],
            recv_sem=hrecv.at[n],
            device_id=other,
            device_id_type=MESH,
        )

    tiles = width // TILE
    norms[...] = jnp.zeros_like(norms)

    @pl.when(section == 0)
    def _():
        x_load = pltpu.make_async_copy(x_in, low, xsem.at[0])
        x_load.start()
        for load in loads:
            load.start()
        x_load.wait()
        for i in range(items):
            rows_a[chunk(i)] = norm_forward(low[chunk(i)].astype(f32), 0)
        loads[0].wait()

        @pl.loop(0, 3)
        def _(j):
            for i in range(items):
                qkv[chunk(i), wide(j)] = nn(rows_a[chunk(i)], w_qkv[:, wide(j)]).astype(bf16)

        @pl.loop(0, items)
        def _(i):
            r = at(i * span, span, 16)
            slabs = range(pairs)
            scores = [nt(stacked(qkv[r, slab_of(0, h)], scale), qkv[r, slab_of(1, h)]) for h in slabs]
            p = [soft(score, key_open[i] > 0.0) for score in scores]
            out = [joined(nn(p[h], qkv[r, slab_of(2, h)]), span).astype(bf16) for h in slabs]
            for h in slabs:
                prob[i * pairs + h] = p[h]
                heads[r, slab_of(0, h)] = out[h]

        loads[1].wait()
        for i in range(items):
            r = chunk(i)
            value = low[r].astype(f32) + nn(heads[r], w_out[...])
            hidden[r] = value
            rows_a[r] = norm_forward(value, 1)
        loads[2].wait()

        @pl.loop(0, blocks_up)
        def _(j):
            for i in range(items):
                e, s = gelu_both(nn(rows_a[chunk(i)], w_up[:, wide(j)]))
                active[chunk(i), wide(j)] = e.astype(bf16)
                slope[chunk(i), wide(j)] = s.astype(bf16)

        loads[3].wait()
        for i in range(items):
            r = chunk(i)
            value = hidden[r] + nn(active[r], w_down[...])
            result[r] = value
            rows_a[r] = norm_forward(value, 2)
        loads[4].wait()
        pl.semaphore_wait(barrier, 1)

        def kv_send(n):
            return crossing_copy(low.at[:, at((n % 3) * TILE, TILE, TILE)], n, n // 2 + tiles * (n % 2))

        for n in range(2 * tiles):
            tile = n // 2 + tiles * (n % 2)
            if n >= 3:
                kv_send(n - 3).wait_send()
            for i in range(items):
                low[chunk(i), pl.ds((n % 3) * TILE, TILE)] = nn(rows_a[chunk(i)], w_cross[:, pl.ds(tile * TILE, TILE)]).astype(bf16)
            kv_send(n).start()
        for n in range(2 * tiles - 3, 2 * tiles):
            kv_send(n).wait_send()

        for n in range(2 * tiles):
            tile = n // 2 + tiles * (n % 2)
            crossing_copy(crossing.at[:, pl.ds(tile * TILE, TILE)], tile, tile).wait_recv()

        grads = [nt(crossing[chunk(i)], w_cross[...]) for i in range(items)]
        grads = [norm_back(result[chunk(i)], grads[i], 2) for i in range(items)]
        for i in range(items):
            result[chunk(i)] = grads[i]
            low[chunk(i)] = grads[i].astype(bf16)

        @pl.loop(0, 2)
        def _(j):
            emit(j, at_cross + j, tn(rows_a[...], crossing[:, wide(j)]))
        done = 2

        @pl.loop(0, blocks_up)
        def _(j):
            for i in range(items):
                r = chunk(i)
                slope[r, wide(j)] = (nt(low[r], w_down[wide(j)]) * slope[r, wide(j)].astype(f32)).astype(bf16)

        @pl.loop(0, blocks_up)
        def _(j):
            emit(done + j, at_down + 2 * j, tn(active[:, wide(j)], low[...]))
        done += blocks_up
        for i in range(items):
            rows_a[chunk(i)] = norm_forward(hidden[chunk(i)], 1)

        @pl.loop(0, blocks_up)
        def _(j):
            emit(done + j, at_up + 2 * j, tn(rows_a[...], slope[:, wide(j)]))
        done += blocks_up
        grads = [nt(slope[chunk(i)], w_up[...]) for i in range(items)]
        grads = [result[chunk(i)] + norm_back(hidden[chunk(i)], grads[i], 1) for i in range(items)]
        rounded = [grad.astype(bf16) for grad in grads]
        back = [nt(grad, w_out[...]).astype(bf16) for grad in rounded]
        for i in range(items):
            result[chunk(i)] = grads[i]
            low[chunk(i)] = rounded[i]
            rows_a[chunk(i)] = back[i]
        emit(done, at_out, tn(heads[...], low[...]))
        done += 1
        x_again = pltpu.make_async_copy(x_in, low, xsem.at[0])
        x_again.start()

        group = 3

        @pl.loop(0, items * pairs // group)
        def _(it):
            i = it // (pairs // group)
            r = at(i * span, span, 16)
            slabs = [group * (it % (pairs // group)) + u for u in range(group)]
            both = [stacked(rows_a[r, slab_of(0, h)]) for h in slabs]
            p = [prob[group * it + u] for u in range(group)]
            dp = [nt(both[u], qkv[r, slab_of(2, h)]) for u, h in enumerate(slabs)]
            dv = [tn(p[u], both[u]).astype(bf16) for u in range(group)]
            ds = [soft_back(p[u], dp[u]) for u in range(group)]
            dq = [(joined(nn(ds[u], qkv[r, slab_of(1, h)]), span) * scale).astype(bf16) for u, h in enumerate(slabs)]
            dk = [tn(ds[u], stacked(qkv[r, slab_of(0, h)], scale)).astype(bf16) for u, h in enumerate(slabs)]
            for u, h in enumerate(slabs):
                active[r, slab_of(0, h)] = dq[u]
                active[r, slab_of(1, h)] = dk[u]
                active[r, slab_of(2, h)] = dv[u]

        x_again.wait()
        for i in range(items):
            rows_a[chunk(i)] = norm_forward(low[chunk(i)].astype(f32), 0)

        @pl.loop(0, 3)
        def _(j):
            emit(done + j, at_qkv + j, tn(rows_a[...], active[:, wide(j)]))
        done += 3
        grads = [nt(active[chunk(i), pl.ds(0, 3 * width)], w_qkv[...]) for i in range(items)]
        grads = [result[chunk(i)] + norm_back(low[chunk(i)].astype(f32), grads[i], 0) for i in range(items)]
        for i in range(items):
            heads[chunk(i)] = grads[i].astype(bf16)
        dx_store = pltpu.make_async_copy(heads, dx_out, xsem.at[0])
        dx_store.start()
        block_store(0, 0).wait()
        block_store(1, 0).wait()
        dx_store.wait()
        for n in range(2):
            end_copy(n).wait_recv()

    @pl.when(section == 1)
    def _():
        dec = items * dec_len
        ra, rb, rc, rd = (pl.ds(n * dec, dec) for n in range(4))
        for n in (0, 1, 4, 2, 3):
            loads[n].start()
        rows_a[ra] = norm_forward(y_in[...].astype(f32), 0)
        if gathers:
            pl.semaphore_wait(barrier, 3 + (z + NZ - 1) // NZ + (2 * NZ - 2 - z) // NZ)
        gather_step(0, 0, dz_in)
        loads[0].wait()

        @pl.loop(0, 3)
        def _(j):
            qkv[ra, wide(j)] = nn(rows_a[ra], w_qkv[:, wide(j)]).astype(bf16)

        own = self_open[...] > 0.0
        own = jnp.concatenate([own, own], axis=0)

        slabs = range(pairs)
        scores = [nt(stacked(qkv[ra, slab_of(0, h)], scale), qkv[ra, slab_of(1, h)]) for h in slabs]
        p = [soft(score, own) for score in scores]
        out = [joined(nn(p[h], qkv[ra, slab_of(2, h)]), dec).astype(bf16) for h in slabs]
        for h in slabs:
            prob[h, pl.ds(0, 2 * dec), pl.ds(0, dec)] = p[h]
            heads[ra, slab_of(0, h)] = out[h]

        gather_step(0, 1, dz_in)
        loads[1].wait()
        value = y_in[...].astype(f32) + nn(heads[ra], w_out[...])
        hidden[ra] = value
        rows_a[rb] = norm_forward(value, 1)
        loads[4].wait()
        low[rb] = nn(rows_a[rb], w_cross[:, pl.ds(0, width)]).astype(bf16)
        loads[2].wait()
        loads[3].wait()
        for step in range(2, NZ + 3):
            gather_step(0, step, dz_in)

        part = 2 * dec_len
        spots = [(u, i) for u in range(TILE // SLAB) for i in range(items)]
        key_rows = jnp.concatenate([jnp.broadcast_to(key_open[i], (part, span)) for u, i in spots], axis=0)

        @pl.loop(0, tiles)
        def _(t):
            for tile in (t, tiles + t):
                crossing_copy(crossing.at[:, at(tile * TILE, TILE, TILE)], tile, tile).wait_recv()

            def slab(n, u):
                return at(n * width + t * TILE + u * SLAB, SLAB, SLAB)
            scores = [
                nt(stacked(low[pl.ds(dec + i * dec_len, dec_len), slab(0, u)], scale), crossing[chunk(i), slab(0, u)])
                for u, i in spots
            ]
            p = soft(jnp.concatenate(scores, axis=0), key_rows > 0.0)
            for u in range(TILE // SLAB):
                prob[pairs + t * (TILE // SLAB) + u, pl.ds(0, items * part)] = p[u * items * part : (u + 1) * items * part]
            out = [nn(p[n * part : (n + 1) * part], crossing[chunk(i), slab(1, u)]) for n, (u, i) in enumerate(spots)]
            for n, (u, i) in enumerate(spots):
                heads[pl.ds(dec + i * dec_len, dec_len), slab(0, u)] = joined(out[n], dec_len).astype(bf16)

        value = hidden[ra] + nn(heads[rb], w_cross[:, pl.ds(width, width)])
        hidden[rb] = value
        rows_a[rc] = norm_forward(value, 2)
        mid = rows_a.at[rc]
        gather_step(1, 0, mid)

        @pl.loop(0, blocks_up)
        def _(j):
            e, s = gelu_both(nn(rows_a[rc], w_up[:, wide(j)]))
            active[ra, wide(j)] = e.astype(bf16)
            active[rb, wide(j)] = (nt(dz_in[...], w_down[wide(j)]) * s).astype(bf16)

        gather_step(1, 1, mid)

        value = dz_in[...].astype(f32) + norm_back(hidden[rb], nt(active[rb], w_up[...]), 2)
        result[ra] = value
        low[ra] = value.astype(bf16)
        rows_a[rd] = nt(low[ra], w_cross[:, pl.ds(width, width)]).astype(bf16)
        if not gathers:
            pl.semaphore_wait(barrier, 1)

        def kv_back(tile):
            return crossing_copy(slope.at[:, at(tile * TILE, TILE, TILE)], tile, tile)

        @pl.loop(0, tiles)
        def _(t):
            def slab(n, u):
                return at(n * width + t * TILE + u * SLAB, SLAB, SLAB)
            both = [stacked(rows_a[pl.ds(3 * dec + i * dec_len, dec_len), slab(0, u)]) for u, i in spots]
            dp = jnp.concatenate([nt(both[n], crossing[chunk(i), slab(1, u)]) for n, (u, i) in enumerate(spots)], axis=0)
            p = jnp.concatenate(
                [prob[pairs + t * (TILE // SLAB) + u, pl.ds(0, items * part)] for u in range(TILE // SLAB)], axis=0
            )
            lines = [slice(n * part, (n + 1) * part) for n in range(len(spots))]
            dv = [tn(p[lines[n]], both[n]).astype(bf16) for n in range(len(spots))]
            q = [stacked(low[pl.ds(dec + i * dec_len, dec_len), slab(0, u)], scale) for u, i in spots]
            ds = soft_back(p, dp)
            dk = [tn(ds[lines[n]], q[n]).astype(bf16) for n in range(len(spots))]
            for n, (u, i) in enumerate(spots):
                slope[chunk(i), slab(0, u)] = dk[n]
                slope[chunk(i), slab(1, u)] = dv[n]
            kv_back(t).start()
            kv_back(tiles + t).start()
            back = [joined(nn(ds[lines[n]], crossing[chunk(i), slab(0, u)]), dec_len) * scale for n, (u, i) in enumerate(spots)]
            for n, (u, i) in enumerate(spots):
                low[pl.ds(3 * dec + i * dec_len, dec_len), slab(0, u)] = back[n].astype(bf16)

        gather_step(1, 2, mid)

        done = 0
        if not gathers:

            @pl.loop(0, blocks_up)
            def _(j):
                emit(j, at_down + 2 * j, tn(active[ra, wide(j)], dz_in[...]))

            @pl.loop(0, blocks_up)
            def _(j):
                emit(blocks_up + j, at_up + 2 * j, tn(rows_a[rc], active[rb, wide(j)]))
            done = 2 * blocks_up
        emit(done, at_cross + 1, tn(heads[rb], low[ra]))
        emit(done + 1, at_cross, tn(rows_a[rb], low[rd]))
        done += 2
        gather_step(1, 3, mid)
        value = result[ra] + norm_back(hidden[ra], nt(low[rd], w_cross[:, pl.ds(0, width)]), 1)
        result[ra] = value
        low[ra] = value.astype(bf16)
        emit(done, at_out, tn(heads[ra], low[ra]))
        done += 1
        rows_a[rd] = nt(low[ra], w_out[...]).astype(bf16)
        gather_step(1, 4, mid)

        both = [stacked(rows_a[rd, slab_of(0, h)]) for h in slabs]
        p = [prob[h, pl.ds(0, 2 * dec), pl.ds(0, dec)] for h in slabs]
        dp = [nt(both[h], qkv[ra, slab_of(2, h)]) for h in slabs]
        dv = [tn(p[h], both[h]).astype(bf16) for h in slabs]
        ds = [soft_back(p[h], dp[h]) for h in slabs]
        dq = [(joined(nn(ds[h], qkv[ra, slab_of(1, h)]), dec) * scale).astype(bf16) for h in slabs]
        dk = [tn(ds[h], stacked(qkv[ra, slab_of(0, h)], scale)).astype(bf16) for h in slabs]
        for h in slabs:
            qkv[rb, slab_of(0, h)] = dq[h]
            qkv[rb, slab_of(1, h)] = dk[h]
            qkv[rb, slab_of(2, h)] = dv[h]

        gather_step(1, 5, mid)

        @pl.loop(0, 3)
        def _(j):
            emit(done + j, at_qkv + j, tn(rows_a[ra], qkv[rb, wide(j)]))
        done += 3
        grad = nt(qkv[rb], w_qkv[...])
        half_width = width // 2
        ends = (
            (result[ra] + norm_back(y_in[...].astype(f32), grad, 0)).astype(bf16),
            (hidden[rb] + nn(active[ra], w_down[...])).astype(bf16),
        )
        for n, (value, out) in enumerate(zip(ends, (dy_out, dec_out))):
            out[...] = value[:, half_width:]
            heads[pl.ds((2 + n) * dec, dec), pl.ds(0, half_width)] = value[:, :half_width]
            end_copy(n).start()
        block_store(0, 0).wait()
        block_store(1, 0).wait()
        for n in range(2):
            end_copy(n).wait_send()
        for tile in range(2 * tiles):
            kv_back(tile).wait_send()
        gather_step(1, 6, mid)


def fused(x, y, dz, weights, gain, shift, key_open, self_open, items, span, dec_len, gathers, collective_id):
    wq, wo, wi, wd, wc = weights
    width, hidden_units = wi.shape
    full = items * span
    dec = items * dec_len
    count = sum(w.size for w in weights) // (width * width)
    here = pl.BlockSpec(memory_space=pltpu.VMEM)
    there = pl.BlockSpec(memory_space=pl.ANY)
    pairs = width // SLAB
    return pl.pallas_call(
        functools.partial(fused_kernel, items, span, dec_len, gathers),
        out_shape=(
            jax.ShapeDtypeStruct((count, width, width), bf16),
            jax.ShapeDtypeStruct((8, width), f32),
            jax.ShapeDtypeStruct((full, width), bf16),
            jax.ShapeDtypeStruct((dec, width // 2), bf16),
            jax.ShapeDtypeStruct((dec, width // 2), bf16),
            jax.ShapeDtypeStruct((2, NZ, 2, 2, dec, width), bf16),
        ),
        in_specs=[there, here, here] + [there] * 5 + [here] * 4,
        out_specs=(there, here, there, here, here, there),
        scratch_shapes=[
            pltpu.VMEM(wq.shape, bf16),
            pltpu.VMEM(wo.shape, bf16),
            pltpu.VMEM(wi.shape, bf16),
            pltpu.VMEM(wd.shape, bf16),
            pltpu.VMEM(wc.shape, bf16),
            pltpu.VMEM((full, 3 * width), bf16),
            pltpu.VMEM((items * pairs, 2 * span, span), bf16),
            pltpu.VMEM((full, width), bf16),
            pltpu.VMEM((full, width), bf16),
            pltpu.VMEM((full, width), bf16),
            pltpu.VMEM((full, width), f32),
            pltpu.VMEM((full, width), f32),
            pltpu.VMEM((full, hidden_units), bf16),
            pltpu.VMEM((full, hidden_units), bf16),
            pltpu.VMEM((full, 2 * width), bf16),
            pltpu.VMEM((2, width, width), bf16),
            pltpu.SemaphoreType.DMA((5,)),
            pltpu.SemaphoreType.DMA((1,)),
            pltpu.SemaphoreType.DMA((2,)),
            pltpu.SemaphoreType.DMA((2 * width // TILE,)),
            pltpu.SemaphoreType.DMA((2 * width // TILE,)),
            pltpu.SemaphoreType.DMA((2, 2, 2, NZ)),
            pltpu.SemaphoreType.DMA((2, 2, 2, NZ)),
            pltpu.SemaphoreType.DMA((2, 2, 2)),
            pltpu.SemaphoreType.DMA((2, 2, 2)),
            pltpu.SemaphoreType.DMA((2,)),
            pltpu.SemaphoreType.DMA((2,)),
            pltpu.SemaphoreType.DMA((2,)),
        ],
        compiler_params=pltpu.CompilerParams(
            collective_id=collective_id, has_side_effects=True, vmem_limit_bytes=63 * 2**20
        ),
    )(x, y, dz, wq, wo, wi, wd, wc, gain, shift, key_open, self_open)


AHEAD = 2
LATE = 2


def ar_kernel(pairs, rows, width, across_block, g, norms, dx, out, norms_out, dx_half, acc, res, rx, up, dn, ry, nbuf, lsem, asend, arecv, zsend, zrecv, nsem, dsem):
    x, y, z, c = place()
    pairs = pairs[0] + (pairs[1] - pairs[0]) * c
    half, block = rows // 2, rows // 8

    def dev(x, y, z):
        return (c, bid(x, y, z))

    across = (dev(1 - x, y, z), dev(x, 1 - y, z))
    above, below = dev(x, y, z + 1), dev(x, y, z - 1)
    bit = (x, y)

    barrier = pltpu.get_barrier_semaphore()
    faraway = dev(x, y, (z + 2) % NZ)
    for d in across + (faraway,):
        pl.semaphore_signal(barrier, inc=1, device_id=d, device_id_type=MESH)

    @pl.when(z < NZ - 1)
    def _():
        pl.semaphore_signal(barrier, inc=1, device_id=above, device_id_type=MESH)

    @pl.when(z > 0)
    def _():
        pl.semaphore_signal(barrier, inc=1, device_id=below, device_id_type=MESH)

    mate = (1 - c, bid(x, y, z))

    @pl.when(c == 1)
    def _():
        pl.semaphore_signal(barrier, inc=1, device_id=mate, device_id_type=MESH)

    pl.semaphore_wait(barrier, 4 - c + (z + NZ - 1) // NZ + (2 * NZ - 2 - z) // NZ)

    def rdma(src, dst, send, recv, device):
        return pltpu.make_async_remote_copy(src_ref=src, dst_ref=dst, send_sem=send, recv_sem=recv, device_id=device, device_id_type=MESH)

    half_width = dx.shape[1] // 2
    dx_own = pltpu.make_async_copy(dx.at[:, pl.ds(0, half_width)], dx_half, dsem.at[0])
    dx_other = rdma(dx.at[:, pl.ds(half_width, half_width)], dx_half, dsem.at[1], dsem.at[2], mate)

    @pl.when(c == 0)
    def _():
        dx_own.start()
        dx_other.start()

    def parts(t, f):
        p = 2 * t + f
        a, b = bit[f], bit[1 - f]
        own = a * half
        other = (1 - a) * half
        return p, own, other, b

    def rows_at(start, n):
        return pl.ds(pl.multiple_of(start, 16), n)

    def panel_of(array, p, start, n):
        columns = pl.ds(pl.multiple_of(p % across_block * width, 128), width)
        return array.at[p // across_block, rows_at(start, n), columns]

    def own_load(t, f):
        p, own, other, b = parts(t, f)
        return pltpu.make_async_copy(panel_of(g, p, own, half), acc.at[p], lsem.at[p, 0])

    def own_store(t, f, k):
        p, own, other, b = parts(t, f)
        start = own if k == 0 else other
        return pltpu.make_async_copy(res.at[p, rows_at(start, half)], panel_of(out, p, start, half), lsem.at[p, k])

    def rs_a(t, f):
        p, own, other, b = parts(t, f)
        return rdma(panel_of(g, p, other, half), rx.at[p], asend.at[p], arecv.at[p, 0], across[f])

    def rs_up(t, f, j):
        p = 2 * t + f
        r = pl.ds((j + 1) * block, (NZ - 1 - j) * block)
        return rdma(acc.at[p, r], up.at[p, r], zsend.at[p, 0], zrecv.at[p, 0, 0], above)

    def rs_dn(t, f, j):
        p = 2 * t + f
        r = pl.ds(0, j * block)
        return rdma(acc.at[p, r], dn.at[p, r], zsend.at[p, 1], zrecv.at[p, 1, 0], below)

    def both_b(t, f):
        p, own, other, b = parts(t, f)
        return rdma(acc.at[p, rows_at(z * block, block)], ry.at[p], asend.at[p], arecv.at[p, 1], across[1 - f])

    def ag_up(t, f, m):
        p, own, other, b = parts(t, f)
        s = res.at[p, rows_at(own + (z - m) * block, block)]
        return rdma(s, s, zsend.at[p, 0], zrecv.at[p, 0, 1 + m], above)

    def ag_dn(t, f, m):
        p, own, other, b = parts(t, f)
        s = res.at[p, rows_at(own + (z + m) * block, block)]
        return rdma(s, s, zsend.at[p, 1], zrecv.at[p, 1, 1 + m], below)

    def ag_a(t, f):
        p, own, other, b = parts(t, f)
        s = res.at[p, rows_at(own, half)]
        return rdma(s, s, asend.at[p], arecv.at[p, 2], across[f])

    def s0(t, f):
        rs_a(t, f).start()
        own_load(t, f).start()

    def s1(t, f):
        p, own, other, b = parts(t, f)
        own_load(t, f).wait()
        rs_a(t, f).wait()
        acc[p] = acc[p] + rx[p]

        @pl.when(z == 0)
        def _():
            rs_up(t, f, 0).start()

        @pl.when(z == NZ - 1)
        def _():
            rs_dn(t, f, NZ - 1).start()

    def chain(t, f, j):
        p = 2 * t + f

        @pl.when(z == j)
        def _():
            rs_up(t, f, j - 1).wait_recv()
            r = pl.ds(j * block, (NZ - j) * block)
            acc[p, r] = acc[p, r] + up[p, r]
            if j < NZ - 1:
                rs_up(t, f, j).start()

        @pl.when(z == NZ - 1 - j)
        def _():
            rs_dn(t, f, NZ - j).wait_recv()
            r = pl.ds(0, (NZ - j) * block)
            acc[p, r] = acc[p, r] + dn[p, r]
            if j < NZ - 1:
                rs_dn(t, f, NZ - 1 - j).start()

    def s4(t, f):
        chain(t, f, NZ - 1)
        both_b(t, f).start()

    def s5(t, f):
        p, own, other, b = parts(t, f)
        both_b(t, f).wait()
        res[p, rows_at(own + z * block, block)] = acc[p, rows_at(z * block, block)] + ry[p]

        for j in range(NZ):

            @pl.when(z == j)
            def _(j=j):
                if j < NZ - 1:
                    rs_up(t, f, j).wait_send()
                    ag_up(t, f, 0).start()
                if j > 0:
                    rs_dn(t, f, j).wait_send()
                    ag_dn(t, f, 0).start()

    def spread(t, f, j):
        @pl.when(z >= j)
        def _():
            ag_up(t, f, j - 1).wait_recv()

            @pl.when(z < NZ - 1)
            def _():
                ag_up(t, f, j - 1).wait_send()
                ag_up(t, f, j).start()

        @pl.when(z + j <= NZ - 1)
        def _():
            ag_dn(t, f, j - 1).wait_recv()

            @pl.when(z > 0)
            def _():
                ag_dn(t, f, j - 1).wait_send()
                ag_dn(t, f, j).start()

    def s9(t, f):
        spread(t, f, NZ - 1)
        ag_a(t, f).start()
        own_store(t, f, 0).start()

    def s10(t, f):
        ag_a(t, f).wait()
        own_store(t, f, 1).start()
        @pl.when(z < NZ - 1)
        def _():
            ag_up(t, f, 0).wait_send()

        @pl.when(z > 0)
        def _():
            ag_dn(t, f, 0).wait_send()

    def s11(t, f):
        own_store(t, f, 0).wait()
        own_store(t, f, 1).wait()

    mates = across + (dev(x, y, z + 1 - 2 * (z % 2)), faraway)

    def norm_swap(j):
        return rdma(norms_out, nbuf.at[j], nsem.at[0, j], nsem.at[1, j], mates[j])

    norms_out[...] = norms[...]
    norm_swap(0).start()

    stages = (
        [(0, s0), (AHEAD, s1)]
        + [(AHEAD + j, functools.partial(lambda j, t, f: chain(t, f, j), j)) for j in range(1, NZ - 1)]
        + [(AHEAD + NZ - 1, s4), (AHEAD + NZ, s5)]
        + [(AHEAD + NZ + j, functools.partial(lambda j, t, f: spread(t, f, j), j)) for j in range(1, NZ - 1)]
        + [(AHEAD + 2 * NZ - 1, s9), (AHEAD + 2 * NZ + LATE, s10), (AHEAD + 2 * NZ + 1 + LATE, s11)]
    )

    def tick(tau, carry):
        for j in range(4):

            @pl.when(tau == 3 * j + 3)
            def _(j=j):
                norm_swap(j).wait()
                norms_out[...] = norms_out[...] + nbuf[j]
                if j < 3:
                    norm_swap(j + 1).start()

        for lag, stage in stages:
            t = tau - lag

            @pl.when((t >= 0) & (t < pairs))
            def _(stage=stage, t=t):
                stage(t, 0)
                stage(t, 1)
        return carry
    lax.fori_loop(0, pairs + AHEAD + 2 * NZ + 2 + LATE, tick, 0)

    @pl.when(c == 0)
    def _():
        dx_own.wait()
        dx_other.wait_send()

    @pl.when(c == 1)
    def _():
        dx_other.wait_recv()


def all_reduce(g, norms, dx, counts, collective_id):
    blocks, rows, block_width = g.shape
    width = 256
    across_block = block_width // width
    n = blocks * across_block
    half, block = rows // 2, rows // 8
    bf = jnp.bfloat16
    return pl.pallas_call(
        functools.partial(ar_kernel, [count * across_block // 2 for count in counts], rows, width, across_block),
        out_shape=(
            jax.ShapeDtypeStruct(g.shape, bf),
            jax.ShapeDtypeStruct(norms.shape, norms.dtype),
            jax.ShapeDtypeStruct((dx.shape[0], dx.shape[1] // 2), bf),
        ),
        in_specs=[pl.BlockSpec(memory_space=pl.ANY), pl.BlockSpec(memory_space=pltpu.VMEM), pl.BlockSpec(memory_space=pl.ANY)],
        out_specs=(pl.BlockSpec(memory_space=pl.ANY), pl.BlockSpec(memory_space=pltpu.VMEM), pl.BlockSpec(memory_space=pl.ANY)),
        scratch_shapes=[
            pltpu.VMEM((n, half, width), bf),
            pltpu.VMEM((n, rows, width), bf),
            pltpu.VMEM((n, half, width), bf),
            pltpu.VMEM((n, half, width), bf),
            pltpu.VMEM((n, half, width), bf),
            pltpu.VMEM((n, block, width), bf),
            pltpu.VMEM((4,) + norms.shape, norms.dtype),
            pltpu.SemaphoreType.DMA((n, 2)),
            pltpu.SemaphoreType.DMA((n,)),
            pltpu.SemaphoreType.DMA((n, 3)),
            pltpu.SemaphoreType.DMA((n, 2)),
            pltpu.SemaphoreType.DMA((n, 2, NZ)),
            pltpu.SemaphoreType.DMA((2, 4)),
            pltpu.SemaphoreType.DMA((3,)),
        ],
        compiler_params=pltpu.CompilerParams(collective_id=collective_id, has_side_effects=True, vmem_limit_bytes=60 * 2**20),
    )(g, norms, dx)


SLOTS = 4


def finish_kernel(counts, gathers, panels, pool, up_in, down_in, *rest):
    outs = rest[:5]
    inbox, stage, rows, grads, w_up, w_down, active, bent, sems, in_sems, out_sems = rest[5:]
    width = panels.shape[1]
    plain = sum(counts[:3])
    total = sum(counts)
    section = lax.axis_index("section")
    targets = []
    for count, out in zip(counts[:3], outs):
        targets += [out.at[0, :, pl.ds(j * width, width)] for j in range(count)]
    for j in range(counts[3]):
        targets += [outs[3].at[0, :, pl.ds(j * width, width)], outs[4].at[0, pl.ds(j * width, width)]]

    def load(n):
        return pltpu.make_async_copy(panels.at[n], inbox.at[n], in_sems.at[n])

    def store(n):
        return pltpu.make_async_copy(stage.at[n % SLOTS], targets[n], out_sems.at[n % SLOTS])

    def put(n, value):
        if n >= SLOTS:
            store(n - SLOTS).wait()
        stage[n % SLOTS] = value
        store(n).start()

    def widen(n):
        load(n).wait()
        put(n, inbox[n].astype(f32))

    for n in range(plain):
        load(n).start()
    summed = (section == 0) if gathers else (section >= 0)
    whole = [
        pltpu.make_async_copy(src, dst, sems.at[n])
        for n, (src, dst) in enumerate(((pool.at[1], rows), (pool.at[0], grads), (up_in, w_up), (down_in, w_down)))
    ]

    @pl.when(summed)
    def _():
        for n in range(plain, total):
            load(n).start()

    if gathers:

        @pl.when(section == 1)
        def _():
            for copy in whole:
                copy.start()

    for n in range(plain):
        widen(n)

    @pl.when(summed)
    def _():
        for n in range(plain, total):
            widen(n)

    if gathers:

        @pl.when(section == 1)
        def _():
            for copy in whole:
                copy.wait()
            size = rows.shape[0] // 4
            for j in range(counts[3]):
                cols = pl.ds(j * width, width)

                @pl.loop(0, 4)
                def _(i):
                    r = at(i * size, size, size)
                    e, s = gelu_both(nn(rows[r], w_up[:, cols]))
                    active[r] = e.astype(bf16)
                    bent[r] = (nt(grads[r], w_down[cols]) * s).astype(bf16)
                put(plain + 2 * j, tn(rows[...], bent[...]))
                put(plain + 2 * j + 1, tn(active[...], grads[...]))

    for n in range(total - SLOTS, total):
        store(n).wait()


def finish(panels, pool, w_up, w_down, shapes, gathers):
    total, high, wide = panels.shape
    counts = [rows * columns // (high * wide) for rows, columns in shapes]
    there = pl.BlockSpec(memory_space=pl.ANY)
    gathered = pool.shape[1] if gathers else 16
    return pl.pallas_call(
        functools.partial(finish_kernel, counts, gathers),
        out_shape=[jax.ShapeDtypeStruct((1,) + shape, f32) for shape in shapes],
        in_specs=[there] * 4,
        out_specs=[there] * 5,
        scratch_shapes=[
            pltpu.VMEM(panels.shape, bf16),
            pltpu.VMEM((SLOTS, high, wide), f32),
            pltpu.VMEM((gathered, wide), bf16),
            pltpu.VMEM((gathered, wide), bf16),
            pltpu.VMEM(w_up.shape, bf16),
            pltpu.VMEM(w_down.shape, bf16),
            pltpu.VMEM((gathered, wide), bf16),
            pltpu.VMEM((gathered, wide), bf16),
            pltpu.SemaphoreType.DMA((4,)),
            pltpu.SemaphoreType.DMA((total,)),
            pltpu.SemaphoreType.DMA((SLOTS,)),
        ],
        compiler_params=pltpu.CompilerParams(vmem_limit_bytes=62 * 2**20),
    )(panels, pool, w_up, w_down)


def per_device(
    enc_input,
    dec_input,
    out_grad,
    attn_qkv,
    attn_out,
    mlp_in,
    mlp_out,
    cross_proj,
    norm_gain,
    norm_shift,
    image_count,
    prefix_len,
    suffix_len,
):
    section = lax.axis_index("section")
    items, enc_len, width = enc_input.shape
    dec_len = dec_input.shape[1]
    span = -(-enc_len // 16) * 16
    weights = (attn_qkv[0], attn_out[0], mlp_in[0], mlp_out[0], cross_proj[0])
    positions = jnp.arange(span, dtype=jnp.int32)[None, :]
    has_image = (jnp.arange(items, dtype=jnp.int32) < image_count[0])[:, None]
    key_open = jnp.where(positions < PATCHES, has_image, positions - PATCHES < prefix_len[:, None])
    key_open = (key_open & (positions < enc_len)).astype(f32)[:, None, :]
    places = jnp.arange(items * dec_len, dtype=jnp.int32)
    item, spot = places // dec_len, places % dec_len
    self_open = (
        (item[:, None] == item[None, :])
        & (spot[None, :] <= spot[:, None])
        & (spot[None, :] < jnp.repeat(suffix_len, dec_len)[None, :])
    ).astype(f32)
    x = jnp.pad(enc_input, ((0, 0), (0, span - enc_len), (0, 0))).reshape(items * span, width)
    gathers = lax.axis_size("batch") == 16
    panels, norms, dx, dec_out, dy, pool = fused(
        x,
        dec_input.reshape(-1, width),
        out_grad.reshape(-1, width),
        weights,
        norm_gain[0].astype(f32),
        norm_shift[0].astype(f32),
        key_open,
        self_open,
        items,
        span,
        dec_len,
        gathers,
        1,
    )
    if gathers:
        blocks = panels.shape[0]
        panels, norms, dx_half = all_reduce(panels, norms, dx, (blocks, blocks - 2 * mlp_in.shape[2] // width), 0)
    else:
        panels, norms = lax.psum(panels, "batch"), lax.psum(norms, "batch")
        half = width // 2
        theirs = lax.dynamic_slice_in_dim(dx, (1 - section) * half, half, 1)
        theirs = lax.ppermute(theirs, "section", [(0, 1), (1, 0)])
        dx_half = jnp.where(section == 0, dx[:, :half], theirs)
    order = (0, 1, 4, 2, 3)
    pool = pool.reshape(2, -1, width) if gathers else pool[:, 0, 0, 0]
    blocks = finish(panels, pool, weights[2], weights[3], [weights[n].shape for n in order], gathers)
    grads = [blocks[order.index(n)] for n in range(len(order))]
    half = width // 2
    return (
        dec_out.reshape(items, dec_len, half),
        dx_half.reshape(items, span, half)[:, :enc_len],
        dy.reshape(items, dec_len, half),
        *grads,
        norms[None, :3],
        norms[None, 3:6],
    )


def solution(mesh):
    items = P("batch", None, None)
    matrix = P("section", None, None)
    halves = P("batch", None, "section")
    return jax.shard_map(
        per_device,
        mesh=mesh,
        in_specs=(items,) * 3 + (matrix,) * 7 + (P("batch"),) * 3,
        out_specs=(halves,) * 3 + (matrix,) * 7,
        check_vma=False,
    )
```

```python
import functools

import jax
import jax.numpy as jnp
from jax import lax
from jax.experimental import pallas as pl
from jax.experimental.pallas import tpu as pltpu
from jax.sharding import PartitionSpec as P

PATCHES = 196
MESH = pl.DeviceIdType.MESH
bf16, f32 = jnp.bfloat16, jnp.float32
epsilon = 1e-06
far_below = -1000000000.0
HEAD = 64
SLAB = 128
TILE = 256
GELU_A = 0.7978845608028654
GELU_B = 0.044715


NZ = 4


def place():
    b = lax.axis_index("batch")
    return b % 2, (b // 2) % 2, b // 4, lax.axis_index("section")


def bid(x, y, z):
    return z * 4 + y * 2 + x


def nn(a, b):
    return jnp.dot(a, b, preferred_element_type=f32)


def nt(a, b):
    return lax.dot_general(a, b, (((1,), (1,)), ((), ())), preferred_element_type=f32)


def tn(a, b):
    return lax.dot_general(a, b, (((0,), (0,)), ((), ())), preferred_element_type=f32)


def normal(v):
    centered = v - jnp.mean(v, axis=-1, keepdims=True)
    spread = lax.rsqrt(jnp.mean(centered * centered, axis=-1, keepdims=True) + epsilon)
    return centered * spread, spread


def gelu_both(u):
    square = u * u
    part = 0.5 + 0.5 * jnp.tanh(u * (GELU_A + (GELU_A * GELU_B) * square))
    slope = part + (part - part * part) * (u * (2.0 * GELU_A + (6.0 * GELU_A * GELU_B) * square))
    return u * part, slope


def at(start, size, unit):
    return pl.ds(pl.multiple_of(start, unit), size)


def gatherer(pool, rows, zsend, zrecv, asend, arecv, lsem):
    x, y, z, section = place()
    beside = ((section, bid(1 - x, y, z)), (section, bid(x, 1 - y, z)))
    above, below = (section, bid(x, y, z + 1)), (section, bid(x, y, z - 1))

    def remote(src, dst, send, recv, device):
        return pltpu.make_async_remote_copy(
            src_ref=src, dst_ref=dst, send_sem=send, recv_sem=recv, device_id=device, device_id_type=MESH
        )

    def half_rows(half):
        return pl.ds(half * (rows // 2), rows // 2)

    def along_z(half, way, k, source=None):
        spot = pool.at[k, y, x, half_rows(half)]
        source = spot if source is None else source
        return remote(source, spot, zsend.at[half, way, k], zrecv.at[half, way, k], (above, below)[way])

    def along_a(half):
        spot = pool.at[:, y, x, half_rows(half)]
        return remote(spot, spot, asend.at[half, 0], arecv.at[half, 0], beside[half])

    def along_b(half):
        spot = pool.at[:, y, :, half_rows(half)] if half == 0 else pool.at[:, :, x, half_rows(half)]
        return remote(spot, spot, asend.at[half, 1], arecv.at[half, 1], beside[1 - half])

    def advance(step, source):
        own = pltpu.make_async_copy(source, pool.at[z, y, x], lsem)
        if step == 0:
            own.start()
        for half in range(2):
            if step == 0:
                mine = source.at[half_rows(half)]

                @pl.when(z < NZ - 1)
                def _():
                    along_z(half, 0, z, mine).start()

                @pl.when(z > 0)
                def _():
                    along_z(half, 1, z, mine).start()
            elif step < NZ:

                @pl.when(z >= step)
                def _():
                    along_z(half, 0, z - step).wait_recv()

                    @pl.when(z < NZ - 1)
                    def _():
                        along_z(half, 0, z - step).start()

                @pl.when(z + step <= NZ - 1)
                def _():
                    along_z(half, 1, z + step).wait_recv()

                    @pl.when(z > 0)
                    def _():
                        along_z(half, 1, z + step).start()
            elif step == NZ:
                if half == 0:
                    own.wait()
                along_a(half).start()
            elif step == NZ + 1:
                along_a(half).wait_recv()
                along_b(half).start()
            else:
                along_b(half).wait()
                along_a(half).wait_send()
                for k in range(NZ):

                    @pl.when((k <= z) & (z < NZ - 1))
                    def _(k=k):
                        along_z(half, 0, k).wait_send()

                    @pl.when((k >= z) & (z > 0))
                    def _(k=k):
                        along_z(half, 1, k).wait_send()

    return advance


GATHER_STEPS = NZ + 3


def gather_semaphores():
    dma = pltpu.SemaphoreType.DMA
    return [dma((2, 2, NZ)), dma((2, 2, NZ)), dma((2, 2)), dma((2, 2)), dma]


def fused_kernel(items, span, enc_len, dec_len, gathers,
                 x_in, y_in, dz_in, wq_in, wo_in, wi_in, wd_in, wc_in, gain_in, shift_in, image_count, prefix_len, suffix_len,
                 panels, norms, dx_out, dec_out, dy_out, pool, mid_out,
                 w_qkv, w_out, w_up, w_down, w_cross,
                 qkv, prob, heads, low, rows_a, hidden, result, active, slope, crossing, stage,
                 wsem, xsem, psem, send_sem, recv_sem, zsend, zrecv, asend, arecv, lsem, hsend, hrecv):
    width = w_out.shape[0]
    hidden_units = w_up.shape[1]
    pairs = width // SLAB
    full = items * span
    blocks_up = hidden_units // width
    at_qkv, at_out, at_cross, at_up, at_down = 0, 3, 4, 6, 7
    section = lax.axis_index("section")
    chip = lax.axis_index("batch")
    other = (1 - section, chip)

    barrier = pltpu.get_barrier_semaphore()
    pl.semaphore_signal(barrier, inc=1, device_id=other, device_id_type=MESH)
    x, y, z, _ = place()
    beside = ((section, bid(1 - x, y, z)), (section, bid(x, 1 - y, z)))
    above, below = (section, bid(x, y, z + 1)), (section, bid(x, y, z - 1))
    if gathers:

        @pl.when(section == 1)
        def _():
            for device in beside:
                pl.semaphore_signal(barrier, inc=1, device_id=device, device_id_type=MESH)

            @pl.when(z < NZ - 1)
            def _():
                pl.semaphore_signal(barrier, inc=1, device_id=above, device_id_type=MESH)

            @pl.when(z > 0)
            def _():
                pl.semaphore_signal(barrier, inc=1, device_id=below, device_id_type=MESH)

    advance = gatherer(pool, items * dec_len, zsend, zrecv, asend, arecv, lsem)

    weights = ((wq_in, w_qkv), (wo_in, w_out), (wi_in, w_up), (wd_in, w_down), (wc_in, w_cross))
    loads = [pltpu.make_async_copy(src, dst, wsem.at[n]) for n, (src, dst) in enumerate(weights)]

    lane = lax.broadcasted_iota(jnp.int32, (1, SLAB), 1)
    is_first = lane < HEAD
    mask_a = jnp.where(is_first, 1.0, 0.0).astype(bf16)
    mask_b = jnp.where(is_first, 0.0, 1.0).astype(bf16)
    scale = HEAD ** (-0.5)
    gain, shift = gain_in[...].astype(f32), shift_in[...].astype(f32)
    spot = lax.broadcasted_iota(jnp.int32, (1, span), 1)

    def key_open(i):
        prefix = (spot >= PATCHES) & (spot - PATCHES < prefix_len[i])
        image = (spot < PATCHES) & (i < image_count[0])
        return (prefix | image) & (spot < enc_len)

    def stacked(slab, factor=1.0):
        return jnp.concatenate([slab * (mask_a * factor).astype(bf16), slab * (mask_b * factor).astype(bf16)], axis=0)

    def joined(both, rows):
        return jnp.where(is_first, both[:rows], both[rows:])

    def soft(scores, is_open):
        scores = jnp.where(is_open, scores, far_below)
        grown = jnp.exp(scores - jnp.max(scores, axis=-1, keepdims=True))
        return (grown * (1.0 / jnp.sum(grown, axis=-1, keepdims=True))).astype(bf16)

    def soft_back(p_low, dp):
        p = p_low.astype(f32)
        t = p * dp
        return (t - p * jnp.sum(t, axis=-1, keepdims=True)).astype(bf16)

    def wide(n):
        return at(n * width, width, width)

    def slab_of(n, h):
        return at(n * width + h * SLAB, SLAB, SLAB)

    def chunk(i):
        return pl.ds(i * span, span)

    def block_store(n, index):
        return pltpu.make_async_copy(stage.at[n % 2], panels.at[index], psem.at[n % 2])

    def emit(n, index, value):
        @pl.when(n >= 2)
        def _():
            block_store(n, index).wait()
        stage[n % 2] = value.astype(bf16)
        block_store(n, index).start()

    def norm_forward(value, index):
        unit, _ = normal(value)
        return (unit * gain[index : index + 1] + shift[index : index + 1]).astype(bf16)

    def norm_back(value, grad, index):
        unit, spread = normal(value)
        norms[index : index + 1] += jnp.sum(grad * unit, axis=0, keepdims=True)
        norms[3 + index : 4 + index] += jnp.sum(grad, axis=0, keepdims=True)
        scaled = grad * gain[index : index + 1]
        return spread * (
            scaled
            - jnp.mean(scaled, axis=-1, keepdims=True)
            - unit * jnp.mean(scaled * unit, axis=-1, keepdims=True)
        )

    def crossing_copy(source, n, tile):
        return pltpu.make_async_remote_copy(
            src_ref=source,
            dst_ref=crossing.at[:, at(tile * TILE, TILE, TILE)],
            send_sem=send_sem.at[n],
            recv_sem=recv_sem.at[tile],
            device_id=other,
            device_id_type=MESH,
        )

    def end_copy(n):
        dec = items * dec_len
        return pltpu.make_async_remote_copy(
            src_ref=heads.at[pl.ds((2 + n) * dec, dec), pl.ds(0, width // 2)],
            dst_ref=(dy_out, dec_out)[n],
            send_sem=hsend.at[n],
            recv_sem=hrecv.at[n],
            device_id=other,
            device_id_type=MESH,
        )

    tiles = width // TILE
    norms[...] = jnp.zeros_like(norms)

    @pl.when(section == 0)
    def _():
        x_load = pltpu.make_async_copy(x_in, low, xsem.at[0])
        x_load.start()
        loads[0].start()
        x_load.wait()
        for i in range(items):
            rows_a[chunk(i)] = norm_forward(low[chunk(i)].astype(f32), 0)
        loads[0].wait()
        for load in loads[1:]:
            load.start()

        @pl.loop(0, 3)
        def _(j):
            for i in range(items):
                qkv[chunk(i), wide(j)] = nn(rows_a[chunk(i)], w_qkv[:, wide(j)]).astype(bf16)

        @pl.loop(0, items)
        def _(i):
            r = at(i * span, span, 16)
            slabs = range(pairs)
            scores = [nt(stacked(qkv[r, slab_of(0, h)], scale), qkv[r, slab_of(1, h)]) for h in slabs]
            p = [soft(score, key_open(i)) for score in scores]
            out = [joined(nn(p[h], qkv[r, slab_of(2, h)]), span).astype(bf16) for h in slabs]
            for h in slabs:
                prob[i * pairs + h] = p[h]
                heads[r, slab_of(0, h)] = out[h]

        loads[1].wait()
        for i in range(items):
            r = chunk(i)
            value = low[r].astype(f32) + nn(heads[r], w_out[...])
            hidden[r] = value
            rows_a[r] = norm_forward(value, 1)
        loads[2].wait()

        @pl.loop(0, blocks_up)
        def _(j):
            for i in range(items):
                e, s = gelu_both(nn(rows_a[chunk(i)], w_up[:, wide(j)]))
                active[chunk(i), wide(j)] = e.astype(bf16)
                slope[chunk(i), wide(j)] = s.astype(bf16)

        loads[3].wait()
        for i in range(items):
            r = chunk(i)
            value = hidden[r] + nn(active[r], w_down[...])
            result[r] = value
            rows_a[r] = norm_forward(value, 2)
        loads[4].wait()
        pl.semaphore_wait(barrier, 1)

        def kv_send(n):
            return crossing_copy(low.at[:, at((n % 3) * TILE, TILE, TILE)], n, n // 2 + tiles * (n % 2))

        for n in range(2 * tiles):
            tile = n // 2 + tiles * (n % 2)
            if n >= 3:
                kv_send(n - 3).wait_send()
            for i in range(items):
                low[chunk(i), pl.ds((n % 3) * TILE, TILE)] = nn(rows_a[chunk(i)], w_cross[:, pl.ds(tile * TILE, TILE)]).astype(bf16)
            kv_send(n).start()
        for n in range(2 * tiles - 3, 2 * tiles):
            kv_send(n).wait_send()

        for n in range(2 * tiles):
            tile = n // 2 + tiles * (n % 2)
            crossing_copy(crossing.at[:, pl.ds(tile * TILE, TILE)], tile, tile).wait_recv()

        grads = [nt(crossing[chunk(i)], w_cross[...]) for i in range(items)]
        grads = [norm_back(result[chunk(i)], grads[i], 2) for i in range(items)]
        for i in range(items):
            result[chunk(i)] = grads[i]
            low[chunk(i)] = grads[i].astype(bf16)

        @pl.loop(0, 2)
        def _(j):
            emit(j, at_cross + j, tn(rows_a[...], crossing[:, wide(j)]))
        done = 2

        @pl.loop(0, blocks_up)
        def _(j):
            for i in range(items):
                r = chunk(i)
                slope[r, wide(j)] = (nt(low[r], w_down[wide(j)]) * slope[r, wide(j)].astype(f32)).astype(bf16)

        @pl.loop(0, blocks_up)
        def _(j):
            emit(done + j, at_down + 2 * j, tn(active[:, wide(j)], low[...]))
        done += blocks_up
        for i in range(items):
            rows_a[chunk(i)] = norm_forward(hidden[chunk(i)], 1)

        @pl.loop(0, blocks_up)
        def _(j):
            emit(done + j, at_up + 2 * j, tn(rows_a[...], slope[:, wide(j)]))
        done += blocks_up
        grads = [nt(slope[chunk(i)], w_up[...]) for i in range(items)]
        grads = [result[chunk(i)] + norm_back(hidden[chunk(i)], grads[i], 1) for i in range(items)]
        rounded = [grad.astype(bf16) for grad in grads]
        back = [nt(grad, w_out[...]).astype(bf16) for grad in rounded]
        for i in range(items):
            result[chunk(i)] = grads[i]
            low[chunk(i)] = rounded[i]
            rows_a[chunk(i)] = back[i]
        emit(done, at_out, tn(heads[...], low[...]))
        done += 1
        x_again = pltpu.make_async_copy(x_in, low, xsem.at[0])
        x_again.start()

        group = 3

        @pl.loop(0, items * pairs // group)
        def _(it):
            i = it // (pairs // group)
            r = at(i * span, span, 16)
            slabs = [group * (it % (pairs // group)) + u for u in range(group)]
            both = [stacked(rows_a[r, slab_of(0, h)]) for h in slabs]
            p = [prob[group * it + u] for u in range(group)]
            dp = [nt(both[u], qkv[r, slab_of(2, h)]) for u, h in enumerate(slabs)]
            dv = [tn(p[u], both[u]).astype(bf16) for u in range(group)]
            ds = [soft_back(p[u], dp[u]) for u in range(group)]
            dq = [(joined(nn(ds[u], qkv[r, slab_of(1, h)]), span) * scale).astype(bf16) for u, h in enumerate(slabs)]
            dk = [tn(ds[u], stacked(qkv[r, slab_of(0, h)], scale)).astype(bf16) for u, h in enumerate(slabs)]
            for u, h in enumerate(slabs):
                active[r, slab_of(0, h)] = dq[u]
                active[r, slab_of(1, h)] = dk[u]
                active[r, slab_of(2, h)] = dv[u]

        x_again.wait()
        for i in range(items):
            rows_a[chunk(i)] = norm_forward(low[chunk(i)].astype(f32), 0)

        @pl.loop(0, 3)
        def _(j):
            emit(done + j, at_qkv + j, tn(rows_a[...], active[:, wide(j)]))
        done += 3
        grads = [nt(active[chunk(i), pl.ds(0, 3 * width)], w_qkv[...]) for i in range(items)]
        grads = [result[chunk(i)] + norm_back(low[chunk(i)].astype(f32), grads[i], 0) for i in range(items)]
        for i in range(items):
            heads[chunk(i)] = grads[i].astype(bf16)
        dx_store = pltpu.make_async_copy(heads, dx_out, xsem.at[0])
        dx_store.start()
        block_store(0, 0).wait()
        block_store(1, 0).wait()
        dx_store.wait()
        for n in range(2):
            end_copy(n).wait_recv()

    @pl.when(section == 1)
    def _():
        dec = items * dec_len
        ra, rb, rc, rd = (pl.ds(n * dec, dec) for n in range(4))
        for n in (0, 1, 4, 2, 3):
            loads[n].start()
        rows_a[ra] = norm_forward(y_in[...].astype(f32), 0)
        if gathers:
            pl.semaphore_wait(barrier, 3 + (z + NZ - 1) // NZ + (2 * NZ - 2 - z) // NZ)
        if gathers:
            advance(0, dz_in)
        loads[0].wait()

        @pl.loop(0, 3)
        def _(j):
            qkv[ra, wide(j)] = nn(rows_a[ra], w_qkv[:, wide(j)]).astype(bf16)

        row = lax.broadcasted_iota(jnp.int32, (2 * dec, dec), 0) % dec
        column = lax.broadcasted_iota(jnp.int32, (2 * dec, dec), 1)
        item, place_in = column // dec_len, column % dec_len
        length = jnp.zeros_like(column)
        for i in range(items):
            length = jnp.where(item == i, suffix_len[i], length)
        own = (row // dec_len == item) & (place_in <= row % dec_len) & (place_in < length)

        slabs = range(pairs)
        scores = [nt(stacked(qkv[ra, slab_of(0, h)], scale), qkv[ra, slab_of(1, h)]) for h in slabs]
        p = [soft(score, own) for score in scores]
        out = [joined(nn(p[h], qkv[ra, slab_of(2, h)]), dec).astype(bf16) for h in slabs]
        for h in slabs:
            prob[h, pl.ds(0, 2 * dec), pl.ds(0, dec)] = p[h]
            heads[ra, slab_of(0, h)] = out[h]

        if gathers:
            advance(1, dz_in)
        loads[1].wait()
        value = y_in[...].astype(f32) + nn(heads[ra], w_out[...])
        hidden[ra] = value
        rows_a[rb] = norm_forward(value, 1)
        loads[4].wait()
        low[rb] = nn(rows_a[rb], w_cross[:, pl.ds(0, width)]).astype(bf16)
        loads[2].wait()
        loads[3].wait()
        if gathers:
            for step in range(2, GATHER_STEPS):
                advance(step, dz_in)

        part = 2 * dec_len
        spots = [(u, i) for u in range(TILE // SLAB) for i in range(items)]
        open_keys = [jnp.where(key_open(i), 1.0, 0.0) for i in range(items)]
        key_rows = jnp.concatenate([jnp.broadcast_to(open_keys[i], (part, span)) for u, i in spots], axis=0)

        @pl.loop(0, tiles)
        def _(t):
            for tile in (t, tiles + t):
                crossing_copy(crossing.at[:, at(tile * TILE, TILE, TILE)], tile, tile).wait_recv()

            def slab(n, u):
                return at(n * width + t * TILE + u * SLAB, SLAB, SLAB)
            scores = [
                nt(stacked(low[pl.ds(dec + i * dec_len, dec_len), slab(0, u)], scale), crossing[chunk(i), slab(0, u)])
                for u, i in spots
            ]
            p = soft(jnp.concatenate(scores, axis=0), key_rows > 0.0)
            for u in range(TILE // SLAB):
                prob[pairs + t * (TILE // SLAB) + u, pl.ds(0, items * part)] = p[u * items * part : (u + 1) * items * part]
            out = [nn(p[n * part : (n + 1) * part], crossing[chunk(i), slab(1, u)]) for n, (u, i) in enumerate(spots)]
            for n, (u, i) in enumerate(spots):
                heads[pl.ds(dec + i * dec_len, dec_len), slab(0, u)] = joined(out[n], dec_len).astype(bf16)

        value = hidden[ra] + nn(heads[rb], w_cross[:, pl.ds(width, width)])
        hidden[rb] = value
        rows_a[rc] = norm_forward(value, 2)
        mid_out[...] = rows_a[rc]

        @pl.loop(0, blocks_up)
        def _(j):
            e, s = gelu_both(nn(rows_a[rc], w_up[:, wide(j)]))
            active[ra, wide(j)] = e.astype(bf16)
            active[rb, wide(j)] = (nt(dz_in[...], w_down[wide(j)]) * s).astype(bf16)


        value = dz_in[...].astype(f32) + norm_back(hidden[rb], nt(active[rb], w_up[...]), 2)
        result[ra] = value
        low[ra] = value.astype(bf16)
        rows_a[rd] = nt(low[ra], w_cross[:, pl.ds(width, width)]).astype(bf16)
        if not gathers:
            pl.semaphore_wait(barrier, 1)

        def kv_back(tile):
            return crossing_copy(slope.at[:, at(tile * TILE, TILE, TILE)], tile, tile)

        @pl.loop(0, tiles)
        def _(t):
            def slab(n, u):
                return at(n * width + t * TILE + u * SLAB, SLAB, SLAB)
            both = [stacked(rows_a[pl.ds(3 * dec + i * dec_len, dec_len), slab(0, u)]) for u, i in spots]
            dp = jnp.concatenate([nt(both[n], crossing[chunk(i), slab(1, u)]) for n, (u, i) in enumerate(spots)], axis=0)
            p = jnp.concatenate(
                [prob[pairs + t * (TILE // SLAB) + u, pl.ds(0, items * part)] for u in range(TILE // SLAB)], axis=0
            )
            lines = [slice(n * part, (n + 1) * part) for n in range(len(spots))]
            dv = [tn(p[lines[n]], both[n]).astype(bf16) for n in range(len(spots))]
            q = [stacked(low[pl.ds(dec + i * dec_len, dec_len), slab(0, u)], scale) for u, i in spots]
            ds = soft_back(p, dp)
            dk = [tn(ds[lines[n]], q[n]).astype(bf16) for n in range(len(spots))]
            for n, (u, i) in enumerate(spots):
                slope[chunk(i), slab(0, u)] = dk[n]
                slope[chunk(i), slab(1, u)] = dv[n]
            kv_back(t).start()
            kv_back(tiles + t).start()
            back = [joined(nn(ds[lines[n]], crossing[chunk(i), slab(0, u)]), dec_len) * scale for n, (u, i) in enumerate(spots)]
            for n, (u, i) in enumerate(spots):
                low[pl.ds(3 * dec + i * dec_len, dec_len), slab(0, u)] = back[n].astype(bf16)


        done = 0
        if not gathers:

            @pl.loop(0, blocks_up)
            def _(j):
                emit(j, at_down + 2 * j, tn(active[ra, wide(j)], dz_in[...]))

            @pl.loop(0, blocks_up)
            def _(j):
                emit(blocks_up + j, at_up + 2 * j, tn(rows_a[rc], active[rb, wide(j)]))
            done = 2 * blocks_up
        emit(done, at_cross + 1, tn(heads[rb], low[ra]))
        emit(done + 1, at_cross, tn(rows_a[rb], low[rd]))
        done += 2
        value = result[ra] + norm_back(hidden[ra], nt(low[rd], w_cross[:, pl.ds(0, width)]), 1)
        result[ra] = value
        low[ra] = value.astype(bf16)
        emit(done, at_out, tn(heads[ra], low[ra]))
        done += 1
        rows_a[rd] = nt(low[ra], w_out[...]).astype(bf16)

        both = [stacked(rows_a[rd, slab_of(0, h)]) for h in slabs]
        p = [prob[h, pl.ds(0, 2 * dec), pl.ds(0, dec)] for h in slabs]
        dp = [nt(both[h], qkv[ra, slab_of(2, h)]) for h in slabs]
        dv = [tn(p[h], both[h]).astype(bf16) for h in slabs]
        ds = [soft_back(p[h], dp[h]) for h in slabs]
        dq = [(joined(nn(ds[h], qkv[ra, slab_of(1, h)]), dec) * scale).astype(bf16) for h in slabs]
        dk = [tn(ds[h], stacked(qkv[ra, slab_of(0, h)], scale)).astype(bf16) for h in slabs]
        for h in slabs:
            qkv[rb, slab_of(0, h)] = dq[h]
            qkv[rb, slab_of(1, h)] = dk[h]
            qkv[rb, slab_of(2, h)] = dv[h]


        @pl.loop(0, 3)
        def _(j):
            emit(done + j, at_qkv + j, tn(rows_a[ra], qkv[rb, wide(j)]))
        done += 3
        grad = nt(qkv[rb], w_qkv[...])
        half_width = width // 2
        ends = (
            (result[ra] + norm_back(y_in[...].astype(f32), grad, 0)).astype(bf16),
            (hidden[rb] + nn(active[ra], w_down[...])).astype(bf16),
        )
        for n, (value, out) in enumerate(zip(ends, (dy_out, dec_out))):
            out[...] = value[:, half_width:]
            heads[pl.ds((2 + n) * dec, dec), pl.ds(0, half_width)] = value[:, :half_width]
            end_copy(n).start()
        block_store(0, 0).wait()
        block_store(1, 0).wait()
        for n in range(2):
            end_copy(n).wait_send()
        for tile in range(2 * tiles):
            kv_back(tile).wait_send()


def fused(x, y, dz, weights, gain, shift, lengths, items, span, enc_len, dec_len, gathers, collective_id):
    wq, wo, wi, wd, wc = weights
    width, hidden_units = wi.shape
    full = items * span
    dec = items * dec_len
    count = sum(w.size for w in weights) // (width * width)
    here = pl.BlockSpec(memory_space=pltpu.VMEM)
    there = pl.BlockSpec(memory_space=pl.ANY)
    pairs = width // SLAB
    return pl.pallas_call(
        functools.partial(fused_kernel, items, span, enc_len, dec_len, gathers),
        out_shape=(
            jax.ShapeDtypeStruct((count, width, width), bf16),
            jax.ShapeDtypeStruct((8, width), f32),
            jax.ShapeDtypeStruct((full, width), bf16),
            jax.ShapeDtypeStruct((dec, width // 2), bf16),
            jax.ShapeDtypeStruct((dec, width // 2), bf16),
            jax.ShapeDtypeStruct((NZ, 2, 2, dec, width), bf16),
            jax.ShapeDtypeStruct((dec, width), bf16),
        ),
        in_specs=[there, here, here] + [there] * 5 + [here] * 2 + [pl.BlockSpec(memory_space=pltpu.SMEM)] * 3,
        out_specs=(there, here, there, here, here, there, here),
        scratch_shapes=[
            pltpu.VMEM(wq.shape, bf16),
            pltpu.VMEM(wo.shape, bf16),
            pltpu.VMEM(wi.shape, bf16),
            pltpu.VMEM(wd.shape, bf16),
            pltpu.VMEM(wc.shape, bf16),
            pltpu.VMEM((full, 3 * width), bf16),
            pltpu.VMEM((items * pairs, 2 * span, span), bf16),
            pltpu.VMEM((full, width), bf16),
            pltpu.VMEM((full, width), bf16),
            pltpu.VMEM((full, width), bf16),
            pltpu.VMEM((full, width), f32),
            pltpu.VMEM((full, width), f32),
            pltpu.VMEM((full, hidden_units), bf16),
            pltpu.VMEM((full, hidden_units), bf16),
            pltpu.VMEM((full, 2 * width), bf16),
            pltpu.VMEM((2, width, width), bf16),
            pltpu.SemaphoreType.DMA((5,)),
            pltpu.SemaphoreType.DMA((1,)),
            pltpu.SemaphoreType.DMA((2,)),
            pltpu.SemaphoreType.DMA((2 * width // TILE,)),
            pltpu.SemaphoreType.DMA((2 * width // TILE,)),
            *gather_semaphores(),
            pltpu.SemaphoreType.DMA((2,)),
            pltpu.SemaphoreType.DMA((2,)),
        ],
        compiler_params=pltpu.CompilerParams(
            collective_id=collective_id, has_side_effects=True, vmem_limit_bytes=63 * 2**20
        ),
    )(x, y, dz, wq, wo, wi, wd, wc, gain, shift, *lengths)


AHEAD = 2
LATE = 2


def ar_kernel(pairs, rows, width, across_block, g, norms, dx, mid, out, norms_out, dx_half, pool, acc, res, rx, up, dn, ry, nbuf, lsem, asend, arecv, zsend, zrecv, nsem, dsem, *gather_sems):
    x, y, z, c = place()
    pairs = pairs[0] + (pairs[1] - pairs[0]) * c
    half, block = rows // 2, rows // 8

    def dev(x, y, z):
        return (c, bid(x, y, z))

    across = (dev(1 - x, y, z), dev(x, 1 - y, z))
    above, below = dev(x, y, z + 1), dev(x, y, z - 1)
    bit = (x, y)

    barrier = pltpu.get_barrier_semaphore()
    faraway = dev(x, y, (z + 2) % NZ)
    for d in across + (faraway,):
        pl.semaphore_signal(barrier, inc=1, device_id=d, device_id_type=MESH)

    @pl.when(z < NZ - 1)
    def _():
        pl.semaphore_signal(barrier, inc=1, device_id=above, device_id_type=MESH)

    @pl.when(z > 0)
    def _():
        pl.semaphore_signal(barrier, inc=1, device_id=below, device_id_type=MESH)

    mate = (1 - c, bid(x, y, z))

    @pl.when(c == 1)
    def _():
        pl.semaphore_signal(barrier, inc=1, device_id=mate, device_id_type=MESH)

    pl.semaphore_wait(barrier, 4 - c + (z + NZ - 1) // NZ + (2 * NZ - 2 - z) // NZ)

    def rdma(src, dst, send, recv, device):
        return pltpu.make_async_remote_copy(src_ref=src, dst_ref=dst, send_sem=send, recv_sem=recv, device_id=device, device_id_type=MESH)

    half_width = dx.shape[1] // 2
    dx_own = pltpu.make_async_copy(dx.at[:, pl.ds(0, half_width)], dx_half, dsem.at[0])
    dx_other = rdma(dx.at[:, pl.ds(half_width, half_width)], dx_half, dsem.at[1], dsem.at[2], mate)

    @pl.when(c == 0)
    def _():
        dx_own.start()
        dx_other.start()

    def parts(t, f):
        p = 2 * t + f
        a, b = bit[f], bit[1 - f]
        own = a * half
        other = (1 - a) * half
        return p, own, other, b

    def rows_at(start, n):
        return pl.ds(pl.multiple_of(start, 16), n)

    def panel_of(array, p, start, n):
        columns = pl.ds(pl.multiple_of(p % across_block * width, 128), width)
        return array.at[p // across_block, rows_at(start, n), columns]

    def own_load(t, f):
        p, own, other, b = parts(t, f)
        return pltpu.make_async_copy(panel_of(g, p, own, half), acc.at[p], lsem.at[p, 0])

    def own_store(t, f, k):
        p, own, other, b = parts(t, f)
        start = own if k == 0 else other
        return pltpu.make_async_copy(res.at[p, rows_at(start, half)], panel_of(out, p, start, half), lsem.at[p, k])

    def rs_a(t, f):
        p, own, other, b = parts(t, f)
        return rdma(panel_of(g, p, other, half), rx.at[p], asend.at[p], arecv.at[p, 0], across[f])

    def rs_up(t, f, j):
        p = 2 * t + f
        r = pl.ds((j + 1) * block, (NZ - 1 - j) * block)
        return rdma(acc.at[p, r], up.at[p, r], zsend.at[p, 0], zrecv.at[p, 0, 0], above)

    def rs_dn(t, f, j):
        p = 2 * t + f
        r = pl.ds(0, j * block)
        return rdma(acc.at[p, r], dn.at[p, r], zsend.at[p, 1], zrecv.at[p, 1, 0], below)

    def both_b(t, f):
        p, own, other, b = parts(t, f)
        return rdma(acc.at[p, rows_at(z * block, block)], ry.at[p], asend.at[p], arecv.at[p, 1], across[1 - f])

    def ag_up(t, f, m):
        p, own, other, b = parts(t, f)
        s = res.at[p, rows_at(own + (z - m) * block, block)]
        return rdma(s, s, zsend.at[p, 0], zrecv.at[p, 0, 1 + m], above)

    def ag_dn(t, f, m):
        p, own, other, b = parts(t, f)
        s = res.at[p, rows_at(own + (z + m) * block, block)]
        return rdma(s, s, zsend.at[p, 1], zrecv.at[p, 1, 1 + m], below)

    def ag_a(t, f):
        p, own, other, b = parts(t, f)
        s = res.at[p, rows_at(own, half)]
        return rdma(s, s, asend.at[p], arecv.at[p, 2], across[f])

    def s0(t, f):
        rs_a(t, f).start()
        own_load(t, f).start()

    def s1(t, f):
        p, own, other, b = parts(t, f)
        own_load(t, f).wait()
        rs_a(t, f).wait()
        acc[p] = acc[p] + rx[p]

        @pl.when(z == 0)
        def _():
            rs_up(t, f, 0).start()

        @pl.when(z == NZ - 1)
        def _():
            rs_dn(t, f, NZ - 1).start()

    def chain(t, f, j):
        p = 2 * t + f

        @pl.when(z == j)
        def _():
            rs_up(t, f, j - 1).wait_recv()
            r = pl.ds(j * block, (NZ - j) * block)
            acc[p, r] = acc[p, r] + up[p, r]
            if j < NZ - 1:
                rs_up(t, f, j).start()

        @pl.when(z == NZ - 1 - j)
        def _():
            rs_dn(t, f, NZ - j).wait_recv()
            r = pl.ds(0, (NZ - j) * block)
            acc[p, r] = acc[p, r] + dn[p, r]
            if j < NZ - 1:
                rs_dn(t, f, NZ - 1 - j).start()

    def s4(t, f):
        chain(t, f, NZ - 1)
        both_b(t, f).start()

    def s5(t, f):
        p, own, other, b = parts(t, f)
        both_b(t, f).wait()
        res[p, rows_at(own + z * block, block)] = acc[p, rows_at(z * block, block)] + ry[p]

        for j in range(NZ):

            @pl.when(z == j)
            def _(j=j):
                if j < NZ - 1:
                    rs_up(t, f, j).wait_send()
                    ag_up(t, f, 0).start()
                if j > 0:
                    rs_dn(t, f, j).wait_send()
                    ag_dn(t, f, 0).start()

    def spread(t, f, j):
        @pl.when(z >= j)
        def _():
            ag_up(t, f, j - 1).wait_recv()

            @pl.when(z < NZ - 1)
            def _():
                ag_up(t, f, j - 1).wait_send()
                ag_up(t, f, j).start()

        @pl.when(z + j <= NZ - 1)
        def _():
            ag_dn(t, f, j - 1).wait_recv()

            @pl.when(z > 0)
            def _():
                ag_dn(t, f, j - 1).wait_send()
                ag_dn(t, f, j).start()

    def s9(t, f):
        spread(t, f, NZ - 1)
        ag_a(t, f).start()
        own_store(t, f, 0).start()

    def s10(t, f):
        ag_a(t, f).wait()
        own_store(t, f, 1).start()
        @pl.when(z < NZ - 1)
        def _():
            ag_up(t, f, 0).wait_send()

        @pl.when(z > 0)
        def _():
            ag_dn(t, f, 0).wait_send()

    def s11(t, f):
        own_store(t, f, 0).wait()
        own_store(t, f, 1).wait()

    mates = across + (dev(x, y, z + 1 - 2 * (z % 2)), faraway)

    def norm_swap(j):
        return rdma(norms_out, nbuf.at[j], nsem.at[0, j], nsem.at[1, j], mates[j])

    norms_out[...] = norms[...]
    norm_swap(0).start()

    stages = (
        [(0, s0), (AHEAD, s1)]
        + [(AHEAD + j, functools.partial(lambda j, t, f: chain(t, f, j), j)) for j in range(1, NZ - 1)]
        + [(AHEAD + NZ - 1, s4), (AHEAD + NZ, s5)]
        + [(AHEAD + NZ + j, functools.partial(lambda j, t, f: spread(t, f, j), j)) for j in range(1, NZ - 1)]
        + [(AHEAD + 2 * NZ - 1, s9), (AHEAD + 2 * NZ + LATE, s10), (AHEAD + 2 * NZ + 1 + LATE, s11)]
    )

    advance = gatherer(pool, mid.shape[0], *gather_sems)

    def tick(tau, carry):
        for step in range(GATHER_STEPS):

            @pl.when((c == 1) & (tau == 2 * step))
            def _(step=step):
                advance(step, mid)

        for j in range(4):

            @pl.when(tau == 3 * j + 3)
            def _(j=j):
                norm_swap(j).wait()
                norms_out[...] = norms_out[...] + nbuf[j]
                if j < 3:
                    norm_swap(j + 1).start()

        for lag, stage in stages:
            t = tau - lag

            @pl.when((t >= 0) & (t < pairs))
            def _(stage=stage, t=t):
                stage(t, 0)
                stage(t, 1)
        return carry
    lax.fori_loop(0, pairs + AHEAD + 2 * NZ + 2 + LATE, tick, 0)

    @pl.when(c == 0)
    def _():
        dx_own.wait()
        dx_other.wait_send()

    @pl.when(c == 1)
    def _():
        dx_other.wait_recv()


def all_reduce(g, norms, dx, mid, counts, collective_id):
    blocks, rows, block_width = g.shape
    width = 256
    across_block = block_width // width
    n = blocks * across_block
    half, block = rows // 2, rows // 8
    bf = jnp.bfloat16
    return pl.pallas_call(
        functools.partial(ar_kernel, [count * across_block // 2 for count in counts], rows, width, across_block),
        out_shape=(
            jax.ShapeDtypeStruct(g.shape, bf),
            jax.ShapeDtypeStruct(norms.shape, norms.dtype),
            jax.ShapeDtypeStruct((dx.shape[0], dx.shape[1] // 2), bf),
            jax.ShapeDtypeStruct((NZ, 2, 2) + mid.shape, bf),
        ),
        in_specs=[pl.BlockSpec(memory_space=pl.ANY), pl.BlockSpec(memory_space=pltpu.VMEM), pl.BlockSpec(memory_space=pl.ANY), pl.BlockSpec(memory_space=pl.ANY)],
        out_specs=(pl.BlockSpec(memory_space=pl.ANY), pl.BlockSpec(memory_space=pltpu.VMEM), pl.BlockSpec(memory_space=pl.ANY), pl.BlockSpec(memory_space=pl.ANY)),
        scratch_shapes=[
            pltpu.VMEM((n, half, width), bf),
            pltpu.VMEM((n, rows, width), bf),
            pltpu.VMEM((n, half, width), bf),
            pltpu.VMEM((n, half, width), bf),
            pltpu.VMEM((n, half, width), bf),
            pltpu.VMEM((n, block, width), bf),
            pltpu.VMEM((4,) + norms.shape, norms.dtype),
            pltpu.SemaphoreType.DMA((n, 2)),
            pltpu.SemaphoreType.DMA((n,)),
            pltpu.SemaphoreType.DMA((n, 3)),
            pltpu.SemaphoreType.DMA((n, 2)),
            pltpu.SemaphoreType.DMA((n, 2, NZ)),
            pltpu.SemaphoreType.DMA((2, 4)),
            pltpu.SemaphoreType.DMA((3,)),
            *gather_semaphores(),
        ],
        compiler_params=pltpu.CompilerParams(collective_id=collective_id, has_side_effects=True, vmem_limit_bytes=60 * 2**20),
    )(g, norms, dx, mid)


SLOTS = 4


def finish_kernel(counts, gathers, panels, pool_rows, pool_grads, up_in, down_in, *rest):
    outs = rest[:5]
    inbox, stage, rows, grads, w_up, w_down, active, bent, sems, in_sems, out_sems = rest[5:]
    width = panels.shape[1]
    plain = sum(counts[:3])
    total = sum(counts)
    section = lax.axis_index("section")
    targets = []
    for count, out in zip(counts[:3], outs):
        targets += [out.at[0, :, pl.ds(j * width, width)] for j in range(count)]
    for j in range(counts[3]):
        targets += [outs[3].at[0, :, pl.ds(j * width, width)], outs[4].at[0, pl.ds(j * width, width)]]

    def load(n):
        return pltpu.make_async_copy(panels.at[n], inbox.at[n], in_sems.at[n])

    def store(n):
        return pltpu.make_async_copy(stage.at[n % SLOTS], targets[n], out_sems.at[n % SLOTS])

    def put(n, value):
        if n >= SLOTS:
            store(n - SLOTS).wait()
        stage[n % SLOTS] = value
        store(n).start()

    def widen(n):
        load(n).wait()
        put(n, inbox[n].astype(f32))

    for n in range(plain):
        load(n).start()
    summed = (section == 0) if gathers else (section >= 0)
    whole = [
        pltpu.make_async_copy(src, dst, sems.at[n])
        for n, (src, dst) in enumerate(((pool_rows, rows), (pool_grads, grads), (up_in, w_up), (down_in, w_down)))
    ]

    @pl.when(summed)
    def _():
        for n in range(plain, total):
            load(n).start()

    if gathers:

        @pl.when(section == 1)
        def _():
            for copy in whole:
                copy.start()

    for n in range(plain):
        widen(n)

    @pl.when(summed)
    def _():
        for n in range(plain, total):
            widen(n)

    if gathers:

        @pl.when(section == 1)
        def _():
            for copy in whole:
                copy.wait()
            size = rows.shape[0] // 4
            for j in range(counts[3]):
                cols = pl.ds(j * width, width)

                @pl.loop(0, 4)
                def _(i):
                    r = at(i * size, size, size)
                    e, s = gelu_both(nn(rows[r], w_up[:, cols]))
                    active[r] = e.astype(bf16)
                    bent[r] = (nt(grads[r], w_down[cols]) * s).astype(bf16)
                put(plain + 2 * j, tn(rows[...], bent[...]))
                put(plain + 2 * j + 1, tn(active[...], grads[...]))

    for n in range(total - SLOTS, total):
        store(n).wait()


def finish(panels, pool_rows, pool_grads, w_up, w_down, shapes, gathers):
    total, high, wide = panels.shape
    counts = [rows * columns // (high * wide) for rows, columns in shapes]
    there = pl.BlockSpec(memory_space=pl.ANY)
    gathered = pool_rows.shape[0] if gathers else 16
    return pl.pallas_call(
        functools.partial(finish_kernel, counts, gathers),
        out_shape=[jax.ShapeDtypeStruct((1,) + shape, f32) for shape in shapes],
        in_specs=[there] * 5,
        out_specs=[there] * 5,
        scratch_shapes=[
            pltpu.VMEM(panels.shape, bf16),
            pltpu.VMEM((SLOTS, high, wide), f32),
            pltpu.VMEM((gathered, wide), bf16),
            pltpu.VMEM((gathered, wide), bf16),
            pltpu.VMEM(w_up.shape, bf16),
            pltpu.VMEM(w_down.shape, bf16),
            pltpu.VMEM((gathered, wide), bf16),
            pltpu.VMEM((gathered, wide), bf16),
            pltpu.SemaphoreType.DMA((4,)),
            pltpu.SemaphoreType.DMA((total,)),
            pltpu.SemaphoreType.DMA((SLOTS,)),
        ],
        compiler_params=pltpu.CompilerParams(vmem_limit_bytes=62 * 2**20),
    )(panels, pool_rows, pool_grads, w_up, w_down)


def per_device(
    enc_input,
    dec_input,
    out_grad,
    attn_qkv,
    attn_out,
    mlp_in,
    mlp_out,
    cross_proj,
    norm_gain,
    norm_shift,
    image_count,
    prefix_len,
    suffix_len,
):
    section = lax.axis_index("section")
    items, enc_len, width = enc_input.shape
    dec_len = dec_input.shape[1]
    span = -(-enc_len // 16) * 16
    weights = (attn_qkv[0], attn_out[0], mlp_in[0], mlp_out[0], cross_proj[0])
    x = jnp.pad(enc_input, ((0, 0), (0, span - enc_len), (0, 0))).reshape(items * span, width)
    gathers = lax.axis_size("batch") == 16
    panels, norms, dx, dec_out, dy, grad_rows, mid = fused(
        x,
        dec_input.reshape(-1, width),
        out_grad.reshape(-1, width),
        weights,
        norm_gain[0],
        norm_shift[0],
        (image_count, prefix_len, suffix_len),
        items,
        span,
        enc_len,
        dec_len,
        gathers,
        1,
    )
    if gathers:
        blocks = panels.shape[0]
        panels, norms, dx_half, rows = all_reduce(panels, norms, dx, mid, (blocks, blocks - 2 * mlp_in.shape[2] // width), 0)
    else:
        panels, norms = lax.psum(panels, "batch"), lax.psum(norms, "batch")
        half = width // 2
        theirs = lax.dynamic_slice_in_dim(dx, (1 - section) * half, half, 1)
        theirs = lax.ppermute(theirs, "section", [(0, 1), (1, 0)])
        dx_half = jnp.where(section == 0, dx[:, :half], theirs)
    order = (0, 1, 4, 2, 3)
    rows = rows.reshape(-1, width) if gathers else mid
    blocks = finish(panels, rows, grad_rows.reshape(-1, width), weights[2], weights[3], [weights[n].shape for n in order], gathers)
    grads = [blocks[order.index(n)] for n in range(len(order))]
    half = width // 2
    return (
        dec_out.reshape(items, dec_len, half),
        dx_half.reshape(items, span, half)[:, :enc_len],
        dy.reshape(items, dec_len, half),
        *grads,
        norms[None, :3],
        norms[None, 3:6],
    )


def solution(mesh):
    items = P("batch", None, None)
    matrix = P("section", None, None)
    halves = P("batch", None, "section")
    return jax.shard_map(
        per_device,
        mesh=mesh,
        in_specs=(items,) * 3 + (matrix,) * 7 + (P("batch"),) * 3,
        out_specs=(halves,) * 3 + (matrix,) * 7,
        check_vma=False,
    )
```

```python
import functools

import jax
import jax.numpy as jnp
from jax import lax
from jax.experimental import pallas as pl
from jax.experimental.pallas import tpu as pltpu
from jax.sharding import PartitionSpec as P

PATCHES = 196
MESH = pl.DeviceIdType.MESH
bf16, f32 = jnp.bfloat16, jnp.float32
epsilon = 1e-06
far_below = -1000000000.0
HEAD = 64
SLAB = 128
TILE = 256
GELU_A = 0.7978845608028654
GELU_B = 0.044715


NZ = 4


def place():
    b = lax.axis_index("batch")
    return b % 2, (b // 2) % 2, b // 4, lax.axis_index("section")


def bid(x, y, z):
    return z * 4 + y * 2 + x


def nn(a, b):
    return jnp.dot(a, b, preferred_element_type=f32)


def nt(a, b):
    return lax.dot_general(a, b, (((1,), (1,)), ((), ())), preferred_element_type=f32)


def tn(a, b):
    return lax.dot_general(a, b, (((0,), (0,)), ((), ())), preferred_element_type=f32)


def normal(v):
    centered = v - jnp.mean(v, axis=-1, keepdims=True)
    spread = lax.rsqrt(jnp.mean(centered * centered, axis=-1, keepdims=True) + epsilon)
    return centered * spread, spread


def gelu_both(u):
    square = u * u
    part = 0.5 + 0.5 * jnp.tanh(u * (GELU_A + (GELU_A * GELU_B) * square))
    slope = part + (part - part * part) * (u * (2.0 * GELU_A + (6.0 * GELU_A * GELU_B) * square))
    return u * part, slope


def at(start, size, unit):
    return pl.ds(pl.multiple_of(start, unit), size)


def gatherer(pool, rows, zsend, zrecv, asend, arecv, lsem):
    x, y, z, section = place()
    beside = ((section, bid(1 - x, y, z)), (section, bid(x, 1 - y, z)))
    above, below = (section, bid(x, y, z + 1)), (section, bid(x, y, z - 1))

    def remote(src, dst, send, recv, device):
        return pltpu.make_async_remote_copy(
            src_ref=src, dst_ref=dst, send_sem=send, recv_sem=recv, device_id=device, device_id_type=MESH
        )

    def half_rows(half):
        return pl.ds(half * (rows // 2), rows // 2)

    def along_z(half, way, k, source=None):
        spot = pool.at[k, y, x, half_rows(half)]
        source = spot if source is None else source
        return remote(source, spot, zsend.at[half, way, k], zrecv.at[half, way, k], (above, below)[way])

    def along_a(half):
        spot = pool.at[:, y, x, half_rows(half)]
        return remote(spot, spot, asend.at[half, 0], arecv.at[half, 0], beside[half])

    def along_b(half):
        spot = pool.at[:, y, :, half_rows(half)] if half == 0 else pool.at[:, :, x, half_rows(half)]
        return remote(spot, spot, asend.at[half, 1], arecv.at[half, 1], beside[1 - half])

    def advance(step, source):
        own = pltpu.make_async_copy(source, pool.at[z, y, x], lsem)
        if step == 0:
            own.start()
        for half in range(2):
            if step == 0:
                mine = source.at[half_rows(half)]

                @pl.when(z < NZ - 1)
                def _():
                    along_z(half, 0, z, mine).start()

                @pl.when(z > 0)
                def _():
                    along_z(half, 1, z, mine).start()
            elif step < NZ:

                @pl.when(z >= step)
                def _():
                    along_z(half, 0, z - step).wait_recv()

                    @pl.when(z < NZ - 1)
                    def _():
                        along_z(half, 0, z - step).start()

                @pl.when(z + step <= NZ - 1)
                def _():
                    along_z(half, 1, z + step).wait_recv()

                    @pl.when(z > 0)
                    def _():
                        along_z(half, 1, z + step).start()
            elif step == NZ:
                if half == 0:
                    own.wait()
                along_a(half).start()
            elif step == NZ + 1:
                along_a(half).wait_recv()
                along_b(half).start()
            else:
                along_b(half).wait()
                along_a(half).wait_send()
                for k in range(NZ):

                    @pl.when((k <= z) & (z < NZ - 1))
                    def _(k=k):
                        along_z(half, 0, k).wait_send()

                    @pl.when((k >= z) & (z > 0))
                    def _(k=k):
                        along_z(half, 1, k).wait_send()

    return advance


GATHER_STEPS = NZ + 3


def gather_semaphores():
    dma = pltpu.SemaphoreType.DMA
    return [dma((2, 2, NZ)), dma((2, 2, NZ)), dma((2, 2)), dma((2, 2)), dma]


def fused_kernel(items, span, enc_len, dec_len, gathers,
                 x_in, y_in, dz_in, wq_in, wo_in, wi_in, wd_in, wc_in, gain_in, shift_in, image_count, prefix_len, suffix_len,
                 panels, norms, dx_out, dec_out, dy_out, pool, mid_out, dqkv_out, stream_out,
                 w_qkv, w_out, w_up, w_down, w_cross,
                 qkv, prob, heads, low, rows_a, hidden, result, active, slope, crossing, stage,
                 wsem, xsem, psem, send_sem, recv_sem, zsend, zrecv, asend, arecv, lsem, hsend, hrecv):
    width = w_out.shape[0]
    hidden_units = w_up.shape[1]
    pairs = width // SLAB
    full = items * span
    blocks_up = hidden_units // width
    at_qkv, at_out, at_cross, at_up, at_down = 0, 3, 4, 6, 7
    section = lax.axis_index("section")
    chip = lax.axis_index("batch")
    other = (1 - section, chip)

    barrier = pltpu.get_barrier_semaphore()
    pl.semaphore_signal(barrier, inc=1, device_id=other, device_id_type=MESH)
    x, y, z, _ = place()
    beside = ((section, bid(1 - x, y, z)), (section, bid(x, 1 - y, z)))
    above, below = (section, bid(x, y, z + 1)), (section, bid(x, y, z - 1))
    if gathers:

        @pl.when(section == 1)
        def _():
            for device in beside:
                pl.semaphore_signal(barrier, inc=1, device_id=device, device_id_type=MESH)

            @pl.when(z < NZ - 1)
            def _():
                pl.semaphore_signal(barrier, inc=1, device_id=above, device_id_type=MESH)

            @pl.when(z > 0)
            def _():
                pl.semaphore_signal(barrier, inc=1, device_id=below, device_id_type=MESH)

    advance = gatherer(pool, items * dec_len, zsend, zrecv, asend, arecv, lsem)

    weights = ((wq_in, w_qkv), (wo_in, w_out), (wi_in, w_up), (wd_in, w_down), (wc_in, w_cross))
    loads = [pltpu.make_async_copy(src, dst, wsem.at[n]) for n, (src, dst) in enumerate(weights)]

    lane = lax.broadcasted_iota(jnp.int32, (1, SLAB), 1)
    is_first = lane < HEAD
    mask_a = jnp.where(is_first, 1.0, 0.0).astype(bf16)
    mask_b = jnp.where(is_first, 0.0, 1.0).astype(bf16)
    scale = HEAD ** (-0.5)
    gain, shift = gain_in[...].astype(f32), shift_in[...].astype(f32)
    spot = lax.broadcasted_iota(jnp.int32, (1, span), 1)

    def key_open(i):
        prefix = (spot >= PATCHES) & (spot - PATCHES < prefix_len[i])
        image = (spot < PATCHES) & (i < image_count[0])
        return (prefix | image) & (spot < enc_len)

    def stacked(slab, factor=1.0):
        return jnp.concatenate([slab * (mask_a * factor).astype(bf16), slab * (mask_b * factor).astype(bf16)], axis=0)

    def joined(both, rows):
        return jnp.where(is_first, both[:rows], both[rows:])

    def soft(scores, is_open):
        scores = jnp.where(is_open, scores, far_below)
        grown = jnp.exp(scores - jnp.max(scores, axis=-1, keepdims=True))
        return (grown * (1.0 / jnp.sum(grown, axis=-1, keepdims=True))).astype(bf16)

    def soft_back(p_low, dp):
        p = p_low.astype(f32)
        t = p * dp
        return (t - p * jnp.sum(t, axis=-1, keepdims=True)).astype(bf16)

    def wide(n):
        return at(n * width, width, width)

    def slab_of(n, h):
        return at(n * width + h * SLAB, SLAB, SLAB)

    def chunk(i):
        return pl.ds(i * span, span)

    def block_store(n, index):
        return pltpu.make_async_copy(stage.at[n % 2], panels.at[index], psem.at[n % 2])

    def emit(n, index, value):
        @pl.when(n >= 2)
        def _():
            block_store(n, index).wait()
        stage[n % 2] = value.astype(bf16)
        block_store(n, index).start()

    def norm_forward(value, index):
        unit, _ = normal(value)
        return (unit * gain[index : index + 1] + shift[index : index + 1]).astype(bf16)

    def norm_back(value, grad, index):
        unit, spread = normal(value)
        norms[index : index + 1] += jnp.sum(grad * unit, axis=0, keepdims=True)
        norms[3 + index : 4 + index] += jnp.sum(grad, axis=0, keepdims=True)
        scaled = grad * gain[index : index + 1]
        return spread * (
            scaled
            - jnp.mean(scaled, axis=-1, keepdims=True)
            - unit * jnp.mean(scaled * unit, axis=-1, keepdims=True)
        )

    def crossing_copy(source, n, tile):
        return pltpu.make_async_remote_copy(
            src_ref=source,
            dst_ref=crossing.at[:, at(tile * TILE, TILE, TILE)],
            send_sem=send_sem.at[n],
            recv_sem=recv_sem.at[tile],
            device_id=other,
            device_id_type=MESH,
        )

    def end_copy(n):
        dec = items * dec_len
        return pltpu.make_async_remote_copy(
            src_ref=heads.at[pl.ds((2 + n) * dec, dec), pl.ds(0, width // 2)],
            dst_ref=(dy_out, dec_out)[n],
            send_sem=hsend.at[n],
            recv_sem=hrecv.at[n],
            device_id=other,
            device_id_type=MESH,
        )

    tiles = width // TILE
    norms[...] = jnp.zeros_like(norms)

    @pl.when(section == 0)
    def _():
        x_load = pltpu.make_async_copy(x_in, low, xsem.at[0])
        x_load.start()
        loads[0].start()
        x_load.wait()
        for i in range(items):
            rows_a[chunk(i)] = norm_forward(low[chunk(i)].astype(f32), 0)
        loads[0].wait()
        for load in loads[1:]:
            load.start()

        @pl.loop(0, 3)
        def _(j):
            for i in range(items):
                qkv[chunk(i), wide(j)] = nn(rows_a[chunk(i)], w_qkv[:, wide(j)]).astype(bf16)

        @pl.loop(0, items)
        def _(i):
            r = at(i * span, span, 16)
            slabs = range(pairs)
            scores = [nt(stacked(qkv[r, slab_of(0, h)], scale), qkv[r, slab_of(1, h)]) for h in slabs]
            p = [soft(score, key_open(i)) for score in scores]
            out = [joined(nn(p[h], qkv[r, slab_of(2, h)]), span).astype(bf16) for h in slabs]
            for h in slabs:
                prob[i * pairs + h] = p[h]
                heads[r, slab_of(0, h)] = out[h]

        loads[1].wait()
        for i in range(items):
            r = chunk(i)
            value = low[r].astype(f32) + nn(heads[r], w_out[...])
            hidden[r] = value
            rows_a[r] = norm_forward(value, 1)
        loads[2].wait()

        @pl.loop(0, blocks_up)
        def _(j):
            for i in range(items):
                e, s = gelu_both(nn(rows_a[chunk(i)], w_up[:, wide(j)]))
                active[chunk(i), wide(j)] = e.astype(bf16)
                slope[chunk(i), wide(j)] = s.astype(bf16)

        loads[3].wait()
        for i in range(items):
            r = chunk(i)
            value = hidden[r] + nn(active[r], w_down[...])
            result[r] = value
            rows_a[r] = norm_forward(value, 2)
        loads[4].wait()
        pl.semaphore_wait(barrier, 1)

        def kv_send(n):
            return crossing_copy(low.at[:, at((n % 3) * TILE, TILE, TILE)], n, n // 2 + tiles * (n % 2))

        for n in range(2 * tiles):
            tile = n // 2 + tiles * (n % 2)
            if n >= 3:
                kv_send(n - 3).wait_send()
            for i in range(items):
                low[chunk(i), pl.ds((n % 3) * TILE, TILE)] = nn(rows_a[chunk(i)], w_cross[:, pl.ds(tile * TILE, TILE)]).astype(bf16)
            kv_send(n).start()
        for n in range(2 * tiles - 3, 2 * tiles):
            kv_send(n).wait_send()

        for n in range(2 * tiles):
            tile = n // 2 + tiles * (n % 2)
            crossing_copy(crossing.at[:, pl.ds(tile * TILE, TILE)], tile, tile).wait_recv()

        grads = [nt(crossing[chunk(i)], w_cross[...]) for i in range(items)]
        grads = [norm_back(result[chunk(i)], grads[i], 2) for i in range(items)]
        for i in range(items):
            result[chunk(i)] = grads[i]
            low[chunk(i)] = grads[i].astype(bf16)

        @pl.loop(0, 2)
        def _(j):
            emit(j, at_cross + j, tn(rows_a[...], crossing[:, wide(j)]))
        done = 2

        @pl.loop(0, blocks_up)
        def _(j):
            for i in range(items):
                r = chunk(i)
                slope[r, wide(j)] = (nt(low[r], w_down[wide(j)]) * slope[r, wide(j)].astype(f32)).astype(bf16)

        @pl.loop(0, blocks_up)
        def _(j):
            emit(done + j, at_down + 2 * j, tn(active[:, wide(j)], low[...]))
        done += blocks_up
        for i in range(items):
            rows_a[chunk(i)] = norm_forward(hidden[chunk(i)], 1)

        @pl.loop(0, blocks_up)
        def _(j):
            emit(done + j, at_up + 2 * j, tn(rows_a[...], slope[:, wide(j)]))
        done += blocks_up
        grads = [nt(slope[chunk(i)], w_up[...]) for i in range(items)]
        grads = [result[chunk(i)] + norm_back(hidden[chunk(i)], grads[i], 1) for i in range(items)]
        rounded = [grad.astype(bf16) for grad in grads]
        back = [nt(grad, w_out[...]).astype(bf16) for grad in rounded]
        for i in range(items):
            result[chunk(i)] = grads[i]
            low[chunk(i)] = rounded[i]
            rows_a[chunk(i)] = back[i]
        emit(done, at_out, tn(heads[...], low[...]))
        done += 1
        x_again = pltpu.make_async_copy(x_in, low, xsem.at[0])
        x_again.start()
        stream_store = pltpu.make_async_copy(result, stream_out, xsem.at[1])
        dqkv_store = pltpu.make_async_copy(active.at[:, pl.ds(0, 3 * width)], dqkv_out, xsem.at[2])
        if gathers:
            stream_store.start()

        group = 3

        @pl.loop(0, items * pairs // group)
        def _(it):
            i = it // (pairs // group)
            r = at(i * span, span, 16)
            slabs = [group * (it % (pairs // group)) + u for u in range(group)]
            both = [stacked(rows_a[r, slab_of(0, h)]) for h in slabs]
            p = [prob[group * it + u] for u in range(group)]
            dp = [nt(both[u], qkv[r, slab_of(2, h)]) for u, h in enumerate(slabs)]
            dv = [tn(p[u], both[u]).astype(bf16) for u in range(group)]
            ds = [soft_back(p[u], dp[u]) for u in range(group)]
            dq = [(joined(nn(ds[u], qkv[r, slab_of(1, h)]), span) * scale).astype(bf16) for u, h in enumerate(slabs)]
            dk = [tn(ds[u], stacked(qkv[r, slab_of(0, h)], scale)).astype(bf16) for u, h in enumerate(slabs)]
            for u, h in enumerate(slabs):
                active[r, slab_of(0, h)] = dq[u]
                active[r, slab_of(1, h)] = dk[u]
                active[r, slab_of(2, h)] = dv[u]

        if gathers:
            dqkv_store.start()
        x_again.wait()
        for i in range(items):
            rows_a[chunk(i)] = norm_forward(low[chunk(i)].astype(f32), 0)

        @pl.loop(0, 3)
        def _(j):
            emit(done + j, at_qkv + j, tn(rows_a[...], active[:, wide(j)]))
        done += 3
        if not gathers:
            grads = [nt(active[chunk(i), pl.ds(0, 3 * width)], w_qkv[...]) for i in range(items)]
            grads = [result[chunk(i)] + norm_back(low[chunk(i)].astype(f32), grads[i], 0) for i in range(items)]
            for i in range(items):
                heads[chunk(i)] = grads[i].astype(bf16)
            dx_store = pltpu.make_async_copy(heads, dx_out, xsem.at[0])
            dx_store.start()
            dx_store.wait()
        block_store(0, 0).wait()
        block_store(1, 0).wait()
        if gathers:
            stream_store.wait()
            dqkv_store.wait()
        for n in range(2):
            end_copy(n).wait_recv()

    @pl.when(section == 1)
    def _():
        dec = items * dec_len
        ra, rb, rc, rd = (pl.ds(n * dec, dec) for n in range(4))
        for n in (0, 1, 4, 2, 3):
            loads[n].start()
        rows_a[ra] = norm_forward(y_in[...].astype(f32), 0)
        if gathers:
            pl.semaphore_wait(barrier, 3 + (z + NZ - 1) // NZ + (2 * NZ - 2 - z) // NZ)
        if gathers:
            advance(0, dz_in)
        loads[0].wait()

        @pl.loop(0, 3)
        def _(j):
            qkv[ra, wide(j)] = nn(rows_a[ra], w_qkv[:, wide(j)]).astype(bf16)

        row = lax.broadcasted_iota(jnp.int32, (2 * dec, dec), 0) % dec
        column = lax.broadcasted_iota(jnp.int32, (2 * dec, dec), 1)
        item, place_in = column // dec_len, column % dec_len
        length = jnp.zeros_like(column)
        for i in range(items):
            length = jnp.where(item == i, suffix_len[i], length)
        own = (row // dec_len == item) & (place_in <= row % dec_len) & (place_in < length)

        slabs = range(pairs)
        scores = [nt(stacked(qkv[ra, slab_of(0, h)], scale), qkv[ra, slab_of(1, h)]) for h in slabs]
        p = [soft(score, own) for score in scores]
        out = [joined(nn(p[h], qkv[ra, slab_of(2, h)]), dec).astype(bf16) for h in slabs]
        for h in slabs:
            prob[h, pl.ds(0, 2 * dec), pl.ds(0, dec)] = p[h]
            heads[ra, slab_of(0, h)] = out[h]

        if gathers:
            advance(1, dz_in)
        loads[1].wait()
        value = y_in[...].astype(f32) + nn(heads[ra], w_out[...])
        hidden[ra] = value
        rows_a[rb] = norm_forward(value, 1)
        loads[4].wait()
        low[rb] = nn(rows_a[rb], w_cross[:, pl.ds(0, width)]).astype(bf16)
        loads[2].wait()
        loads[3].wait()
        if gathers:
            for step in range(2, GATHER_STEPS):
                advance(step, dz_in)

        part = 2 * dec_len
        spots = [(u, i) for u in range(TILE // SLAB) for i in range(items)]
        open_keys = [jnp.where(key_open(i), 1.0, 0.0) for i in range(items)]
        key_rows = jnp.concatenate([jnp.broadcast_to(open_keys[i], (part, span)) for u, i in spots], axis=0)

        @pl.loop(0, tiles)
        def _(t):
            for tile in (t, tiles + t):
                crossing_copy(crossing.at[:, at(tile * TILE, TILE, TILE)], tile, tile).wait_recv()

            def slab(n, u):
                return at(n * width + t * TILE + u * SLAB, SLAB, SLAB)
            scores = [
                nt(stacked(low[pl.ds(dec + i * dec_len, dec_len), slab(0, u)], scale), crossing[chunk(i), slab(0, u)])
                for u, i in spots
            ]
            p = soft(jnp.concatenate(scores, axis=0), key_rows > 0.0)
            for u in range(TILE // SLAB):
                prob[pairs + t * (TILE // SLAB) + u, pl.ds(0, items * part)] = p[u * items * part : (u + 1) * items * part]
            out = [nn(p[n * part : (n + 1) * part], crossing[chunk(i), slab(1, u)]) for n, (u, i) in enumerate(spots)]
            for n, (u, i) in enumerate(spots):
                heads[pl.ds(dec + i * dec_len, dec_len), slab(0, u)] = joined(out[n], dec_len).astype(bf16)

        value = hidden[ra] + nn(heads[rb], w_cross[:, pl.ds(width, width)])
        hidden[rb] = value
        rows_a[rc] = norm_forward(value, 2)
        mid_out[...] = rows_a[rc]

        @pl.loop(0, blocks_up)
        def _(j):
            e, s = gelu_both(nn(rows_a[rc], w_up[:, wide(j)]))
            active[ra, wide(j)] = e.astype(bf16)
            active[rb, wide(j)] = (nt(dz_in[...], w_down[wide(j)]) * s).astype(bf16)


        value = dz_in[...].astype(f32) + norm_back(hidden[rb], nt(active[rb], w_up[...]), 2)
        result[ra] = value
        low[ra] = value.astype(bf16)
        rows_a[rd] = nt(low[ra], w_cross[:, pl.ds(width, width)]).astype(bf16)
        if not gathers:
            pl.semaphore_wait(barrier, 1)

        def kv_back(tile):
            return crossing_copy(slope.at[:, at(tile * TILE, TILE, TILE)], tile, tile)

        @pl.loop(0, tiles)
        def _(t):
            def slab(n, u):
                return at(n * width + t * TILE + u * SLAB, SLAB, SLAB)
            both = [stacked(rows_a[pl.ds(3 * dec + i * dec_len, dec_len), slab(0, u)]) for u, i in spots]
            dp = jnp.concatenate([nt(both[n], crossing[chunk(i), slab(1, u)]) for n, (u, i) in enumerate(spots)], axis=0)
            p = jnp.concatenate(
                [prob[pairs + t * (TILE // SLAB) + u, pl.ds(0, items * part)] for u in range(TILE // SLAB)], axis=0
            )
            lines = [slice(n * part, (n + 1) * part) for n in range(len(spots))]
            dv = [tn(p[lines[n]], both[n]).astype(bf16) for n in range(len(spots))]
            q = [stacked(low[pl.ds(dec + i * dec_len, dec_len), slab(0, u)], scale) for u, i in spots]
            ds = soft_back(p, dp)
            dk = [tn(ds[lines[n]], q[n]).astype(bf16) for n in range(len(spots))]
            for n, (u, i) in enumerate(spots):
                slope[chunk(i), slab(0, u)] = dk[n]
                slope[chunk(i), slab(1, u)] = dv[n]
            kv_back(t).start()
            kv_back(tiles + t).start()
            back = [joined(nn(ds[lines[n]], crossing[chunk(i), slab(0, u)]), dec_len) * scale for n, (u, i) in enumerate(spots)]
            for n, (u, i) in enumerate(spots):
                low[pl.ds(3 * dec + i * dec_len, dec_len), slab(0, u)] = back[n].astype(bf16)


        done = 0
        if not gathers:

            @pl.loop(0, blocks_up)
            def _(j):
                emit(j, at_down + 2 * j, tn(active[ra, wide(j)], dz_in[...]))

            @pl.loop(0, blocks_up)
            def _(j):
                emit(blocks_up + j, at_up + 2 * j, tn(rows_a[rc], active[rb, wide(j)]))
            done = 2 * blocks_up
        emit(done, at_cross + 1, tn(heads[rb], low[ra]))
        emit(done + 1, at_cross, tn(rows_a[rb], low[rd]))
        done += 2
        value = result[ra] + norm_back(hidden[ra], nt(low[rd], w_cross[:, pl.ds(0, width)]), 1)
        result[ra] = value
        low[ra] = value.astype(bf16)
        emit(done, at_out, tn(heads[ra], low[ra]))
        done += 1
        rows_a[rd] = nt(low[ra], w_out[...]).astype(bf16)

        both = [stacked(rows_a[rd, slab_of(0, h)]) for h in slabs]
        p = [prob[h, pl.ds(0, 2 * dec), pl.ds(0, dec)] for h in slabs]
        dp = [nt(both[h], qkv[ra, slab_of(2, h)]) for h in slabs]
        dv = [tn(p[h], both[h]).astype(bf16) for h in slabs]
        ds = [soft_back(p[h], dp[h]) for h in slabs]
        dq = [(joined(nn(ds[h], qkv[ra, slab_of(1, h)]), dec) * scale).astype(bf16) for h in slabs]
        dk = [tn(ds[h], stacked(qkv[ra, slab_of(0, h)], scale)).astype(bf16) for h in slabs]
        for h in slabs:
            qkv[rb, slab_of(0, h)] = dq[h]
            qkv[rb, slab_of(1, h)] = dk[h]
            qkv[rb, slab_of(2, h)] = dv[h]


        @pl.loop(0, 3)
        def _(j):
            emit(done + j, at_qkv + j, tn(rows_a[ra], qkv[rb, wide(j)]))
        done += 3
        grad = nt(qkv[rb], w_qkv[...])
        half_width = width // 2
        ends = (
            (result[ra] + norm_back(y_in[...].astype(f32), grad, 0)).astype(bf16),
            (hidden[rb] + nn(active[ra], w_down[...])).astype(bf16),
        )
        for n, (value, out) in enumerate(zip(ends, (dy_out, dec_out))):
            out[...] = value[:, half_width:]
            heads[pl.ds((2 + n) * dec, dec), pl.ds(0, half_width)] = value[:, :half_width]
            end_copy(n).start()
        block_store(0, 0).wait()
        block_store(1, 0).wait()
        for n in range(2):
            end_copy(n).wait_send()
        for tile in range(2 * tiles):
            kv_back(tile).wait_send()


def fused(x, y, dz, weights, gain, shift, lengths, items, span, enc_len, dec_len, gathers, collective_id):
    wq, wo, wi, wd, wc = weights
    width, hidden_units = wi.shape
    full = items * span
    dec = items * dec_len
    count = sum(w.size for w in weights) // (width * width)
    here = pl.BlockSpec(memory_space=pltpu.VMEM)
    there = pl.BlockSpec(memory_space=pl.ANY)
    pairs = width // SLAB
    return pl.pallas_call(
        functools.partial(fused_kernel, items, span, enc_len, dec_len, gathers),
        out_shape=(
            jax.ShapeDtypeStruct((count, width, width), bf16),
            jax.ShapeDtypeStruct((8, width), f32),
            jax.ShapeDtypeStruct((full, width), bf16),
            jax.ShapeDtypeStruct((dec, width // 2), bf16),
            jax.ShapeDtypeStruct((dec, width // 2), bf16),
            jax.ShapeDtypeStruct((NZ, 2, 2, dec, width), bf16),
            jax.ShapeDtypeStruct((dec, width), bf16),
            jax.ShapeDtypeStruct((full, 3 * width), bf16),
            jax.ShapeDtypeStruct((full, width), f32),
        ),
        in_specs=[there, here, here] + [there] * 5 + [here] * 2 + [pl.BlockSpec(memory_space=pltpu.SMEM)] * 3,
        out_specs=(there, here, there, here, here, there, here, there, there),
        scratch_shapes=[
            pltpu.VMEM(wq.shape, bf16),
            pltpu.VMEM(wo.shape, bf16),
            pltpu.VMEM(wi.shape, bf16),
            pltpu.VMEM(wd.shape, bf16),
            pltpu.VMEM(wc.shape, bf16),
            pltpu.VMEM((full, 3 * width), bf16),
            pltpu.VMEM((items * pairs, 2 * span, span), bf16),
            pltpu.VMEM((full, width), bf16),
            pltpu.VMEM((full, width), bf16),
            pltpu.VMEM((full, width), bf16),
            pltpu.VMEM((full, width), f32),
            pltpu.VMEM((full, width), f32),
            pltpu.VMEM((full, hidden_units), bf16),
            pltpu.VMEM((full, hidden_units), bf16),
            pltpu.VMEM((full, 2 * width), bf16),
            pltpu.VMEM((2, width, width), bf16),
            pltpu.SemaphoreType.DMA((5,)),
            pltpu.SemaphoreType.DMA((3,)),
            pltpu.SemaphoreType.DMA((2,)),
            pltpu.SemaphoreType.DMA((2 * width // TILE,)),
            pltpu.SemaphoreType.DMA((2 * width // TILE,)),
            *gather_semaphores(),
            pltpu.SemaphoreType.DMA((2,)),
            pltpu.SemaphoreType.DMA((2,)),
        ],
        compiler_params=pltpu.CompilerParams(
            collective_id=collective_id, has_side_effects=True, vmem_limit_bytes=63 * 2**20
        ),
    )(x, y, dz, wq, wo, wi, wd, wc, gain, shift, *lengths)


AHEAD = 2
LATE = 2


def ar_kernel(pairs, rows, width, across_block, g, norms, dqkv, stream, x_in, wq_in, gain, mid, out, norms_out, dx_half, pool, acc, res, rx, up, dn, ry, nbuf, lsem, asend, arecv, zsend, zrecv, nsem, dsem, w_qkv, dqkv_part, stream_part, x_part, dx, isem, *gather_sems):
    x, y, z, c = place()
    pairs = pairs[0] + (pairs[1] - pairs[0]) * c
    half, block = rows // 2, rows // 8

    def dev(x, y, z):
        return (c, bid(x, y, z))

    across = (dev(1 - x, y, z), dev(x, 1 - y, z))
    above, below = dev(x, y, z + 1), dev(x, y, z - 1)
    bit = (x, y)

    barrier = pltpu.get_barrier_semaphore()
    faraway = dev(x, y, (z + 2) % NZ)
    for d in across + (faraway,):
        pl.semaphore_signal(barrier, inc=1, device_id=d, device_id_type=MESH)

    @pl.when(z < NZ - 1)
    def _():
        pl.semaphore_signal(barrier, inc=1, device_id=above, device_id_type=MESH)

    @pl.when(z > 0)
    def _():
        pl.semaphore_signal(barrier, inc=1, device_id=below, device_id_type=MESH)

    mate = (1 - c, bid(x, y, z))

    @pl.when(c == 1)
    def _():
        pl.semaphore_signal(barrier, inc=1, device_id=mate, device_id_type=MESH)

    pl.semaphore_wait(barrier, 4 - c + (z + NZ - 1) // NZ + (2 * NZ - 2 - z) // NZ)

    def rdma(src, dst, send, recv, device):
        return pltpu.make_async_remote_copy(src_ref=src, dst_ref=dst, send_sem=send, recv_sem=recv, device_id=device, device_id_type=MESH)

    half_width = dx.shape[1] // 2
    dx_own = pltpu.make_async_copy(dx.at[:, pl.ds(0, half_width)], dx_half, dsem.at[0])
    dx_other = rdma(dx.at[:, pl.ds(half_width, half_width)], dx_half, dsem.at[1], dsem.at[2], mate)

    w_load = pltpu.make_async_copy(wq_in, w_qkv, isem.at[3])

    @pl.when(c == 0)
    def _():
        w_load.start()

    span = dqkv_part.shape[0]
    items = dx.shape[0] // span

    def last_step(i):
        r = rows_at(i * span, span)
        parts = ((dqkv, dqkv_part), (stream, stream_part), (x_in, x_part))
        loads = [pltpu.make_async_copy(src.at[r], dst, isem.at[n]) for n, (src, dst) in enumerate(parts)]
        for load in loads:
            load.start()
        for load in loads:
            load.wait()

        @pl.when(i == 0)
        def _():
            w_load.wait()
        grad = nt(dqkv_part[...], w_qkv[...])
        unit, spread = normal(x_part[...].astype(f32))
        norms_out[0:1] += jnp.sum(grad * unit, axis=0, keepdims=True)
        norms_out[3:4] += jnp.sum(grad, axis=0, keepdims=True)
        scaled = grad * gain[0:1].astype(f32)
        back = spread * (
            scaled
            - jnp.mean(scaled, axis=-1, keepdims=True)
            - unit * jnp.mean(scaled * unit, axis=-1, keepdims=True)
        )
        dx[r] = (stream_part[...] + back).astype(jnp.bfloat16)

    def parts(t, f):
        p = 2 * t + f
        a, b = bit[f], bit[1 - f]
        own = a * half
        other = (1 - a) * half
        return p, own, other, b

    def rows_at(start, n):
        return pl.ds(pl.multiple_of(start, 16), n)

    def panel_of(array, p, start, n):
        columns = pl.ds(pl.multiple_of(p % across_block * width, 128), width)
        return array.at[p // across_block, rows_at(start, n), columns]

    def own_load(t, f):
        p, own, other, b = parts(t, f)
        return pltpu.make_async_copy(panel_of(g, p, own, half), acc.at[p], lsem.at[p, 0])

    def own_store(t, f, k):
        p, own, other, b = parts(t, f)
        start = own if k == 0 else other
        return pltpu.make_async_copy(res.at[p, rows_at(start, half)], panel_of(out, p, start, half), lsem.at[p, k])

    def rs_a(t, f):
        p, own, other, b = parts(t, f)
        return rdma(panel_of(g, p, other, half), rx.at[p], asend.at[p], arecv.at[p, 0], across[f])

    def rs_up(t, f, j):
        p = 2 * t + f
        r = pl.ds((j + 1) * block, (NZ - 1 - j) * block)
        return rdma(acc.at[p, r], up.at[p, r], zsend.at[p, 0], zrecv.at[p, 0, 0], above)

    def rs_dn(t, f, j):
        p = 2 * t + f
        r = pl.ds(0, j * block)
        return rdma(acc.at[p, r], dn.at[p, r], zsend.at[p, 1], zrecv.at[p, 1, 0], below)

    def both_b(t, f):
        p, own, other, b = parts(t, f)
        return rdma(acc.at[p, rows_at(z * block, block)], ry.at[p], asend.at[p], arecv.at[p, 1], across[1 - f])

    def ag_up(t, f, m):
        p, own, other, b = parts(t, f)
        s = res.at[p, rows_at(own + (z - m) * block, block)]
        return rdma(s, s, zsend.at[p, 0], zrecv.at[p, 0, 1 + m], above)

    def ag_dn(t, f, m):
        p, own, other, b = parts(t, f)
        s = res.at[p, rows_at(own + (z + m) * block, block)]
        return rdma(s, s, zsend.at[p, 1], zrecv.at[p, 1, 1 + m], below)

    def ag_a(t, f):
        p, own, other, b = parts(t, f)
        s = res.at[p, rows_at(own, half)]
        return rdma(s, s, asend.at[p], arecv.at[p, 2], across[f])

    def s0(t, f):
        rs_a(t, f).start()
        own_load(t, f).start()

    def s1(t, f):
        p, own, other, b = parts(t, f)
        own_load(t, f).wait()
        rs_a(t, f).wait()
        acc[p] = acc[p] + rx[p]

        @pl.when(z == 0)
        def _():
            rs_up(t, f, 0).start()

        @pl.when(z == NZ - 1)
        def _():
            rs_dn(t, f, NZ - 1).start()

    def chain(t, f, j):
        p = 2 * t + f

        @pl.when(z == j)
        def _():
            rs_up(t, f, j - 1).wait_recv()
            r = pl.ds(j * block, (NZ - j) * block)
            acc[p, r] = acc[p, r] + up[p, r]
            if j < NZ - 1:
                rs_up(t, f, j).start()

        @pl.when(z == NZ - 1 - j)
        def _():
            rs_dn(t, f, NZ - j).wait_recv()
            r = pl.ds(0, (NZ - j) * block)
            acc[p, r] = acc[p, r] + dn[p, r]
            if j < NZ - 1:
                rs_dn(t, f, NZ - 1 - j).start()

    def s4(t, f):
        chain(t, f, NZ - 1)
        both_b(t, f).start()

    def s5(t, f):
        p, own, other, b = parts(t, f)
        both_b(t, f).wait()
        res[p, rows_at(own + z * block, block)] = acc[p, rows_at(z * block, block)] + ry[p]

        for j in range(NZ):

            @pl.when(z == j)
            def _(j=j):
                if j < NZ - 1:
                    rs_up(t, f, j).wait_send()
                    ag_up(t, f, 0).start()
                if j > 0:
                    rs_dn(t, f, j).wait_send()
                    ag_dn(t, f, 0).start()

    def spread(t, f, j):
        @pl.when(z >= j)
        def _():
            ag_up(t, f, j - 1).wait_recv()

            @pl.when(z < NZ - 1)
            def _():
                ag_up(t, f, j - 1).wait_send()
                ag_up(t, f, j).start()

        @pl.when(z + j <= NZ - 1)
        def _():
            ag_dn(t, f, j - 1).wait_recv()

            @pl.when(z > 0)
            def _():
                ag_dn(t, f, j - 1).wait_send()
                ag_dn(t, f, j).start()

    def s9(t, f):
        spread(t, f, NZ - 1)
        ag_a(t, f).start()
        own_store(t, f, 0).start()

    def s10(t, f):
        ag_a(t, f).wait()
        own_store(t, f, 1).start()
        @pl.when(z < NZ - 1)
        def _():
            ag_up(t, f, 0).wait_send()

        @pl.when(z > 0)
        def _():
            ag_dn(t, f, 0).wait_send()

    def s11(t, f):
        own_store(t, f, 0).wait()
        own_store(t, f, 1).wait()

    mates = across + (dev(x, y, z + 1 - 2 * (z % 2)), faraway)

    def norm_swap(j):
        return rdma(norms_out, nbuf.at[j], nsem.at[0, j], nsem.at[1, j], mates[j])

    norms_out[...] = norms[...]

    stages = (
        [(0, s0), (AHEAD, s1)]
        + [(AHEAD + j, functools.partial(lambda j, t, f: chain(t, f, j), j)) for j in range(1, NZ - 1)]
        + [(AHEAD + NZ - 1, s4), (AHEAD + NZ, s5)]
        + [(AHEAD + NZ + j, functools.partial(lambda j, t, f: spread(t, f, j), j)) for j in range(1, NZ - 1)]
        + [(AHEAD + 2 * NZ - 1, s9), (AHEAD + 2 * NZ + LATE, s10), (AHEAD + 2 * NZ + 1 + LATE, s11)]
    )

    advance = gatherer(pool, mid.shape[0], *gather_sems)

    def tick(tau, carry):
        for step in range(GATHER_STEPS):

            @pl.when((c == 1) & (tau == 2 * step))
            def _(step=step):
                advance(step, mid)

        for j in range(4):

            @pl.when(tau == items + 3 * j + 3)
            def _(j=j):
                norm_swap(j).wait()
                norms_out[...] = norms_out[...] + nbuf[j]
                if j < 3:
                    norm_swap(j + 1).start()

        for lag, stage in stages:
            t = tau - lag

            @pl.when((t >= 0) & (t < pairs))
            def _(stage=stage, t=t):
                stage(t, 0)
                stage(t, 1)

        @pl.when((c == 0) & (tau < items))
        def _():
            last_step(tau)

        @pl.when(tau == items)
        def _():
            norm_swap(0).start()

            @pl.when(c == 0)
            def _():
                dx_own.start()
                dx_other.start()
        return carry
    lax.fori_loop(0, pairs + AHEAD + 2 * NZ + 2 + LATE, tick, 0)

    @pl.when(c == 0)
    def _():
        dx_own.wait()
        dx_other.wait_send()

    @pl.when(c == 1)
    def _():
        dx_other.wait_recv()


def all_reduce(g, norms, dqkv, stream, x, wq, gain, mid, items, counts, collective_id):
    blocks, rows, block_width = g.shape
    width = 256
    across_block = block_width // width
    n = blocks * across_block
    half, block = rows // 2, rows // 8
    bf = jnp.bfloat16
    there, here = pl.BlockSpec(memory_space=pl.ANY), pl.BlockSpec(memory_space=pltpu.VMEM)
    span = x.shape[0] // items
    return pl.pallas_call(
        functools.partial(ar_kernel, [count * across_block // 2 for count in counts], rows, width, across_block),
        out_shape=(
            jax.ShapeDtypeStruct(g.shape, bf),
            jax.ShapeDtypeStruct(norms.shape, norms.dtype),
            jax.ShapeDtypeStruct((x.shape[0], x.shape[1] // 2), bf),
            jax.ShapeDtypeStruct((NZ, 2, 2) + mid.shape, bf),
        ),
        in_specs=[there, here, there, there, there, there, here, there],
        out_specs=(pl.BlockSpec(memory_space=pl.ANY), pl.BlockSpec(memory_space=pltpu.VMEM), pl.BlockSpec(memory_space=pl.ANY), pl.BlockSpec(memory_space=pl.ANY)),
        scratch_shapes=[
            pltpu.VMEM((n, half, width), bf),
            pltpu.VMEM((n, rows, width), bf),
            pltpu.VMEM((n, half, width), bf),
            pltpu.VMEM((n, half, width), bf),
            pltpu.VMEM((n, half, width), bf),
            pltpu.VMEM((n, block, width), bf),
            pltpu.VMEM((4,) + norms.shape, norms.dtype),
            pltpu.SemaphoreType.DMA((n, 2)),
            pltpu.SemaphoreType.DMA((n,)),
            pltpu.SemaphoreType.DMA((n, 3)),
            pltpu.SemaphoreType.DMA((n, 2)),
            pltpu.SemaphoreType.DMA((n, 2, NZ)),
            pltpu.SemaphoreType.DMA((2, 4)),
            pltpu.SemaphoreType.DMA((3,)),
            pltpu.VMEM(wq.shape, bf),
            pltpu.VMEM((span, dqkv.shape[1]), bf),
            pltpu.VMEM((span, x.shape[1]), f32),
            pltpu.VMEM((span, x.shape[1]), bf),
            pltpu.VMEM(x.shape, bf),
            pltpu.SemaphoreType.DMA((4,)),
            *gather_semaphores(),
        ],
        compiler_params=pltpu.CompilerParams(collective_id=collective_id, has_side_effects=True, vmem_limit_bytes=60 * 2**20),
    )(g, norms, dqkv, stream, x, wq, gain, mid)


SLOTS = 4


def finish_kernel(counts, gathers, panels, pool_rows, pool_grads, up_in, down_in, *rest):
    outs = rest[:5]
    inbox, stage, rows, grads, w_up, w_down, active, bent, sems, in_sems, out_sems = rest[5:]
    width = panels.shape[1]
    plain = sum(counts[:3])
    total = sum(counts)
    section = lax.axis_index("section")
    targets = []
    for count, out in zip(counts[:3], outs):
        targets += [out.at[0, :, pl.ds(j * width, width)] for j in range(count)]
    for j in range(counts[3]):
        targets += [outs[3].at[0, :, pl.ds(j * width, width)], outs[4].at[0, pl.ds(j * width, width)]]

    def load(n):
        return pltpu.make_async_copy(panels.at[n], inbox.at[n], in_sems.at[n])

    def store(n):
        return pltpu.make_async_copy(stage.at[n % SLOTS], targets[n], out_sems.at[n % SLOTS])

    def put(n, value):
        if n >= SLOTS:
            store(n - SLOTS).wait()
        stage[n % SLOTS] = value
        store(n).start()

    def widen(n):
        load(n).wait()
        put(n, inbox[n].astype(f32))

    for n in range(plain):
        load(n).start()
    summed = (section == 0) if gathers else (section >= 0)
    whole = [
        pltpu.make_async_copy(src, dst, sems.at[n])
        for n, (src, dst) in enumerate(((pool_rows, rows), (pool_grads, grads), (up_in, w_up), (down_in, w_down)))
    ]

    @pl.when(summed)
    def _():
        for n in range(plain, total):
            load(n).start()

    if gathers:

        @pl.when(section == 1)
        def _():
            for copy in whole:
                copy.start()

    for n in range(plain):
        widen(n)

    @pl.when(summed)
    def _():
        for n in range(plain, total):
            widen(n)

    if gathers:

        @pl.when(section == 1)
        def _():
            for copy in whole:
                copy.wait()
            size = rows.shape[0] // 4
            for j in range(counts[3]):
                cols = pl.ds(j * width, width)

                @pl.loop(0, 4)
                def _(i):
                    r = at(i * size, size, size)
                    e, s = gelu_both(nn(rows[r], w_up[:, cols]))
                    active[r] = e.astype(bf16)
                    bent[r] = (nt(grads[r], w_down[cols]) * s).astype(bf16)
                put(plain + 2 * j, tn(rows[...], bent[...]))
                put(plain + 2 * j + 1, tn(active[...], grads[...]))

    for n in range(total - SLOTS, total):
        store(n).wait()


def finish(panels, pool_rows, pool_grads, w_up, w_down, shapes, gathers):
    total, high, wide = panels.shape
    counts = [rows * columns // (high * wide) for rows, columns in shapes]
    there = pl.BlockSpec(memory_space=pl.ANY)
    gathered = pool_rows.shape[0] if gathers else 16
    return pl.pallas_call(
        functools.partial(finish_kernel, counts, gathers),
        out_shape=[jax.ShapeDtypeStruct((1,) + shape, f32) for shape in shapes],
        in_specs=[there] * 5,
        out_specs=[there] * 5,
        scratch_shapes=[
            pltpu.VMEM(panels.shape, bf16),
            pltpu.VMEM((SLOTS, high, wide), f32),
            pltpu.VMEM((gathered, wide), bf16),
            pltpu.VMEM((gathered, wide), bf16),
            pltpu.VMEM(w_up.shape, bf16),
            pltpu.VMEM(w_down.shape, bf16),
            pltpu.VMEM((gathered, wide), bf16),
            pltpu.VMEM((gathered, wide), bf16),
            pltpu.SemaphoreType.DMA((4,)),
            pltpu.SemaphoreType.DMA((total,)),
            pltpu.SemaphoreType.DMA((SLOTS,)),
        ],
        compiler_params=pltpu.CompilerParams(vmem_limit_bytes=62 * 2**20),
    )(panels, pool_rows, pool_grads, w_up, w_down)


def per_device(
    enc_input,
    dec_input,
    out_grad,
    attn_qkv,
    attn_out,
    mlp_in,
    mlp_out,
    cross_proj,
    norm_gain,
    norm_shift,
    image_count,
    prefix_len,
    suffix_len,
):
    section = lax.axis_index("section")
    items, enc_len, width = enc_input.shape
    dec_len = dec_input.shape[1]
    span = -(-enc_len // 16) * 16
    weights = (attn_qkv[0], attn_out[0], mlp_in[0], mlp_out[0], cross_proj[0])
    x = jnp.pad(enc_input, ((0, 0), (0, span - enc_len), (0, 0))).reshape(items * span, width)
    gathers = lax.axis_size("batch") == 16
    panels, norms, dx, dec_out, dy, grad_rows, mid, dqkv, stream = fused(
        x,
        dec_input.reshape(-1, width),
        out_grad.reshape(-1, width),
        weights,
        norm_gain[0],
        norm_shift[0],
        (image_count, prefix_len, suffix_len),
        items,
        span,
        enc_len,
        dec_len,
        gathers,
        1,
    )
    if gathers:
        blocks = panels.shape[0]
        panels, norms, dx_half, rows = all_reduce(panels, norms, dqkv, stream, x, weights[0], norm_gain[0], mid, items, (blocks, blocks - 2 * mlp_in.shape[2] // width), 0)
    else:
        panels, norms = lax.psum(panels, "batch"), lax.psum(norms, "batch")
        half = width // 2
        theirs = lax.dynamic_slice_in_dim(dx, (1 - section) * half, half, 1)
        theirs = lax.ppermute(theirs, "section", [(0, 1), (1, 0)])
        dx_half = jnp.where(section == 0, dx[:, :half], theirs)
    order = (0, 1, 4, 2, 3)
    rows = rows.reshape(-1, width) if gathers else mid
    blocks = finish(panels, rows, grad_rows.reshape(-1, width), weights[2], weights[3], [weights[n].shape for n in order], gathers)
    grads = [blocks[order.index(n)] for n in range(len(order))]
    half = width // 2
    return (
        dec_out.reshape(items, dec_len, half),
        dx_half.reshape(items, span, half)[:, :enc_len],
        dy.reshape(items, dec_len, half),
        *grads,
        norms[None, :3],
        norms[None, 3:6],
    )


def solution(mesh):
    items = P("batch", None, None)
    matrix = P("section", None, None)
    halves = P("batch", None, "section")
    return jax.shard_map(
        per_device,
        mesh=mesh,
        in_specs=(items,) * 3 + (matrix,) * 7 + (P("batch"),) * 3,
        out_specs=(halves,) * 3 + (matrix,) * 7,
        check_vma=False,
    )
```
